128 devices in a mesh: section: 8 (over z, x_hi), tensor: 16 (over y, x_lo, core).
Axes of the slice: x: 4 (x_hi: 2, x_lo: 2; x = x_hi * 2 + x_lo), y: 4, z: 4, core: 2. Of those that a mesh axis runs over, the one named last changes fastest.
Arguments:
- forward_in: bfloat16 [8, 768, 6144], P('section', 'tensor'), may hold values from -6 to 6
- grad_out: bfloat16 [8, 768, 6144], P('section', 'tensor'), may hold values from -1.1953125 to 1.1953125
- saved_in: bfloat16 [8, 768, 6144], P('section', 'tensor'), may hold values from -6 to 6
- weight: bfloat16 [8, 6144, 6144], P('section', 'tensor'), may hold values from -0.078125 to 0.078125
- gain: bfloat16 [8, 6144], P('section', 'tensor'), may hold values from 0.099609375 to 1.8984375
Outputs:
- next_input: bfloat16 [8, 768, 6144], P('section', 'tensor')
- prev_grad: bfloat16 [8, 768, 6144], P('section', 'tensor')
- weight_grad: bfloat16 [8, 6144, 6144], P('section', 'tensor')
- gain_grad: float32 [8, 6144], P('section', 'tensor')
The draws below stay inside these ranges and needn't reach their ends.
All inputs are finite; a program needn't handle non-finite values.
Results may differ from the reference program's by a relative error of at most 0.019.
Values may be sent and summed in bfloat16 or wider, within the bound.
A program may use at most 192 MiB of HBM per device.

```python
import jax
import jax.numpy as jnp
from jax import lax

D = 6144
TOKENS = 768
N_SECTION = 8
N_TENSOR = 16


def shard_levels(key, dims, cuts, smallest, top_value):
    def one(dim, shards_of):
        draws = jax.random.uniform(jax.random.fold_in(jax.random.fold_in(key, 6), dim), (shards_of,), jnp.float32, smallest / len(cuts), top_value / len(cuts))
        return jnp.repeat(jnp.exp(draws), dims[dim] // shards_of).reshape((-1,) + (1,) * (len(dims) - dim - 1))

    level = one(*cuts[0])
    for cut in cuts[1:]:
        level = level * one(*cut)
    return level


def gaussian(own_key, shape, deviation, most, cuts=(), dtype=jnp.bfloat16):
    result = jax.random.normal(own_key, shape, jnp.float32) * deviation
    if len(cuts) > 0:
        result = shard_levels(own_key, shape, cuts, -0.22, 0.18) * result
    return jnp.clip(result, min=-most, max=most).astype(dtype)


def setup_inputs(seed: int = 0) -> dict:
    arg_keys = jax.random.split(jax.random.key(seed), 6)
    forward_in = gaussian(arg_keys[0], (N_SECTION, TOKENS, D), 1.0, 6.0, ((0, 8), (1, 16)))
    grad_out = gaussian(arg_keys[1], (N_SECTION, TOKENS, D), 0.2, 1.1953125, ((0, 8), (1, 16)))
    saved_in = gaussian(arg_keys[2], (N_SECTION, TOKENS, D), 1.0, 6.0, ((0, 8), (1, 16)))
    weight = gaussian(arg_keys[3], (N_SECTION, D, D), D ** -0.5, 0.078125, ((0, 8), (1, 16)))
    gain = jnp.clip(1.0 + 0.18 * jax.random.normal(arg_keys[4], (N_SECTION, D), jnp.float32), 0.099609375, 1.8984375).astype(jnp.bfloat16)
    return {"forward_in": forward_in, "grad_out": grad_out, "saved_in": saved_in, "weight": weight, "gain": gain}


def normalize(values):
    center = lax.optimization_barrier(jnp.mean(values, axis=1, keepdims=True))
    shifted = values - center
    recip = lax.rsqrt(lax.optimization_barrier(jnp.mean(shifted * shifted, axis=1, keepdims=True)) + 1e-05)
    return (shifted * recip, recip)

def section_forward(inputs):
    layer_in, matrix, scales = inputs
    widened = layer_in.astype(jnp.float32)
    normed, ignored = normalize(widened)
    hidden = (normed * scales.astype(jnp.float32)).astype(jnp.bfloat16)
    block_width = D // N_TENSOR
    hidden_blocks = jnp.transpose(hidden.reshape(TOKENS, N_TENSOR, block_width), (1, 0, 2))
    matrix_blocks = matrix.reshape(N_TENSOR, block_width, D)

    def accumulate(summed, operands):
        partial_value = jnp.dot(operands[0], operands[1], preferred_element_type=jnp.float32)
        rounded = lax.optimization_barrier(partial_value.astype(jnp.bfloat16))
        return (summed + rounded.astype(jnp.float32), None)
    summed, ignored = lax.scan(accumulate, jnp.zeros((TOKENS, D), jnp.float32), (hidden_blocks, matrix_blocks))
    return (widened + summed).astype(jnp.bfloat16)

def section_backward(inputs):
    saved, upstream, matrix, scales = inputs
    scale_values = scales.astype(jnp.float32)
    normed, recip = normalize(saved.astype(jnp.float32))
    hidden = (normed * scale_values).astype(jnp.bfloat16)
    grad_hidden = jnp.dot(upstream, matrix.T, preferred_element_type=jnp.float32)
    gain_grad = lax.optimization_barrier(jnp.sum(grad_hidden * normed, axis=0))
    rounded = lax.optimization_barrier(grad_hidden.astype(jnp.bfloat16)).astype(jnp.float32)
    grad_normed = rounded * scale_values
    inner = grad_normed - lax.optimization_barrier(jnp.mean(grad_normed, axis=1, keepdims=True)) - normed * lax.optimization_barrier(jnp.mean(grad_normed * normed, axis=1, keepdims=True))
    grad_in = (upstream.astype(jnp.float32) + recip * inner).astype(jnp.bfloat16)
    weight_grad = jnp.dot(hidden.T, upstream, preferred_element_type=jnp.float32).astype(jnp.bfloat16)
    return (grad_in, weight_grad, gain_grad)

def reference(forward_in, grad_out, saved_in, weight, gain):
    outputs = lax.map(section_forward, (forward_in, weight, gain))
    grads, weight_grad, gain_grad = lax.map(section_backward, (saved_in[::-1], grad_out, weight, gain))
    return (jnp.roll(outputs, 1, axis=0), jnp.roll(grads, -1, axis=0), weight_grad, gain_grad)
```

```python
import jax
import jax.numpy as jnp
from jax import lax
from jax.experimental import pallas as pl
from jax.experimental.pallas import tpu as pltpu
from jax.sharding import PartitionSpec as P

D = 6144
TOKENS = 768
ROWS = 48
CHIP = 96
WIDTH = 384
HALF = D // 2
CA = 1280
CB = HALF - CA
STRIP = 16
BF = jnp.bfloat16
F32 = jnp.float32
EPS = 1e-05


def block(r, d):
    return (r * 4 + d) * CHIP


def normalize(values):
    center = jnp.mean(values, axis=1, keepdims=True)
    shifted = values - center
    recip = lax.rsqrt(jnp.mean(shifted * shifted, axis=1, keepdims=True) + EPS)
    return shifted * recip, recip


def strips(rows, body):
    def step(i, carry):
        body(pl.ds(pl.multiple_of(i * STRIP, STRIP), STRIP), i)
        return carry

    lax.fori_loop(0, rows // STRIP, step, 0)


def kernel(
    x_ref, g_ref, s_ref, w_ref, gain_ref,
    next_ref, prev_ref, wg_ref, gg_ref,
    G, W, WC, PF, HN, XR, XO, NX, SO, NS, SR, BHT, DH, GI, XRES,
    SA, RA, SA2, RA2, SAF, RAF, SB2, RB2, SBF, RBF, SBX, RBX, OA, OB,
    QC, QS, QR, EC, ES, ER,
    send_sem, recv_sem, local_sem, group_sem,
):
    s = lax.axis_index("section")
    t = lax.axis_index("tensor")
    y, xl, c = t // 4, (t // 2) % 2, t % 2
    sib = (s, t + 1 - 2 * c)
    yp = (s, ((y + 1) % 4) * 4 + xl * 2 + c)
    ym = (s, ((y + 3) % 4) * 4 + xl * 2 + c)
    pair = (s, y * 4 + (1 - xl) * 2 + c)
    mirrored, following, previous = 7 - s, (s + 1) % 8, (s + 7) % 8

    def columns(start, width):
        return pl.ds(pl.multiple_of(start, 128), width)

    mine = c * HALF
    other = (1 - c) * HALF
    cols_a = columns(mine, CA)
    cols_b = columns(mine + CA, CB)

    names = {}
    sent = []

    def send(name, src, dst, device, landing=None):
        i = names.setdefault(name, (len(names), dst if landing is None else landing))[0]
        copy = pltpu.make_async_remote_copy(
            src_ref=src, dst_ref=dst, send_sem=send_sem.at[i], recv_sem=recv_sem.at[i],
            device_id=device, device_id_type=pl.DeviceIdType.MESH,
        )
        copy.start()
        sent.append(copy)

    def arrived(ref, sem, scratch_sem):
        pltpu.make_async_remote_copy(
            src_ref=ref, dst_ref=ref, send_sem=scratch_sem, recv_sem=sem,
            device_id=sib, device_id_type=pl.DeviceIdType.MESH,
        ).wait_recv()

    def left(ref, sem, scratch_sem):
        pltpu.make_async_remote_copy(
            src_ref=ref, dst_ref=ref, send_sem=sem, recv_sem=scratch_sem,
            device_id=sib, device_id_type=pl.DeviceIdType.MESH,
        ).wait_send()

    def recv(name):
        i, landing = names[name]
        arrived(landing, recv_sem.at[i], send_sem.at[i])

    X_IN, X_OUT, S_IN, S_OUT, Q_IN, Q_OUT, E_IN, E_OUT, G_IN, G_OUT, P_IN, P_OUT, N_IN, N_OUT = range(14)

    def grouped(src, dst, out, into, device):
        pltpu.make_async_remote_copy(
            src_ref=src, dst_ref=dst, send_sem=group_sem.at[out], recv_sem=group_sem.at[into],
            device_id=device, device_id_type=pl.DeviceIdType.MESH,
        ).start()

    load_x = pltpu.make_async_copy(x_ref, XO, local_sem.at[0])
    load_g = pltpu.make_async_copy(g_ref, G.at[pl.ds(pl.multiple_of(c * ROWS, 16), ROWS), :], local_sem.at[1])
    load_s = pltpu.make_async_copy(s_ref, SO, local_sem.at[2])
    load_w = pltpu.make_async_copy(w_ref, W, local_sem.at[3])
    load_wc = pltpu.make_async_copy(w_ref.at[:, columns(mine, HALF)], WC.at[0:WIDTH, :], local_sem.at[4])
    load_xres = pltpu.make_async_copy(
        x_ref.at[:, columns(mine, HALF)], XRES.at[pl.ds(pl.multiple_of(c * ROWS, 16), ROWS), :], local_sem.at[5]
    )
    for load in (load_x, load_g, load_s, load_wc, load_xres, load_w):
        load.start()

    barrier = pltpu.get_barrier_semaphore()

    def greet(section, first):
        def step(i, carry):
            pl.semaphore_signal(
                barrier, inc=1, device_id=(section, (t + i) % 16), device_id_type=pl.DeviceIdType.MESH
            )
            return carry

        lax.fori_loop(first, 16, step, 0)

    greet(s, 1)
    greet(mirrored, 0)
    greet(following, 0)
    greet(previous, 0)

    load_x.wait()

    def norm_x(rows, i):
        NX[rows, :] = normalize(XO[rows, :].astype(F32))[0].astype(BF)

    strips(ROWS, norm_x)

    pl.semaphore_wait(barrier, 63)

    own_rows = pl.ds(pl.multiple_of(c * ROWS, 16), ROWS)
    send("g_half", g_ref.at[:, columns(other, HALF)], G.at[own_rows, columns(other, HALF)], sib)
    send("w_half", w_ref.at[:, columns(other, HALF)], WC.at[WIDTH : 2 * WIDTH, :], sib)
    send("x_half", x_ref.at[:, columns(other, HALF)], XRES.at[own_rows, :], sib)
    send("g_rest", g_ref.at[:, columns(mine, HALF)], G.at[own_rows, columns(mine, HALF)], sib)

    def slot_at(target):
        d = (y + 4 - target // 4) % 4
        r = (xl + (target // 2) % 2) % 2
        return (r * 4 + d) * 2 + c

    def slot_rows(slot):
        return pl.ds(pl.multiple_of(slot * ROWS, 16), ROWS)

    own_x = pltpu.make_async_copy(
        NX.at[:, columns(t * WIDTH, WIDTH)], XR.at[slot_rows(c), :], group_sem.at[X_IN]
    )
    own_x.start()

    def send_x(i, carry):
        target = (t + i) % 16
        grouped(
            NX.at[:, columns(target * WIDTH, WIDTH)], XR.at[slot_rows(slot_at(target)), :], X_OUT, X_IN, (s, target)
        )
        return carry

    lax.fori_loop(1, 16, send_x, 0)

    load_g.wait()
    recv("g_half")

    def own(cols, r=0, d=0, first=0, rows=CHIP):
        return G.at[block(r, d) + first : block(r, d) + first + rows, cols]

    send("a_p", own(cols_a), own(cols_a, 0, 3), yp)
    send("a_m", own(cols_a), own(cols_a, 0, 1), ym)
    send("b_x", own(cols_b), own(cols_b, 1, 0), pair)
    send("a_x0", own(cols_a), own(cols_a, 1, 0), pair)
    send("b_p", own(cols_b), own(cols_b, 0, 3), yp)
    send("b_m", own(cols_b), own(cols_b, 0, 1), ym)

    load_s.wait()
    QC[...] = jnp.zeros(QC.shape, F32)

    def norm_s(rows, i):
        normed, recip = normalize(SO[rows, :].astype(F32))
        NS[rows, :] = normed.astype(BF)
        QC[rows, :] = jnp.broadcast_to(recip, (STRIP, 128))

    strips(ROWS, norm_s)
    QS[...] = QC[...].T[0:8, :]

    def send_s(i, carry):
        target = (t + i) % 16
        slot = slot_at(target)
        grouped(
            NS.at[:, columns(target * WIDTH, WIDTH)], SR.at[slot_rows(slot), :], S_OUT, S_IN, (mirrored, target)
        )
        grouped(QS, QR.at[slot], Q_OUT, Q_IN, (mirrored, target))
        return carry

    lax.fori_loop(0, 16, send_s, 0)

    def to_sibling(cols, r, d, first=0, rows=CHIP):
        ref = own(cols, r, d, first, rows)
        grouped(ref, ref, G_OUT, G_IN, sib)

    recv("a_p")
    send("a_pp", own(cols_a, 0, 3, 0, ROWS), own(cols_a, 0, 2, 0, ROWS), yp)
    send("a_x3", own(cols_a, 0, 3), own(cols_a, 1, 3), pair)
    to_sibling(cols_a, 0, 3)
    recv("a_m")
    send("a_mm", own(cols_a, 0, 1, ROWS, ROWS), own(cols_a, 0, 2, ROWS, ROWS), ym)
    send("a_x1", own(cols_a, 0, 1), own(cols_a, 1, 1), pair)
    to_sibling(cols_a, 0, 1)
    recv("b_x")
    send("bx_p", own(cols_b, 1, 0), own(cols_b, 1, 3), yp)
    send("bx_m", own(cols_b, 1, 0), own(cols_b, 1, 1), ym)
    to_sibling(cols_b, 1, 0)

    arrived(XR, group_sem.at[X_IN], group_sem.at[X_OUT])
    scale = gain_ref[...].astype(F32)

    def make_hidden(rows, i):
        HN[rows, 0:WIDTH] = (XR[rows, :].astype(F32) * scale).astype(BF)

    strips(TOKENS, make_hidden)
    send("hidden", HN.at[:, 0:WIDTH], HN.at[:, WIDTH : 2 * WIDTH], sib)
    load_wc.wait()
    load_xres.wait()
    recv("w_half")
    recv("x_half")
    recv("hidden")

    def project(first, rows, start, width, step, store):
        def tile(i, carry):
            at = pl.multiple_of(start + i * step, 128)
            store(
                pl.multiple_of(i * step, 128),
                jnp.dot(HN[first : first + rows, :], WC[:, pl.ds(at, step)], preferred_element_type=F32),
            )
            return carry

        lax.fori_loop(0, width // step, tile, 0)

    def store_pair(at, value):
        here = pl.ds(at, 256)
        SA[0:CHIP, here] = (value[0:CHIP] + XRES[:, here].astype(F32)).astype(BF)
        SA[CHIP : 4 * CHIP, here] = value[CHIP : 4 * CHIP].astype(BF)

    project(0, 4 * CHIP, 0, CA, 256, store_pair)
    for d in (2, 1, 3, 0):
        send("ra%d" % d, SA.at[d * CHIP : (d + 1) * CHIP, :], RA.at[d * CHIP : (d + 1) * CHIP, :], pair)

    recv("b_p")
    send("b_pp", own(cols_b, 0, 3), own(cols_b, 0, 2), yp)
    to_sibling(cols_b, 0, 3)
    recv("bx_m")
    send("bx_mm", own(cols_b, 1, 1), own(cols_b, 1, 2), ym)
    to_sibling(cols_b, 1, 1)
    recv("a_pp")
    recv("a_mm")
    send("a_x2", own(cols_a, 0, 2), own(cols_a, 1, 2), pair)
    to_sibling(cols_a, 0, 2)
    recv("b_m")
    to_sibling(cols_b, 0, 1)
    recv("bx_p")
    to_sibling(cols_b, 1, 3)

    def store_b(at, value):
        PF[:, pl.ds(pl.multiple_of(CA + at, 128), 256)] = value

    project(0, TOKENS, CA, CB, 256, store_b)

    def combine(dst, terms, first=0, rows=CHIP):
        def body(at, i):
            total = None
            for ref, base, cols in terms:
                here = pl.ds(pl.multiple_of(base + first + i * STRIP, STRIP), STRIP)
                value = ref[here, cols].astype(F32)
                total = value if total is None else total + value
            ref, base = dst
            ref[pl.ds(pl.multiple_of(base + first + i * STRIP, STRIP), STRIP), :] = total.astype(BF)

        strips(rows, body)

    in_a, in_b = slice(0, CA), slice(CA, HALF)
    all_a, all_b = slice(0, CA), slice(0, CB)

    def part(ref, base, first=0, rows=CHIP):
        return ref.at[base + first : base + first + rows, :]

    combine((SB2, 0), [(PF, block(0, 2), in_b)])
    send("rb2p", part(SB2, 0), part(RB2, 0), yp)
    combine((SB2, CHIP), [(PF, block(1, 2), in_b)])
    send("rb2m", part(SB2, CHIP), part(RB2, CHIP), ym)
    combine((SBF, CHIP), [(PF, block(1, 1), in_b)])
    send("rbf01", part(SBF, CHIP), part(RBF, CHIP), yp)
    combine((SBF, 2 * CHIP), [(PF, block(0, 3), in_b)])
    send("rbf10", part(SBF, 2 * CHIP), part(RBF, 2 * CHIP), ym)

    def store_a(at, value):
        PF[4 * CHIP : 8 * CHIP, pl.ds(at, 256)] = value

    project(4 * CHIP, 4 * CHIP, 0, CA, 256, store_a)

    recv("ra2")
    combine((SA2, 0), [(PF, block(1, 2), in_a), (RA, 2 * CHIP, all_a)])
    send("ra2p", part(SA2, 0, 0, ROWS), part(RA2, 0, 0, ROWS), yp)
    send("ra2m", part(SA2, 0, ROWS, ROWS), part(RA2, 0, ROWS, ROWS), ym)
    recv("ra1")
    combine((SAF, 0), [(PF, block(1, 1), in_a), (RA, CHIP, all_a)], ROWS, ROWS)
    send("rafp1", part(SAF, 0, ROWS, ROWS), part(RAF, 0, ROWS, ROWS), yp)
    recv("ra3")
    combine((SAF, CHIP), [(PF, block(1, 3), in_a), (RA, 3 * CHIP, all_a)], 0, ROWS)
    send("rafm0", part(SAF, CHIP, 0, ROWS), part(RAF, CHIP, 0, ROWS), ym)

    for d in (0, 3, 1, 2):
        recv("a_x%d" % d)
        to_sibling(cols_a, 1, d)
    recv("b_pp")
    to_sibling(cols_b, 0, 2)
    recv("bx_mm")
    to_sibling(cols_b, 1, 2)

    recv("rb2p")
    combine((SBF, 0), [(PF, block(0, 1), in_b), (RB2, 0, all_b)])
    send("rbf00", part(SBF, 0), part(RBF, 0), yp)
    recv("rb2m")
    combine((SBF, 3 * CHIP), [(PF, block(1, 3), in_b), (RB2, CHIP, all_b)])
    send("rbf11", part(SBF, 3 * CHIP), part(RBF, 3 * CHIP), ym)
    recv("ra2p")
    combine((SAF, 0), [(PF, block(1, 1), in_a), (RA, CHIP, all_a), (RA2, 0, all_a)], 0, ROWS)
    send("rafp0", part(SAF, 0, 0, ROWS), part(RAF, 0, 0, ROWS), yp)
    recv("ra2m")
    combine((SAF, CHIP), [(PF, block(1, 3), in_a), (RA, 3 * CHIP, all_a), (RA2, 0, all_a)], ROWS, ROWS)
    send("rafm1", part(SAF, CHIP, ROWS, ROWS), part(RAF, CHIP, ROWS, ROWS), ym)

    recv("g_rest")
    arrived(G.at[CHIP:TOKENS, 0:HALF], group_sem.at[G_IN], group_sem.at[G_OUT])
    load_w.wait()
    DH[...] = jnp.zeros(DH.shape, F32)

    def hidden_grad(i, carry):
        here = pl.ds(pl.multiple_of(i * 512, 128), 512)
        DH[...] += lax.dot_general(
            G[:, here], W[:, here], (((1,), (1,)), ((), ())), preferred_element_type=F32
        )
        return carry

    lax.fori_loop(0, D // 512, hidden_grad, 0)

    arrived(SR, group_sem.at[S_IN], group_sem.at[S_OUT])
    arrived(QR, group_sem.at[Q_IN], group_sem.at[Q_OUT])
    EC[...] = jnp.zeros(EC.shape, F32)
    gg_ref[...] = jnp.zeros(gg_ref.shape, F32)
    lane = lax.broadcasted_iota(jnp.int32, (CHIP, 128), 1)

    def chip_of(b):
        return ((y + b % 4) % 4) * 2 + (xl + b // 4) % 2

    def chunk_sums(b, carry):
        rows = pl.ds(pl.multiple_of(b * CHIP, CHIP), CHIP)
        grad = DH[rows, :]
        normed = SR[rows, :].astype(F32)
        gg_ref[...] += jnp.sum(grad * normed, axis=0, keepdims=True)
        scaled = grad.astype(BF).astype(F32) * scale
        first = jnp.sum(scaled, axis=1, keepdims=True)
        second = jnp.sum(scaled * normed, axis=1, keepdims=True)
        at = 2 * chip_of(b)
        EC[0:CHIP, :] += jnp.where(lane == at, first, 0.0) + jnp.where(lane == at + 1, second, 0.0)
        return carry

    lax.fori_loop(0, 8, chunk_sums, 0)
    ES[...] = EC[...].T[0:16, :]
    own_e = pltpu.make_async_copy(ES, ER.at[c], group_sem.at[E_IN])
    own_e.start()

    def send_e(i, carry):
        target = (t + i) % 16
        grouped(ES, ER.at[slot_at(target)], E_OUT, E_IN, (s, target))
        return carry

    lax.fori_loop(1, 16, send_e, 0)

    def deliver(src, cols):
        for core in range(2):
            grouped(
                src.at[core * ROWS : (core + 1) * ROWS, :],
                next_ref.at[:, cols],
                N_OUT,
                N_IN,
                (following, y * 4 + (1 - xl) * 2 + core),
            )

    recv("rbf00")
    recv("rbf10")
    combine(
        (SBX, 0),
        [(PF, block(0, 0), in_b), (RBF, 0, all_b), (RBF, 2 * CHIP, all_b), (XRES, 0, in_b)],
    )
    send("rbx", SBX, RBX, pair)
    recv("ra0")
    for name in ("rafp0", "rafp1", "rafm0", "rafm1"):
        recv(name)
    combine((OA, 0), [(PF, block(1, 0), in_a), (RA, 0, all_a), (RAF, 0, all_a), (RAF, CHIP, all_a)])
    deliver(OA, cols_a)

    arrived(ER, group_sem.at[E_IN], group_sem.at[E_OUT])
    EC[...] = jnp.zeros(EC.shape, F32)
    total = ER[0]
    for k in range(1, 16):
        total = total + ER[k]
    QC[0:16, :] = total * (1.0 / D)
    for b in range(8):
        EC[2 * b : 2 * b + 2, :] = QC[pl.ds(2 * chip_of(b), 2), :]
    means = EC[...].T
    QC[...] = jnp.zeros(QC.shape, F32)
    for k in range(16):
        QC[k : k + 1, :] = QR[k, 0:1, :]
    recips = QC[...].T
    for b in range(8):
        for core in range(2):
            k = b * 2 + core
            rows = pl.ds(k * ROWS, ROWS)
            mean_e = means[core * ROWS : (core + 1) * ROWS, 2 * b : 2 * b + 1]
            mean_en = means[core * ROWS : (core + 1) * ROWS, 2 * b + 1 : 2 * b + 2]
            recip = recips[0:ROWS, k : k + 1]
            scaled = DH[rows, :].astype(BF).astype(F32) * scale
            inner = scaled - mean_e - SR[rows, :].astype(F32) * mean_en
            upstream = G[rows, columns(t * WIDTH, WIDTH)].astype(F32)
            GI[rows, :] = (upstream + recip * inner).astype(BF)
            target = chip_of(b) * 2 + core
            grouped(
                GI.at[rows, :], prev_ref.at[:, columns(t * WIDTH, WIDTH)], P_OUT, P_IN, (previous, target)
            )

    recv("rbf01")
    recv("rbf11")
    recv("rbx")
    combine(
        (OB, 0),
        [(PF, block(1, 0), in_b), (RBF, CHIP, all_b), (RBF, 3 * CHIP, all_b), (RBX, 0, all_b)],
    )
    deliver(OB, cols_b)

    BHT[...] = (SR[...].astype(F32) * scale).T.astype(BF)

    def weight_grad(i, carry):
        here = pl.ds(pl.multiple_of(i * 256, 128), 256)
        W[:, here] = jnp.dot(BHT[...], G[:, here], preferred_element_type=F32).astype(BF)
        pltpu.make_async_copy(W.at[:, here], wg_ref.at[:, here], local_sem.at[6]).start()
        return carry

    lax.fori_loop(0, D // 256, weight_grad, 0)

    pltpu.make_async_copy(W, wg_ref, local_sem.at[6]).wait()
    for copy in sent:
        copy.wait_send()
    left(NX.at[:, 0 : 15 * WIDTH], group_sem.at[X_OUT], group_sem.at[X_IN])
    left(NS, group_sem.at[S_OUT], group_sem.at[S_IN])
    left(QR, group_sem.at[Q_OUT], group_sem.at[Q_IN])
    left(ER.at[0:15], group_sem.at[E_OUT], group_sem.at[E_IN])
    left(G.at[CHIP:TOKENS, 0:HALF], group_sem.at[G_OUT], group_sem.at[G_IN])
    left(GI, group_sem.at[P_OUT], group_sem.at[P_IN])
    left(next_ref, group_sem.at[N_OUT], group_sem.at[N_IN])
    arrived(prev_ref, group_sem.at[P_IN], group_sem.at[P_OUT])
    arrived(next_ref, group_sem.at[N_IN], group_sem.at[N_OUT])


def local(forward_in, grad_out, saved_in, weight, gain):
    anywhere = pl.BlockSpec(memory_space=pl.ANY)
    vmem = pl.BlockSpec(memory_space=pltpu.VMEM)
    v = pltpu.VMEM
    outs = pl.pallas_call(
        kernel,
        out_shape=(
            jax.ShapeDtypeStruct((ROWS, D), BF),
            jax.ShapeDtypeStruct((ROWS, D), BF),
            jax.ShapeDtypeStruct((WIDTH, D), BF),
            jax.ShapeDtypeStruct((1, WIDTH), F32),
        ),
        in_specs=[anywhere, anywhere, anywhere, anywhere, vmem],
        out_specs=(anywhere, anywhere, anywhere, vmem),
        scratch_shapes=[
            v((TOKENS, D), BF),
            v((WIDTH, D), BF),
            v((2 * WIDTH, HALF), BF),
            v((TOKENS, HALF), F32),
            v((TOKENS, 2 * WIDTH), BF),
            v((TOKENS, WIDTH), BF),
            v((ROWS, D), BF),
            v((ROWS, D), BF),
            v((ROWS, D), BF),
            v((ROWS, D), BF),
            v((TOKENS, WIDTH), BF),
            v((WIDTH, TOKENS), BF),
            v((TOKENS, WIDTH), F32),
            v((TOKENS, WIDTH), BF),
            v((CHIP, HALF), BF),
            v((4 * CHIP, CA), BF),
            v((4 * CHIP, CA), BF),
            v((CHIP, CA), BF),
            v((CHIP, CA), BF),
            v((2 * CHIP, CA), BF),
            v((2 * CHIP, CA), BF),
            v((2 * CHIP, CB), BF),
            v((2 * CHIP, CB), BF),
            v((4 * CHIP, CB), BF),
            v((4 * CHIP, CB), BF),
            v((CHIP, CB), BF),
            v((CHIP, CB), BF),
            v((CHIP, CA), BF),
            v((CHIP, CB), BF),
            v((128, 128), F32),
            v((8, 128), F32),
            v((16, 8, 128), F32),
            v((128, 128), F32),
            v((16, 128), F32),
            v((16, 16, 128), F32),
            pltpu.SemaphoreType.DMA((48,)),
            pltpu.SemaphoreType.DMA((48,)),
            pltpu.SemaphoreType.DMA((7,)),
            pltpu.SemaphoreType.DMA((14,)),
        ],
        compiler_params=pltpu.CompilerParams(
            collective_id=0, has_side_effects=True, vmem_limit_bytes=60 * 2**20
        ),
        cost_estimate=pl.CostEstimate(
            flops=6 * TOKENS * WIDTH * D, bytes_accessed=20 * 2**20, transcendentals=0
        ),
    )(forward_in[0], grad_out[0], saved_in[0], weight[0], gain)
    next_input, prev_grad, weight_grad, gain_grad = outs
    return next_input[None], prev_grad[None], weight_grad[None], gain_grad


def solution(mesh):
    rows = P("section", "tensor", None)
    return jax.shard_map(
        local,
        mesh=mesh,
        in_specs=(rows, rows, rows, rows, P("section", "tensor")),
        out_specs=(rows, rows, rows, P("section", "tensor")),
        check_vma=False,
    )
```

```python
import jax
import jax.numpy as jnp
from jax import lax
from jax.experimental import pallas as pl
from jax.experimental.pallas import tpu as pltpu
from jax.sharding import PartitionSpec as P

D = 6144
TOKENS = 768
ROWS = 48
CHIP = 96
WIDTH = 384
PAIRED = 2 * WIDTH
HALF = D // 2
GA = 1408
GB = HALF - GA
CA = 1280
CB = HALF - CA
SUB_A = ((0, 768), (768, 512))
SUB_B = ((0, 768), (768, 512), (1280, 512))
ORDER = (
    "first_o", "norm_s", "norm_x", "first_s", "x01", "inchip", "x03", "x12", "x02", "x13", "s11", "x10", "x11", "ap",
    "bx", "s01", "s10", "k_ax0", "am", "bp", "s02", "s12", "hidden", "dh0", "k_ax3", "bxm", "proj_a", "k_bm", "s03",
    "proj_b", "k_ax1", "ax2", "s00", "k_bxp", "rbf10_1", "s13", "rbf10_0", "rb2m_0", "rb2m_1", "ra2_0", "dh1",
    "rb2p_0", "rb2p_1", "k_bxmm", "rb2p_2", "ra3_0", "ra0_0", "dh2", "k_ax2", "k_bpp", "proj_c", "s_sib", "rbf00_0",
    "dh3", "sums", "rbf01_0", "bht", "rbf11_0", "rbx_0", "rbf01_1", "rbf00_2", "rbf10_2", "rbf00_1", "ra1_0",
    "rb2m_2", "gi", "a2_0", "a3_0", "ra2_1", "fin_b_0", "p_go", "p00", "rbf11_1", "p01", "p12", "p03", "wg2", "a1_0",
    "p11", "a2m_0", "wg0", "p10", "ra3_1", "ra1_1", "p02", "rbx_1", "a2p_0", "p13", "rbf01_2", "rbf11_2", "a2_1",
    "a3_1", "a2m_1", "fin_a_0", "rbx_2", "fin_b_1", "a1_1", "ra0_1", "a2p_1", "fin_b_2", "fin_a_1", "wg3", "wg1",
)
STRIP = 16
BF = jnp.bfloat16
F32 = jnp.float32
EPS = 1e-05
MESH = pl.DeviceIdType.MESH


def block(r, d):
    return (r * 4 + d) * CHIP


def normalize(values):
    center = jnp.mean(values, axis=1, keepdims=True)
    shifted = values - center
    recip = lax.rsqrt(jnp.mean(shifted * shifted, axis=1, keepdims=True) + EPS)
    return shifted * recip, recip


def strips(rows, body):
    def step(i, carry):
        body(pl.ds(pl.multiple_of(i * STRIP, STRIP), STRIP), i)
        return carry

    lax.fori_loop(0, rows // STRIP, step, 0)


def columns(start, width):
    return pl.ds(pl.multiple_of(start, 128), width)


def kernel(
    x_ref, g_ref, s_ref, w_ref, gain_ref,
    next_ref, prev_ref, wg_ref, gg_ref,
    G, W, WC, PF, HN, XR, XO, NX, SO, NS, SR, SF, BHT, DH, GI, GR, XRES, GS,
    SA, RA, SA2, RA2, SAF, RAF, SB2, RB2, SBF, RBF, SBX, RBX, OA, OB,
    QC, QS, QR, QF, EC, ES, ER,
    send_sem, recv_sem, local_sem, group_sem, entered,
):
    s = lax.axis_index("section")
    t = lax.axis_index("tensor")
    y, xl, c = t // 4, (t // 2) % 2, t % 2
    mirrored, following, previous = 7 - s, (s + 1) % 8, (s + 7) % 8

    def at(section, along_y, row, core):
        return (section, ((y + along_y) % 4) * 4 + row * 2 + core)

    def row(r):
        return xl if r == 0 else 1 - xl

    sib = at(s, 0, xl, 1 - c)
    yp, ym = at(s, 1, xl, c), at(s, 3, xl, c)
    pair = at(s, 0, 1 - xl, c)

    mine = c * HALF
    other = (1 - c) * HALF
    cols_a = columns(mine, GA)
    cols_b = columns(mine + GA, GB)
    own_rows = pl.ds(pl.multiple_of(c * ROWS, 16), ROWS)
    sib_rows = pl.ds(pl.multiple_of((1 - c) * ROWS, 16), ROWS)

    names = {}
    sent = []

    def send(name, src, dst, device):
        i = names.setdefault(name, (len(names), dst))[0]
        copy = pltpu.make_async_remote_copy(
            src_ref=src, dst_ref=dst, send_sem=send_sem.at[i], recv_sem=recv_sem.at[i],
            device_id=device, device_id_type=MESH,
        )
        copy.start()
        sent.append(copy)

    def arrived(ref, sem, scratch_sem):
        pltpu.make_async_remote_copy(
            src_ref=ref, dst_ref=ref, send_sem=scratch_sem, recv_sem=sem, device_id=sib, device_id_type=MESH
        ).wait_recv()

    def left(ref, sem, scratch_sem):
        pltpu.make_async_remote_copy(
            src_ref=ref, dst_ref=ref, send_sem=sem, recv_sem=scratch_sem, device_id=sib, device_id_type=MESH
        ).wait_send()

    def recv(*wanted):
        for name in wanted:
            i, landing = names[name]
            arrived(landing, recv_sem.at[i], send_sem.at[i])

    E_IN, E_OUT, P_IN, P_OUT, N_IN, N_OUT = range(6)

    def grouped(src, dst, out, into, device):
        pltpu.make_async_remote_copy(
            src_ref=src, dst_ref=dst, send_sem=group_sem.at[out], recv_sem=group_sem.at[into],
            device_id=device, device_id_type=MESH,
        ).start()

    barrier = pltpu.get_barrier_semaphore()
    gateways = [at(section, 0, xl, c) for section in (mirrored, previous, following)]
    comrades = [at(s, e, row(r), core) for e in (1, 3, 0, 2) for r in range(2) for core in (c, 1 - c)]
    comrades = [comrade for i, comrade in enumerate(comrades) if i != 8]
    for friend in comrades + gateways:
        pl.semaphore_signal(barrier, inc=1, device_id=friend, device_id_type=MESH)

    load_x = pltpu.make_async_copy(x_ref, XO, local_sem.at[0])
    load_g = pltpu.make_async_copy(g_ref, G.at[own_rows, :], local_sem.at[1])
    load_s = pltpu.make_async_copy(s_ref, SO, local_sem.at[2])
    load_w = pltpu.make_async_copy(w_ref, W, local_sem.at[3])
    weight_rows = pl.ds(pl.multiple_of(c * WIDTH, 128), WIDTH)
    load_wc = pltpu.make_async_copy(w_ref.at[:, columns(mine, HALF)], WC.at[weight_rows, :], local_sem.at[4])
    load_xres = pltpu.make_async_copy(x_ref.at[:, columns(mine, HALF)], XRES.at[own_rows, :], local_sem.at[5])
    for load in (load_x, load_g, load_s, load_wc, load_xres, load_w):
        load.start()
    scale = gain_ref[...].astype(F32)
    GS[:, columns(c * WIDTH, WIDTH)] = jnp.broadcast_to(scale, (8, WIDTH))

    pl.semaphore_wait(barrier, 18)

    for gateway, entry in zip(gateways, (0, 2, 1)):
        pl.semaphore_signal(entered.at[entry], inc=1, device_id=gateway, device_id_type=MESH)

    def own(cols, r=0, d=0, first=0, rows=CHIP):
        return G.at[block(r, d) + first : block(r, d) + first + rows, cols]

    def near(cols, rows, r, d):
        return G.at[pl.ds(pl.multiple_of(block(r, d) + rows.start, 16), ROWS), cols]

    def from_here(e, r):
        return r * 4 + (4 - e) % 4

    tasks = {}

    def task(run):
        tasks[run.__name__] = run
        return run

    def first_step(part, a, b):
        send("b_x" + part, b[0], near(cols_b, b[1], 1, 0), pair)
        send("a_p" + part, a[0], near(cols_a, a[1], 0, 3), yp)
        send("a_m" + part, a[0], near(cols_a, a[1], 0, 1), ym)
        send("b_p" + part, b[0], near(cols_b, b[1], 0, 3), yp)
        send("b_m" + part, b[0], near(cols_b, b[1], 0, 1), ym)
        send("a_x0" + part, a[0], near(cols_a, a[1], 1, 0), pair)

    @task
    def first_o():
        send("g_half", g_ref.at[:, columns(other, HALF)], G.at[own_rows, columns(other, HALF)], sib)
        first_step("o", (g_ref.at[:, cols_a], own_rows), (g_ref.at[:, cols_b], own_rows))

    @task
    def first_s():
        recv("g_half")
        first_step("s", (G.at[sib_rows, cols_a], sib_rows), (G.at[sib_rows, cols_b], sib_rows))

    @task
    def inchip():
        send("gain", GS.at[:, columns(c * WIDTH, WIDTH)], GS.at[:, columns(c * WIDTH, WIDTH)], sib)
        send("w_half", w_ref.at[:, columns(other, HALF)], WC.at[weight_rows, :], sib)
        send("x_half", x_ref.at[:, columns(other, HALF)], XRES.at[own_rows, :], sib)
        send("g_rest", g_ref.at[:, columns(mine, HALF)], G.at[own_rows, columns(mine, HALF)], sib)

    @task
    def norm_x():
        load_x.wait()

        def body(rows, i):
            NX[rows, :] = normalize(XO[rows, :].astype(F32))[0].astype(BF)

        strips(ROWS, body)

    def features(e, r):
        return columns((((y + e) % 4) * 2 + row(r)) * PAIRED, PAIRED)

    def x_task(e, r):
        def run():
            send("x%d%d" % (r, e), NX.at[:, features(e, r)], XR.at[from_here(e, r)], at(s, e, row(r), c))

        tasks["x%d%d" % (r, e)] = run

    @task
    def norm_s():
        load_s.wait()
        QC[...] = jnp.zeros(QC.shape, F32)

        def body(rows, i):
            normed, recip = normalize(SO[rows, :].astype(F32))
            NS[rows, :] = normed.astype(BF)
            QC[rows, :] = jnp.broadcast_to(recip, (STRIP, 128))

        strips(ROWS, body)
        QS[...] = QC[...].T[0:8, :]
        pl.semaphore_wait(entered.at[0], 1)

    def s_task(e, r):
        def run():
            target = at(mirrored, e, row(r), c)
            send("s%d%d" % (r, e), NS.at[:, features(e, r)], SR.at[from_here(e, r)], target)
            send("q%d%d" % (r, e), QS, QR.at[from_here(e, r)], target)

        tasks["s%d%d" % (r, e)] = run

    for e in range(4):
        for r in range(2):
            s_task(e, r)
            if (e, r) != (0, 0):
                x_task(e, r)

    def share(name, cols, r, d):
        ref = own(cols, r, d)
        send(name, ref, ref, sib)

    @task
    def bx():
        recv("b_xo", "b_xs")
        send("bx_p", own(cols_b, 1, 0), own(cols_b, 1, 3), yp)
        send("bx_m", own(cols_b, 1, 0), own(cols_b, 1, 1), ym)
        share("Gb10", cols_b, 1, 0)

    @task
    def ap():
        recv("a_po", "a_ps")
        send("a_pp", own(cols_a, 0, 3, 0, ROWS), own(cols_a, 0, 2, 0, ROWS), yp)
        send("a_x3", own(cols_a, 0, 3), own(cols_a, 1, 3), pair)
        share("Ga03", cols_a, 0, 3)

    @task
    def am():
        recv("a_mo", "a_ms")
        send("a_mm", own(cols_a, 0, 1, ROWS, ROWS), own(cols_a, 0, 2, ROWS, ROWS), ym)
        send("a_x1", own(cols_a, 0, 1), own(cols_a, 1, 1), pair)
        share("Ga01", cols_a, 0, 1)

    @task
    def bp():
        recv("b_po", "b_ps")
        send("b_pp", own(cols_b, 0, 3), own(cols_b, 0, 2), yp)
        share("Gb03", cols_b, 0, 3)

    @task
    def bxm():
        recv("bx_m")
        send("bx_mm", own(cols_b, 1, 1), own(cols_b, 1, 2), ym)
        share("Gb11", cols_b, 1, 1)

    @task
    def ax2():
        recv("a_pp", "a_mm")
        send("a_x2", own(cols_a, 0, 2), own(cols_a, 1, 2), pair)
        share("Ga02", cols_a, 0, 2)

    def keep_task(name, wanted, cols, r, d):
        def run():
            recv(*wanted)
            share("G%s%d%d" % ("a" if cols is cols_a else "b", r, d), cols, r, d)

        tasks[name] = run

    keep_task("k_bm", ("b_mo", "b_ms"), cols_b, 0, 1)
    keep_task("k_bxp", ("bx_p",), cols_b, 1, 3)
    keep_task("k_ax0", ("a_x0o", "a_x0s"), cols_a, 1, 0)
    keep_task("k_ax3", ("a_x3",), cols_a, 1, 3)
    keep_task("k_ax1", ("a_x1",), cols_a, 1, 1)
    keep_task("k_bpp", ("b_pp",), cols_b, 0, 2)
    keep_task("k_bxmm", ("bx_mm",), cols_b, 1, 2)
    keep_task("k_ax2", ("a_x2",), cols_a, 1, 2)

    @task
    def hidden():
        recv("gain")
        both = GS[0:1, :]
        for d in (0, 3, 1, 2):
            for r in range(2):
                if (d, r) == (0, 0):
                    values = NX[:, features(0, 0)]
                else:
                    recv("x%d%d" % (r, (4 - d) % 4))
                    values = XR[r * 4 + d]
                HN[r * 4 + d, own_rows, :] = (values.astype(F32) * both).astype(BF)
        send("hid", HN.at[:, own_rows, :], HN.at[:, own_rows, :], sib)

    def project(first, chips, start, width, store):
        def tile(i, carry):
            here = pl.multiple_of(i * 256, 256)
            there = pl.ds(pl.multiple_of(start + here, 256), 256)
            store(
                pl.ds(here, 256),
                there,
                jnp.dot(
                    HN[first : first + chips].reshape(chips * CHIP, PAIRED),
                    WC[:, there],
                    preferred_element_type=F32,
                ),
            )
            return carry

        lax.fori_loop(0, width // 256, tile, 0)

    @task
    def proj_a():
        pl.semaphore_wait(entered.at[2], 1)
        load_wc.wait()
        load_xres.wait()
        recv("hid", "w_half", "x_half")

        def store(here, there, value):
            SA[0:CHIP, here] = (value[0:CHIP] + XRES[:, here].astype(F32)).astype(BF)
            SA[CHIP : 4 * CHIP, here] = value[CHIP : 4 * CHIP].astype(BF)

        project(0, 4, 0, CA, store)

    @task
    def proj_b():
        def store(here, there, value):
            PF[:, there] = value

        project(0, 8, CA, CB, store)

    @task
    def proj_c():
        def store(here, there, value):
            PF[4 * CHIP : 8 * CHIP, here] = value

        project(4, 4, 0, CA, store)

    def combine(dst, terms, width, first=0, rows=CHIP):
        def body(strip, i):
            total = None
            for ref, base, start in terms:
                here = pl.ds(pl.multiple_of(base + first + i * STRIP, STRIP), STRIP)
                value = ref[here, start : start + width].astype(F32)
                total = value if total is None else total + value
            ref, base, start = dst
            ref[pl.ds(pl.multiple_of(base + first + i * STRIP, STRIP), STRIP), start : start + width] = total.astype(BF)

        strips(rows, body)

    def deliver(src, start, width, offset):
        for core in range(2):
            grouped(
                src.at[core * ROWS : (core + 1) * ROWS, start : start + width],
                next_ref.at[:, columns(mine + offset + start, width)],
                N_OUT,
                N_IN,
                at(following, 0, 1 - xl, core),
            )

    def reduce_a(k):
        a, w = SUB_A[k]

        def pass_on(name, src, dst, first, rows, device):
            send(
                "%s_%d" % (name, k), src.at[first : first + rows, a : a + w], dst.at[first : first + rows, a : a + w], device
            )

        def cross(d):
            def run():
                pass_on("ra%d" % d, SA, RA, d * CHIP, CHIP, pair)

            tasks["ra%d_%d" % (d, k)] = run

        for d in range(4):
            cross(d)

        def a2():
            recv("ra2_%d" % k)
            combine((SA2, 0, a), [(PF, block(1, 2), a), (RA, 2 * CHIP, a)], w)
            pass_on("ra2p", SA2, RA2, 0, ROWS, yp)
            pass_on("ra2m", SA2, RA2, ROWS, ROWS, ym)

        def a1():
            recv("ra1_%d" % k)
            combine((SAF, 0, a), [(PF, block(1, 1), a), (RA, CHIP, a)], w, ROWS, ROWS)
            pass_on("rafp1", SAF, RAF, ROWS, ROWS, yp)

        def a3():
            recv("ra3_%d" % k)
            combine((SAF, CHIP, a), [(PF, block(1, 3), a), (RA, 3 * CHIP, a)], w, 0, ROWS)
            pass_on("rafm0", SAF, RAF, CHIP, ROWS, ym)

        def a2p():
            recv("ra2p_%d" % k)
            combine((SAF, 0, a), [(PF, block(1, 1), a), (RA, CHIP, a), (RA2, 0, a)], w, 0, ROWS)
            pass_on("rafp0", SAF, RAF, 0, ROWS, yp)

        def a2m():
            recv("ra2m_%d" % k)
            combine((SAF, CHIP, a), [(PF, block(1, 3), a), (RA, 3 * CHIP, a), (RA2, 0, a)], w, ROWS, ROWS)
            pass_on("rafm1", SAF, RAF, CHIP + ROWS, ROWS, ym)

        def fin_a():
            for name in ("ra0", "rafp0", "rafp1", "rafm0", "rafm1"):
                recv("%s_%d" % (name, k))
            combine((OA, 0, a), [(PF, block(1, 0), a), (RA, 0, a), (RAF, 0, a), (RAF, CHIP, a)], w)
            deliver(OA, a, w, 0)

        for run in (a2, a1, a3, a2p, a2m, fin_a):
            tasks["%s_%d" % (run.__name__, k)] = run

    def reduce_b(k):
        a, w = SUB_B[k]

        def hand(name, src, dst, first, device, terms):
            combine((src, first, a), terms, w)
            send(
                "%s_%d" % (name, k), src.at[first : first + CHIP, a : a + w], dst.at[first : first + CHIP, a : a + w], device
            )

        def rb2p():
            hand("rb2p", SB2, RB2, 0, yp, [(PF, block(0, 2), CA + a)])

        def rb2m():
            hand("rb2m", SB2, RB2, CHIP, ym, [(PF, block(1, 2), CA + a)])

        def rbf01():
            hand("rbf01", SBF, RBF, CHIP, yp, [(PF, block(1, 1), CA + a)])

        def rbf10():
            hand("rbf10", SBF, RBF, 2 * CHIP, ym, [(PF, block(0, 3), CA + a)])

        def rbf00():
            recv("rb2p_%d" % k)
            hand("rbf00", SBF, RBF, 0, yp, [(PF, block(0, 1), CA + a), (RB2, 0, a)])

        def rbf11():
            recv("rb2m_%d" % k)
            hand("rbf11", SBF, RBF, 3 * CHIP, ym, [(PF, block(1, 3), CA + a), (RB2, CHIP, a)])

        def rbx():
            recv("rbf00_%d" % k, "rbf10_%d" % k)
            hand(
                "rbx", SBX, RBX, 0, pair,
                [(PF, block(0, 0), CA + a), (RBF, 0, a), (RBF, 2 * CHIP, a), (XRES, 0, CA + a)],
            )

        def fin_b():
            recv("rbf01_%d" % k, "rbf11_%d" % k, "rbx_%d" % k)
            combine((OB, 0, a), [(PF, block(1, 0), CA + a), (RBF, CHIP, a), (RBF, 3 * CHIP, a), (RBX, 0, a)], w)
            deliver(OB, a, w, CA)

        for run in (rb2p, rb2m, rbf01, rbf10, rbf00, rbf11, rbx, fin_b):
            tasks["%s_%d" % (run.__name__, k)] = run

    for k in range(len(SUB_A)):
        reduce_a(k)
    for k in range(len(SUB_B)):
        reduce_b(k)

    def dh_task(i, blocks, wanted):
        def run():
            recv(*wanted)
            if i == 0:
                load_g.wait()
                load_w.wait()
            first, second = (pl.ds(block(r, d), CHIP) for r, d in blocks)
            DH[first, :] = jnp.zeros((CHIP, WIDTH), F32)
            DH[second, :] = jnp.zeros((CHIP, WIDTH), F32)

            def step(j, carry):
                here = pl.ds(pl.multiple_of(j * 1024, 1024), 1024)
                part = lax.dot_general(
                    jnp.concatenate([G[first, here], G[second, here]], axis=0),
                    W[:, here],
                    (((1,), (1,)), ((), ())),
                    preferred_element_type=F32,
                )
                DH[first, :] += part[0:CHIP]
                DH[second, :] += part[CHIP : 2 * CHIP]
                return carry

            lax.fori_loop(0, D // 1024, step, 0)

        tasks["dh%d" % i] = run

    dh_task(0, ((0, 0), (1, 0)), ("g_rest", "Ga10", "Gb10"))
    dh_task(1, ((0, 1), (0, 3)), ("Ga03", "Ga01", "Gb03", "Gb01"))
    dh_task(2, ((1, 1), (1, 3)), ("Ga13", "Ga11", "Gb13", "Gb11"))
    dh_task(3, ((0, 2), (1, 2)), ("Ga02", "Ga12", "Gb02", "Gb12"))

    def local_copy(i, src, dst):
        copy = pltpu.make_async_copy(src, dst, local_sem.at[i])
        copy.start()
        return copy

    kept = {}

    @task
    def s_sib():
        for e in (1, 3, 2, 0):
            for r in range(2):
                recv("s%d%d" % (r, e), "q%d%d" % (r, e))
        send("s_sib", SR.at[:, :, columns((1 - c) * WIDTH, WIDTH)], SF.at[:, own_rows, :], sib)
        send("q_sib", QR, QF.at[:, c], sib)
        kept["s"] = local_copy(7, SR.at[:, :, columns(c * WIDTH, WIDTH)], SF.at[:, own_rows, :])
        kept["q"] = local_copy(8, QR, QF.at[:, c])

    def chip_of(b):
        return ((y + b % 4) % 4) * 2 + (xl + b // 4) % 2

    @task
    def sums():
        recv("s_sib", "q_sib")
        kept["s"].wait()
        kept["q"].wait()
        EC[...] = jnp.zeros(EC.shape, F32)
        gg_ref[...] = jnp.zeros(gg_ref.shape, F32)
        lane = lax.broadcasted_iota(jnp.int32, (CHIP, 128), 1)

        def chunk(b, carry):
            grad = DH[pl.ds(pl.multiple_of(b * CHIP, CHIP), CHIP), :]
            normed = SF[b].astype(F32)
            gg_ref[...] += jnp.sum(grad * normed, axis=0, keepdims=True)
            scaled = grad.astype(BF).astype(F32) * scale
            first = jnp.sum(scaled, axis=1, keepdims=True)
            second = jnp.sum(scaled * normed, axis=1, keepdims=True)
            place = 2 * chip_of(b)
            EC[0:CHIP, :] += jnp.where(lane == place, first, 0.0) + jnp.where(lane == place + 1, second, 0.0)
            return carry

        lax.fori_loop(0, 8, chunk, 0)
        ES[...] = EC[...].T[0:16, :]
        pltpu.make_async_copy(ES, ER.at[c], group_sem.at[E_IN]).start()
        for e in (2, 1, 3, 0):
            for r in range(2):
                grouped(ES, ER.at[from_here(e, r) * 2 + c], E_OUT, E_IN, at(s, e, row(r), 1 - c))
                if (e, r) != (0, 0):
                    grouped(ES, ER.at[from_here(e, r) * 2 + c], E_OUT, E_IN, at(s, e, row(r), c))

    @task
    def gi():
        arrived(ER, group_sem.at[E_IN], group_sem.at[E_OUT])
        total = ER[0]
        for k in range(1, 16):
            total = total + ER[k]
        QC[0:16, :] = total * (1.0 / D)
        EC[...] = jnp.zeros(EC.shape, F32)
        for b in range(8):
            EC[2 * b : 2 * b + 2, :] = QC[pl.ds(2 * chip_of(b), 2), :]
        means = EC[...].T
        QC[...] = jnp.zeros(QC.shape, F32)
        for b in range(8):
            for core in range(2):
                QC[b * 2 + core : b * 2 + core + 1, :] = QF[b, core, 0:1, :]
        recips = QC[...].T
        for b in range(8):
            for core in range(2):
                k = b * 2 + core
                part = slice(core * ROWS, (core + 1) * ROWS)
                rows = slice(k * ROWS, (k + 1) * ROWS)
                mean_e = means[part, 2 * b : 2 * b + 1]
                mean_en = means[part, 2 * b + 1 : 2 * b + 2]
                recip = recips[0:ROWS, k : k + 1]
                scaled = DH[rows, :].astype(BF).astype(F32) * scale
                inner = scaled - mean_e - SF[b, part, :].astype(F32) * mean_en
                upstream = G[rows, columns(t * WIDTH, WIDTH)].astype(F32)
                GI[b, part, :] = (upstream + recip * inner).astype(BF)
        here = columns(c * WIDTH, WIDTH)
        send("p_sib", GI.at[:, sib_rows, :], GR.at[:, :, here], sib)
        kept["p"] = local_copy(9, GI.at[:, own_rows, :], GR.at[:, :, here])

    @task
    def p_go():
        pl.semaphore_wait(entered.at[1], 1)
        kept["p"].wait()
        recv("p_sib")

    def p_task(e, r):
        def run():
            grouped(GR.at[r * 4 + e], prev_ref.at[:, features(0, 0)], P_OUT, P_IN, at(previous, e, row(r), c))

        tasks["p%d%d" % (r, e)] = run

    for e in range(4):
        for r in range(2):
            p_task(e, r)

    @task
    def bht():
        BHT[...] = (SF[...].reshape(TOKENS, WIDTH).astype(F32) * scale).T.astype(BF)

    def wg_task(i):
        def run():
            def step(j, carry):
                here = pl.ds(pl.multiple_of(j * 256, 256), 256)
                W[:, here] = jnp.dot(BHT[...], G[:, here], preferred_element_type=F32).astype(BF)
                pltpu.make_async_copy(W.at[:, here], wg_ref.at[:, here], local_sem.at[6]).start()
                return carry

            lax.fori_loop(i * 6, (i + 1) * 6, step, 0)

        tasks["wg%d" % i] = run

    for i in range(4):
        wg_task(i)

    for name in ORDER:
        tasks[name]()

    pltpu.make_async_copy(W, wg_ref, local_sem.at[6]).wait()
    for copy in sent:
        copy.wait_send()
    left(ER.at[0:15], group_sem.at[E_OUT], group_sem.at[E_IN])
    left(next_ref, group_sem.at[N_OUT], group_sem.at[N_IN])
    left(prev_ref, group_sem.at[P_OUT], group_sem.at[P_IN])
    arrived(prev_ref, group_sem.at[P_IN], group_sem.at[P_OUT])
    arrived(next_ref, group_sem.at[N_IN], group_sem.at[N_OUT])


PARTS = 6


def hand_over(next_in, prev_in, wg_in, gg_in, next_out, prev_out, wg_out, gg_out, near_next, near_prev, near_wg, sems):
    gg_out[...] = gg_in[...]
    rows = WIDTH // PARTS
    moves = [(wg_in.at[i], near_wg.at[i], wg_out.at[i]) for i in (pl.ds(k * rows, rows) for k in range(PARTS))]
    moves += [(next_in, near_next, next_out), (prev_in, near_prev, prev_out)]
    inward = [pltpu.make_async_copy(src, via, sems.at[0, i]) for i, (src, via, dst) in enumerate(moves)]
    outward = [pltpu.make_async_copy(via, dst, sems.at[1, i]) for i, (src, via, dst) in enumerate(moves)]
    for copy in inward:
        copy.start()
    for before, after in zip(inward, outward):
        before.wait()
        after.start()
    for copy in outward:
        copy.wait()


def local(forward_in, grad_out, saved_in, weight, gain):
    anywhere = pl.BlockSpec(memory_space=pl.ANY)
    vmem = pl.BlockSpec(memory_space=pltpu.VMEM)
    v = pltpu.VMEM
    out_shape = (
        jax.ShapeDtypeStruct((ROWS, D), BF),
        jax.ShapeDtypeStruct((ROWS, D), BF),
        jax.ShapeDtypeStruct((WIDTH, D), BF),
        jax.ShapeDtypeStruct((1, WIDTH), F32),
    )
    raw = pl.pallas_call(
        kernel,
        out_shape=out_shape,
        in_specs=[anywhere, anywhere, anywhere, anywhere, vmem],
        out_specs=(anywhere, anywhere, anywhere, vmem),
        scratch_shapes=[
            v((TOKENS, D), BF),
            v((WIDTH, D), BF),
            v((PAIRED, HALF), BF),
            v((TOKENS, HALF), F32),
            v((8, CHIP, PAIRED), BF),
            v((8, ROWS, PAIRED), BF),
            v((ROWS, D), BF),
            v((ROWS, D), BF),
            v((ROWS, D), BF),
            v((ROWS, D), BF),
            v((8, ROWS, PAIRED), BF),
            v((8, CHIP, WIDTH), BF),
            v((WIDTH, TOKENS), BF),
            v((TOKENS, WIDTH), F32),
            v((8, CHIP, WIDTH), BF),
            v((8, ROWS, PAIRED), BF),
            v((CHIP, HALF), BF),
            v((8, PAIRED), F32),
            v((4 * CHIP, CA), BF),
            v((4 * CHIP, CA), BF),
            v((CHIP, CA), BF),
            v((CHIP, CA), BF),
            v((2 * CHIP, CA), BF),
            v((2 * CHIP, CA), BF),
            v((2 * CHIP, CB), BF),
            v((2 * CHIP, CB), BF),
            v((4 * CHIP, CB), BF),
            v((4 * CHIP, CB), BF),
            v((CHIP, CB), BF),
            v((CHIP, CB), BF),
            v((CHIP, CA), BF),
            v((CHIP, CB), BF),
            v((128, 128), F32),
            v((8, 128), F32),
            v((8, 8, 128), F32),
            v((8, 2, 8, 128), F32),
            v((128, 128), F32),
            v((16, 128), F32),
            v((16, 16, 128), F32),
            pltpu.SemaphoreType.DMA((128,)),
            pltpu.SemaphoreType.DMA((128,)),
            pltpu.SemaphoreType.DMA((10,)),
            pltpu.SemaphoreType.DMA((6,)),
            pltpu.SemaphoreType.REGULAR((3,)),
        ],
        compiler_params=pltpu.CompilerParams(
            collective_id=0, has_side_effects=True, vmem_limit_bytes=60 * 2**20
        ),
        cost_estimate=pl.CostEstimate(
            flops=6 * TOKENS * WIDTH * D, bytes_accessed=20 * 2**20, transcendentals=0
        ),
    )(forward_in[0], grad_out[0], saved_in[0], weight[0], gain)
    next_input, prev_grad, weight_grad, gain_grad = pl.pallas_call(
        hand_over,
        out_shape=out_shape,
        in_specs=[pl.BlockSpec(memory_space=pltpu.HBM)] * 3 + [vmem],
        out_specs=(anywhere, anywhere, anywhere, vmem),
        scratch_shapes=[
            v((ROWS, D), BF),
            v((ROWS, D), BF),
            v((WIDTH, D), BF),
            pltpu.SemaphoreType.DMA((2, PARTS + 2)),
        ],
        cost_estimate=pl.CostEstimate(flops=0, bytes_accessed=12 * 2**20, transcendentals=0),
    )(*raw)
    return next_input[None], prev_grad[None], weight_grad[None], gain_grad


def solution(mesh):
    rows = P("section", "tensor", None)
    return jax.shard_map(
        local,
        mesh=mesh,
        in_specs=(rows, rows, rows, rows, P("section", "tensor")),
        out_specs=(rows, rows, rows, P("section", "tensor")),
        check_vma=False,
    )
```

```python
import jax
import jax.numpy as jnp
from jax import lax
from jax.experimental import pallas as pl
from jax.experimental.pallas import tpu as pltpu
from jax.sharding import PartitionSpec as P

D = 6144
TOKENS = 768
ROWS = 48
CHIP = 96
WIDTH = 384
PAIRED = 2 * WIDTH
HALF = D // 2
GA = 1408
GB = HALF - GA
CA = 1280
CB = HALF - CA
SUB_A = ((0, 768), (768, 512))
SUB_B = ((0, 768), (768, 512), (1280, 512))
ORDER = (
    6, 0, 9, 7, 1, 23, 19, 2, 17, 25,
    8, 3, 21, 10, 11, 15, 26, 4, 13, 12,
    5, 22, 28, 40, 27, 34, 24, 32, 29, 30,
    41, 18, 20, 42, 64, 31, 14, 36, 75, 16,
    35, 43, 37, 89, 46, 33, 67, 47, 65, 88,
    66, 68, 39, 80, 45, 81, 38, 56, 83, 90,
    92, 91, 93, 94, 72, 84, 69, 70, 104, 48,
    95, 97, 55, 50, 99, 103, 102, 82, 96, 58,
    71, 44, 49, 106, 86, 52, 51, 57, 73, 54,
    101, 59, 76, 105, 85, 53, 100, 98, 61, 60,
    62, 77, 107, 78, 74, 87, 63, 79, 108,
)
STRIP = 16
ROUNDS = 5
BF = jnp.bfloat16
F32 = jnp.float32
EPS = 1e-05
MESH = pl.DeviceIdType.MESH


def block(r, d):
    return (r * 4 + d) * CHIP


def normalize(values):
    center = jnp.mean(values, axis=1, keepdims=True)
    shifted = values - center
    recip = lax.rsqrt(jnp.mean(shifted * shifted, axis=1, keepdims=True) + EPS)
    return shifted * recip, recip


def strips(rows, body):
    def step(i, carry):
        body(pl.ds(pl.multiple_of(i * STRIP, STRIP), STRIP), i)
        return carry

    lax.fori_loop(0, rows // STRIP, step, 0)


def columns(start, width):
    return pl.ds(pl.multiple_of(start, 128), width)


def kernel(
    x_ref, g_ref, s_ref, w_ref, gain_ref,
    next_ref, prev_ref, wg_ref, gg_ref,
    G, W, WC, PF, HN, XR, XO, NX, SO, NS, SR, SF, BHT, DH, GI, XRES, GS,
    SA, RA, SA2, RA2, SAF, RAF, SB2, RB2, SBF, RBF, SBX, RBX, OA, OB,
    QC, QS, QR, QF, EC, ES, ER, MT, RT,
    send_sem, recv_sem, local_sem, group_sem, heard,
):
    s = lax.axis_index("section")
    t = lax.axis_index("tensor")
    y, xl, c = t // 4, (t // 2) % 2, t % 2
    mirrored, following, previous = 7 - s, (s + 1) % 8, (s + 7) % 8

    def at(section, along_y, row, core):
        return (section, ((y + along_y) % 4) * 4 + row * 2 + core)

    def row(r):
        return xl if r == 0 else 1 - xl

    sib = at(s, 0, xl, 1 - c)
    yp, ym = at(s, 1, xl, c), at(s, 3, xl, c)
    pair = at(s, 0, 1 - xl, c)

    mine = c * HALF
    other = (1 - c) * HALF
    cols_a = columns(mine, GA)
    cols_b = columns(mine + GA, GB)
    own_rows = pl.ds(pl.multiple_of(c * ROWS, 16), ROWS)
    sib_rows = pl.ds(pl.multiple_of((1 - c) * ROWS, 16), ROWS)

    names = {}
    sent = []

    def send(name, src, dst, device):
        i = names.setdefault(name, (len(names), dst))[0]
        copy = pltpu.make_async_remote_copy(
            src_ref=src, dst_ref=dst, send_sem=send_sem.at[i], recv_sem=recv_sem.at[i],
            device_id=device, device_id_type=MESH,
        )
        copy.start()
        sent.append(copy)

    def arrived(ref, sem, scratch_sem):
        pltpu.make_async_remote_copy(
            src_ref=ref, dst_ref=ref, send_sem=scratch_sem, recv_sem=sem, device_id=sib, device_id_type=MESH
        ).wait_recv()

    def left(ref, sem, scratch_sem):
        pltpu.make_async_remote_copy(
            src_ref=ref, dst_ref=ref, send_sem=sem, recv_sem=scratch_sem, device_id=sib, device_id_type=MESH
        ).wait_send()

    def recv(*wanted):
        for name in wanted:
            i, landing = names[name]
            arrived(landing, recv_sem.at[i], send_sem.at[i])

    E_IN, E_OUT, P_IN, P_OUT, N_IN, N_OUT = range(6)

    def grouped(src, dst, out, into, device):
        pltpu.make_async_remote_copy(
            src_ref=src, dst_ref=dst, send_sem=group_sem.at[out], recv_sem=group_sem.at[into],
            device_id=device, device_id_type=MESH,
        ).start()

    barrier = pltpu.get_barrier_semaphore()
    across = at(s + 1 - 2 * (s % 2), 0, 1 - xl, c)
    nearest = [sib, yp, ym, pair, across, at((s + 2) % 8, 0, xl, c), at((s + 6) % 8, 0, xl, c)]
    for friend in nearest:
        pl.semaphore_signal(barrier, inc=1, device_id=friend, device_id_type=MESH)

    load_x = pltpu.make_async_copy(x_ref, XO, local_sem.at[0])
    load_g = pltpu.make_async_copy(g_ref, G.at[own_rows, :], local_sem.at[1])
    load_s = pltpu.make_async_copy(s_ref, SO, local_sem.at[2])
    load_w = pltpu.make_async_copy(w_ref, W, local_sem.at[3])
    weight_rows = pl.ds(pl.multiple_of(c * WIDTH, 128), WIDTH)
    load_wc = pltpu.make_async_copy(w_ref.at[:, columns(mine, HALF)], WC.at[weight_rows, :], local_sem.at[4])
    load_xres = pltpu.make_async_copy(x_ref.at[:, columns(mine, HALF)], XRES.at[own_rows, :], local_sem.at[5])
    for load in (load_x, load_g, load_s, load_wc, load_xres, load_w):
        load.start()
    scale = gain_ref[...].astype(F32)
    GS[:, columns(c * WIDTH, WIDTH)] = jnp.broadcast_to(scale, (8, WIDTH))

    pl.semaphore_wait(barrier, len(nearest))

    def own(cols, r=0, d=0, first=0, rows=CHIP):
        return G.at[block(r, d) + first : block(r, d) + first + rows, cols]

    def near(cols, rows, r, d):
        return G.at[pl.ds(pl.multiple_of(block(r, d) + rows.start, 16), ROWS), cols]

    def from_here(e, r):
        return r * 4 + (4 - e) % 4

    tasks = []

    def task(run):
        tasks.append(run)
        return run

    def round_task(i):
        def run():
            if i > 1:
                pl.semaphore_wait(heard.at[i - 2], len(nearest))
            if i <= ROUNDS:
                for friend in nearest:
                    pl.semaphore_signal(heard.at[i - 1], inc=1, device_id=friend, device_id_type=MESH)

        tasks.append(run)

    for i in range(1, ROUNDS + 2):
        round_task(i)

    def first_step(part, a, b):
        send(("b_x", part), b[0], near(cols_b, b[1], 1, 0), pair)
        send(("a_p", part), a[0], near(cols_a, a[1], 0, 3), yp)
        send(("a_m", part), a[0], near(cols_a, a[1], 0, 1), ym)
        send(("b_p", part), b[0], near(cols_b, b[1], 0, 3), yp)
        send(("b_m", part), b[0], near(cols_b, b[1], 0, 1), ym)
        send(("a_x0", part), a[0], near(cols_a, a[1], 1, 0), pair)

    @task
    def first_o():
        send("g_half", g_ref.at[:, columns(other, HALF)], G.at[own_rows, columns(other, HALF)], sib)
        first_step(0, (g_ref.at[:, cols_a], own_rows), (g_ref.at[:, cols_b], own_rows))

    @task
    def first_s():
        recv("g_half")
        first_step(1, (G.at[sib_rows, cols_a], sib_rows), (G.at[sib_rows, cols_b], sib_rows))

    @task
    def inchip():
        send("gain", GS.at[:, columns(c * WIDTH, WIDTH)], GS.at[:, columns(c * WIDTH, WIDTH)], sib)
        send("w_half", w_ref.at[:, columns(other, HALF)], WC.at[weight_rows, :], sib)
        send("x_half", x_ref.at[:, columns(other, HALF)], XRES.at[own_rows, :], sib)
        send("g_rest", g_ref.at[:, columns(mine, HALF)], G.at[own_rows, columns(mine, HALF)], sib)

    @task
    def norm_x():
        load_x.wait()

        def body(rows, i):
            NX[rows, :] = normalize(XO[rows, :].astype(F32))[0].astype(BF)

        strips(ROWS, body)

    def features(e, r):
        return columns((((y + e) % 4) * 2 + row(r)) * PAIRED, PAIRED)

    def x_task(e, r):
        def run():
            send(("x", r, e), NX.at[:, features(e, r)], XR.at[from_here(e, r)], at(s, e, row(r), c))

        tasks.append(run)

    @task
    def norm_s():
        load_s.wait()
        QC[...] = jnp.zeros(QC.shape, F32)

        def body(rows, i):
            normed, recip = normalize(SO[rows, :].astype(F32))
            NS[rows, :] = normed.astype(BF)
            QC[rows, :] = jnp.broadcast_to(recip, (STRIP, 128))

        strips(ROWS, body)
        QS[...] = QC[...].T[0:8, :]

    def s_task(e, r):
        def run():
            target = at(mirrored, e, row(r), c)
            send(("s", r, e), NS.at[:, features(e, r)], SR.at[from_here(e, r)], target)
            send(("q", r, e), QS, QR.at[from_here(e, r)], target)

        tasks.append(run)

    for e in range(4):
        for r in range(2):
            s_task(e, r)
            if (e, r) != (0, 0):
                x_task(e, r)

    def share(cols, r, d):
        ref = own(cols, r, d)
        send((cols is cols_a, r, d), ref, ref, sib)

    def halves(name):
        return (name, 0), (name, 1)

    @task
    def bx():
        recv(*halves("b_x"))
        send("bx_p", own(cols_b, 1, 0), own(cols_b, 1, 3), yp)
        send("bx_m", own(cols_b, 1, 0), own(cols_b, 1, 1), ym)
        share(cols_b, 1, 0)

    @task
    def ap():
        recv(*halves("a_p"))
        send("a_pp", own(cols_a, 0, 3, 0, ROWS), own(cols_a, 0, 2, 0, ROWS), yp)
        send("a_x3", own(cols_a, 0, 3), own(cols_a, 1, 3), pair)
        share(cols_a, 0, 3)

    @task
    def am():
        recv(*halves("a_m"))
        send("a_mm", own(cols_a, 0, 1, ROWS, ROWS), own(cols_a, 0, 2, ROWS, ROWS), ym)
        send("a_x1", own(cols_a, 0, 1), own(cols_a, 1, 1), pair)
        share(cols_a, 0, 1)

    @task
    def bp():
        recv(*halves("b_p"))
        send("b_pp", own(cols_b, 0, 3), own(cols_b, 0, 2), yp)
        share(cols_b, 0, 3)

    @task
    def bxm():
        recv("bx_m")
        send("bx_mm", own(cols_b, 1, 1), own(cols_b, 1, 2), ym)
        share(cols_b, 1, 1)

    @task
    def ax2():
        recv("a_pp", "a_mm")
        send("a_x2", own(cols_a, 0, 2), own(cols_a, 1, 2), pair)
        share(cols_a, 0, 2)

    def keep_task(wanted, cols, r, d):
        def run():
            recv(*wanted)
            share(cols, r, d)

        tasks.append(run)

    keep_task(halves("b_m"), cols_b, 0, 1)
    keep_task(("bx_p",), cols_b, 1, 3)
    keep_task(halves("a_x0"), cols_a, 1, 0)
    keep_task(("a_x3",), cols_a, 1, 3)
    keep_task(("a_x1",), cols_a, 1, 1)
    keep_task(("b_pp",), cols_b, 0, 2)
    keep_task(("bx_mm",), cols_b, 1, 2)
    keep_task(("a_x2",), cols_a, 1, 2)

    @task
    def hidden():
        load_g.wait()
        load_w.wait()
        recv("gain")
        both = GS[0:1, :]
        for d in (0, 3, 1, 2):
            for r in range(2):
                if (d, r) == (0, 0):
                    values = NX[:, features(0, 0)]
                else:
                    recv(("x", r, (4 - d) % 4))
                    values = XR[r * 4 + d]
                HN[r * 4 + d, own_rows, :] = (values.astype(F32) * both).astype(BF)
        send("hid", HN.at[:, own_rows, :], HN.at[:, own_rows, :], sib)

    def project(first, chips, start, width, store):
        def tile(i, carry):
            here = pl.multiple_of(i * 256, 256)
            there = pl.ds(pl.multiple_of(start + here, 256), 256)
            store(
                pl.ds(here, 256),
                there,
                jnp.dot(
                    HN[first : first + chips].reshape(chips * CHIP, PAIRED),
                    WC[:, there],
                    preferred_element_type=F32,
                ),
            )
            return carry

        lax.fori_loop(0, width // 256, tile, 0)

    @task
    def proj_a():
        load_wc.wait()
        load_xres.wait()
        recv("hid", "w_half", "x_half")

        def store(here, there, value):
            SA[0:CHIP, here] = (value[0:CHIP] + XRES[:, here].astype(F32)).astype(BF)
            SA[CHIP : 4 * CHIP, here] = value[CHIP : 4 * CHIP].astype(BF)

        project(0, 4, 0, CA, store)

    @task
    def proj_b():
        def store(here, there, value):
            PF[:, there] = value

        project(0, 8, CA, CB, store)

    @task
    def proj_c():
        def store(here, there, value):
            PF[4 * CHIP : 8 * CHIP, here] = value

        project(4, 4, 0, CA, store)

    def combine(dst, terms, width, first=0, rows=CHIP):
        def body(strip, i):
            total = None
            for ref, base, start in terms:
                here = pl.ds(pl.multiple_of(base + first + i * STRIP, STRIP), STRIP)
                value = ref[here, start : start + width].astype(F32)
                total = value if total is None else total + value
            ref, base, start = dst
            ref[pl.ds(pl.multiple_of(base + first + i * STRIP, STRIP), STRIP), start : start + width] = total.astype(BF)

        strips(rows, body)

    def deliver(src, start, width, offset):
        for core in range(2):
            grouped(
                src.at[core * ROWS : (core + 1) * ROWS, start : start + width],
                next_ref.at[:, columns(mine + offset + start, width)],
                N_OUT,
                N_IN,
                at(following, 0, 1 - xl, core),
            )

    def reduce_a(k):
        a, w = SUB_A[k]

        def pass_on(name, src, dst, first, rows, device):
            send(
                (name, k), src.at[first : first + rows, a : a + w], dst.at[first : first + rows, a : a + w], device
            )

        def cross(d):
            def run():
                pass_on(d, SA, RA, d * CHIP, CHIP, pair)

            tasks.append(run)

        for d in range(4):
            cross(d)

        def a2():
            recv((2, k))
            combine((SA2, 0, a), [(PF, block(1, 2), a), (RA, 2 * CHIP, a)], w)
            pass_on("ra2p", SA2, RA2, 0, ROWS, yp)
            pass_on("ra2m", SA2, RA2, ROWS, ROWS, ym)

        def a1():
            recv((1, k))
            combine((SAF, 0, a), [(PF, block(1, 1), a), (RA, CHIP, a)], w, ROWS, ROWS)
            pass_on("rafp1", SAF, RAF, ROWS, ROWS, yp)

        def a3():
            recv((3, k))
            combine((SAF, CHIP, a), [(PF, block(1, 3), a), (RA, 3 * CHIP, a)], w, 0, ROWS)
            pass_on("rafm0", SAF, RAF, CHIP, ROWS, ym)

        def a2p():
            recv(("ra2p", k))
            combine((SAF, 0, a), [(PF, block(1, 1), a), (RA, CHIP, a), (RA2, 0, a)], w, 0, ROWS)
            pass_on("rafp0", SAF, RAF, 0, ROWS, yp)

        def a2m():
            recv(("ra2m", k))
            combine((SAF, CHIP, a), [(PF, block(1, 3), a), (RA, 3 * CHIP, a), (RA2, 0, a)], w, ROWS, ROWS)
            pass_on("rafm1", SAF, RAF, CHIP + ROWS, ROWS, ym)

        def fin_a():
            for name in (0, "rafp0", "rafp1", "rafm0", "rafm1"):
                recv((name, k))
            combine((OA, 0, a), [(PF, block(1, 0), a), (RA, 0, a), (RAF, 0, a), (RAF, CHIP, a)], w)
            deliver(OA, a, w, 0)

        tasks.extend((a2, a1, a3, a2p, a2m, fin_a))

    def reduce_b(k):
        a, w = SUB_B[k]

        def hand(name, src, dst, first, device, terms):
            combine((src, first, a), terms, w)
            send(
                (name, k), src.at[first : first + CHIP, a : a + w], dst.at[first : first + CHIP, a : a + w], device
            )

        def rb2p():
            hand("rb2p", SB2, RB2, 0, yp, [(PF, block(0, 2), CA + a)])

        def rb2m():
            hand("rb2m", SB2, RB2, CHIP, ym, [(PF, block(1, 2), CA + a)])

        def rbf01():
            hand("rbf01", SBF, RBF, CHIP, yp, [(PF, block(1, 1), CA + a)])

        def rbf10():
            hand("rbf10", SBF, RBF, 2 * CHIP, ym, [(PF, block(0, 3), CA + a)])

        def rbf00():
            recv(("rb2p", k))
            hand("rbf00", SBF, RBF, 0, yp, [(PF, block(0, 1), CA + a), (RB2, 0, a)])

        def rbf11():
            recv(("rb2m", k))
            hand("rbf11", SBF, RBF, 3 * CHIP, ym, [(PF, block(1, 3), CA + a), (RB2, CHIP, a)])

        def rbx():
            recv(("rbf00", k), ("rbf10", k))
            hand(
                "rbx", SBX, RBX, 0, pair,
                [(PF, block(0, 0), CA + a), (RBF, 0, a), (RBF, 2 * CHIP, a), (XRES, 0, CA + a)],
            )

        def fin_b():
            recv(("rbf01", k), ("rbf11", k), ("rbx", k))
            combine((OB, 0, a), [(PF, block(1, 0), CA + a), (RBF, CHIP, a), (RBF, 3 * CHIP, a), (RBX, 0, a)], w)
            deliver(OB, a, w, CA)

        tasks.extend((rb2p, rb2m, rbf01, rbf10, rbf00, rbf11, rbx, fin_b))

    for k in range(len(SUB_A)):
        reduce_a(k)
    for k in range(len(SUB_B)):
        reduce_b(k)

    def dh_task(blocks, wanted):
        def run():
            recv(*wanted)
            first, second = (pl.ds(block(r, d), CHIP) for r, d in blocks)
            DH[first, :] = jnp.zeros((CHIP, WIDTH), F32)
            DH[second, :] = jnp.zeros((CHIP, WIDTH), F32)

            def step(j, carry):
                here = pl.ds(pl.multiple_of(j * 1024, 1024), 1024)
                part = lax.dot_general(
                    jnp.concatenate([G[first, here], G[second, here]], axis=0),
                    W[:, here],
                    (((1,), (1,)), ((), ())),
                    preferred_element_type=F32,
                )
                DH[first, :] += part[0:CHIP]
                DH[second, :] += part[CHIP : 2 * CHIP]
                return carry

            lax.fori_loop(0, D // 1024, step, 0)

        tasks.append(run)

    dh_task(((0, 0), (1, 0)), ("g_rest", (True, 1, 0), (False, 1, 0)))
    dh_task(((0, 1), (0, 3)), ((True, 0, 3), (True, 0, 1), (False, 0, 3), (False, 0, 1)))
    dh_task(((1, 1), (1, 3)), ((True, 1, 3), (True, 1, 1), (False, 1, 3), (False, 1, 1)))
    dh_task(((0, 2), (1, 2)), ((True, 0, 2), (True, 1, 2), (False, 0, 2), (False, 1, 2)))

    def local_copy(i, src, dst):
        copy = pltpu.make_async_copy(src, dst, local_sem.at[i])
        copy.start()
        return copy

    kept = {}

    @task
    def s_sib():
        for e in (1, 3, 2, 0):
            for r in range(2):
                recv(("s", r, e), ("q", r, e))
        send("s_sib", SR.at[:, :, columns((1 - c) * WIDTH, WIDTH)], SF.at[:, own_rows, :], sib)
        send("q_sib", QR, QF.at[:, c], sib)
        kept["s"] = local_copy(7, SR.at[:, :, columns(c * WIDTH, WIDTH)], SF.at[:, own_rows, :])
        kept["q"] = local_copy(8, QR, QF.at[:, c])

    def chip_of(b):
        return ((y + b % 4) % 4) * 2 + (xl + b // 4) % 2

    def add_sums(blocks):
        lane = lax.broadcasted_iota(jnp.int32, (CHIP, 128), 1)
        for b in blocks:
            grad = DH[b * CHIP : (b + 1) * CHIP, :]
            normed = SF[b].astype(F32)
            gg_ref[...] += jnp.sum(grad * normed, axis=0, keepdims=True)
            scaled = grad.astype(BF).astype(F32) * scale
            first = jnp.sum(scaled, axis=1, keepdims=True)
            second = jnp.sum(scaled * normed, axis=1, keepdims=True)
            place = 2 * chip_of(b)
            EC[0:CHIP, :] += jnp.where(lane == place, first, 0.0) + jnp.where(lane == place + 1, second, 0.0)

    @task
    def sums_a():
        recv("s_sib", "q_sib")
        kept["s"].wait()
        kept["q"].wait()
        EC[...] = jnp.zeros(EC.shape, F32)
        gg_ref[...] = jnp.zeros(gg_ref.shape, F32)
        add_sums((0, 4, 1, 3, 5, 7))

    @task
    def sums_b():
        add_sums((2, 6))
        ES[...] = EC[...].T[0:16, :]
        pltpu.make_async_copy(ES, ER.at[c], group_sem.at[E_IN]).start()
        for e in (2, 1, 3, 0):
            for r in range(2):
                grouped(ES, ER.at[from_here(e, r) * 2 + c], E_OUT, E_IN, at(s, e, row(r), 1 - c))
                if (e, r) != (0, 0):
                    grouped(ES, ER.at[from_here(e, r) * 2 + c], E_OUT, E_IN, at(s, e, row(r), c))

    @task
    def gi():
        arrived(ER, group_sem.at[E_IN], group_sem.at[E_OUT])
        total = ER[0]
        for k in range(1, 16):
            total = total + ER[k]
        QC[0:16, :] = total * (1.0 / D)
        EC[...] = jnp.zeros(EC.shape, F32)
        for b in range(8):
            EC[2 * b : 2 * b + 2, :] = QC[pl.ds(2 * chip_of(b), 2), :]
        MT[...] = EC[...].T
        QC[...] = jnp.zeros(QC.shape, F32)
        for b in range(8):
            for core in range(2):
                QC[b * 2 + core : b * 2 + core + 1, :] = QF[b, core, 0:1, :]
        RT[...] = QC[...].T

    def p_task(e, r):
        def run():
            b = r * 4 + e
            for core in range(2):
                k = b * 2 + core
                part = slice(core * ROWS, (core + 1) * ROWS)
                rows = slice(k * ROWS, (k + 1) * ROWS)
                mean_e = MT[part, 2 * b : 2 * b + 1]
                mean_en = MT[part, 2 * b + 1 : 2 * b + 2]
                recip = RT[0:ROWS, k : k + 1]
                scaled = DH[rows, :].astype(BF).astype(F32) * scale
                inner = scaled - mean_e - SF[b, part, :].astype(F32) * mean_en
                upstream = G[rows, columns(t * WIDTH, WIDTH)].astype(F32)
                GI[b, part, :] = (upstream + recip * inner).astype(BF)
                grouped(
                    GI.at[b, part, :],
                    prev_ref.at[:, columns(t * WIDTH, WIDTH)],
                    P_OUT,
                    P_IN,
                    at(previous, e, row(r), core),
                )

        tasks.append(run)

    for e in range(4):
        for r in range(2):
            p_task(e, r)

    @task
    def bht():
        BHT[...] = (SF[...].reshape(TOKENS, WIDTH).astype(F32) * scale).T.astype(BF)

    def wg_task(i):
        def run():
            def step(j, carry):
                here = pl.ds(pl.multiple_of(j * 256, 256), 256)
                W[:, here] = jnp.dot(BHT[...], G[:, here], preferred_element_type=F32).astype(BF)
                pltpu.make_async_copy(W.at[:, here], wg_ref.at[:, here], local_sem.at[6]).start()
                return carry

            lax.fori_loop(i * 6, (i + 1) * 6, step, 0)

        tasks.append(run)

    for i in range(4):
        wg_task(i)

    for i in ORDER:
        tasks[i]()

    pltpu.make_async_copy(W, wg_ref, local_sem.at[6]).wait()
    for copy in sent:
        copy.wait_send()
    left(ER.at[0:15], group_sem.at[E_OUT], group_sem.at[E_IN])
    left(next_ref, group_sem.at[N_OUT], group_sem.at[N_IN])
    left(prev_ref, group_sem.at[P_OUT], group_sem.at[P_IN])
    arrived(prev_ref, group_sem.at[P_IN], group_sem.at[P_OUT])
    arrived(next_ref, group_sem.at[N_IN], group_sem.at[N_OUT])


PARTS = 2


def hand_over(next_in, prev_in, wg_in, gg_in, next_out, prev_out, wg_out, gg_out, near_next, near_prev, near_wg, sems):
    gg_out[...] = gg_in[...]
    rows = WIDTH // PARTS
    moves = [(wg_in.at[i], near_wg.at[i], wg_out.at[i]) for i in (pl.ds(k * rows, rows) for k in range(PARTS))]
    moves += [(next_in, near_next, next_out), (prev_in, near_prev, prev_out)]
    inward = [pltpu.make_async_copy(src, via, sems.at[0, i]) for i, (src, via, dst) in enumerate(moves)]
    outward = [pltpu.make_async_copy(via, dst, sems.at[1, i]) for i, (src, via, dst) in enumerate(moves)]
    for copy in inward:
        copy.start()
    for before, after in zip(inward, outward):
        before.wait()
        after.start()
    for copy in outward:
        copy.wait()


def local(forward_in, grad_out, saved_in, weight, gain):
    anywhere = pl.BlockSpec(memory_space=pl.ANY)
    vmem = pl.BlockSpec(memory_space=pltpu.VMEM)
    v = pltpu.VMEM
    out_shape = (
        jax.ShapeDtypeStruct((ROWS, D), BF),
        jax.ShapeDtypeStruct((ROWS, D), BF),
        jax.ShapeDtypeStruct((WIDTH, D), BF),
        jax.ShapeDtypeStruct((1, WIDTH), F32),
    )
    raw = pl.pallas_call(
        kernel,
        out_shape=out_shape,
        in_specs=[anywhere, anywhere, anywhere, anywhere, vmem],
        out_specs=(anywhere, anywhere, anywhere, vmem),
        scratch_shapes=[
            v((TOKENS, D), BF),
            v((WIDTH, D), BF),
            v((PAIRED, HALF), BF),
            v((TOKENS, HALF), F32),
            v((8, CHIP, PAIRED), BF),
            v((8, ROWS, PAIRED), BF),
            v((ROWS, D), BF),
            v((ROWS, D), BF),
            v((ROWS, D), BF),
            v((ROWS, D), BF),
            v((8, ROWS, PAIRED), BF),
            v((8, CHIP, WIDTH), BF),
            v((WIDTH, TOKENS), BF),
            v((TOKENS, WIDTH), F32),
            v((8, CHIP, WIDTH), BF),
            v((CHIP, HALF), BF),
            v((8, PAIRED), F32),
            v((4 * CHIP, CA), BF),
            v((4 * CHIP, CA), BF),
            v((CHIP, CA), BF),
            v((CHIP, CA), BF),
            v((2 * CHIP, CA), BF),
            v((2 * CHIP, CA), BF),
            v((2 * CHIP, CB), BF),
            v((2 * CHIP, CB), BF),
            v((4 * CHIP, CB), BF),
            v((4 * CHIP, CB), BF),
            v((CHIP, CB), BF),
            v((CHIP, CB), BF),
            v((CHIP, CA), BF),
            v((CHIP, CB), BF),
            v((128, 128), F32),
            v((8, 128), F32),
            v((8, 8, 128), F32),
            v((8, 2, 8, 128), F32),
            v((128, 128), F32),
            v((16, 128), F32),
            v((16, 16, 128), F32),
            v((128, 128), F32),
            v((128, 128), F32),
            pltpu.SemaphoreType.DMA((128,)),
            pltpu.SemaphoreType.DMA((128,)),
            pltpu.SemaphoreType.DMA((9,)),
            pltpu.SemaphoreType.DMA((6,)),
            pltpu.SemaphoreType.REGULAR((ROUNDS,)),
        ],
        compiler_params=pltpu.CompilerParams(
            collective_id=0, has_side_effects=True, vmem_limit_bytes=60 * 2**20
        ),
        cost_estimate=pl.CostEstimate(
            flops=6 * TOKENS * WIDTH * D, bytes_accessed=20 * 2**20, transcendentals=0
        ),
    )(forward_in[0], grad_out[0], saved_in[0], weight[0], gain)
    next_input, prev_grad, weight_grad, gain_grad = pl.pallas_call(
        hand_over,
        out_shape=out_shape,
        in_specs=[pl.BlockSpec(memory_space=pltpu.HBM)] * 3 + [vmem],
        out_specs=(anywhere, anywhere, anywhere, vmem),
        scratch_shapes=[
            v((ROWS, D), BF),
            v((ROWS, D), BF),
            v((WIDTH, D), BF),
            pltpu.SemaphoreType.DMA((2, PARTS + 2)),
        ],
        cost_estimate=pl.CostEstimate(flops=0, bytes_accessed=12 * 2**20, transcendentals=0),
    )(*raw)
    return next_input[None], prev_grad[None], weight_grad[None], gain_grad


def solution(mesh):
    rows = P("section", "tensor", None)
    return jax.shard_map(
        local,
        mesh=mesh,
        in_specs=(rows, rows, rows, rows, P("section", "tensor")),
        out_specs=(rows, rows, rows, P("section", "tensor")),
        check_vma=False,
    )
```

```python
import jax
import jax.numpy as jnp
from jax import lax
from jax.experimental import pallas as pl
from jax.experimental.pallas import tpu as pltpu
from jax.sharding import PartitionSpec as P

D = 6144
TOKENS = 768
ROWS = 48
CHIP = 96
WIDTH = 384
PAIRED = 2 * WIDTH
HALF = D // 2
GA = 1408
GB = HALF - GA
CA = 1280
CB = HALF - CA
SUB_A = ((0, 512), (512, 512), (1024, 256))
SUB_B = ((0, 768), (768, 512), (1280, 512))
ORDER = (
    6, 0, 9, 23, 1, 7, 8, 2, 19, 21,
    17, 3, 25, 10, 15, 4, 18, 26, 20, 13,
    27, 22, 34, 11, 28, 40, 29, 41, 30, 42,
    82, 75, 66, 5, 32, 12, 14, 35, 43, 31,
    99, 33, 36, 57, 24, 74, 85, 56, 98, 83,
    16, 38, 55, 65, 86, 77, 39, 100, 78, 37,
    84, 46, 102, 76, 88, 87, 79, 101, 80, 103,
    104, 90, 60, 54, 89, 114, 58, 81, 67, 59,
    93, 91, 47, 105, 107, 69, 62, 94, 106, 113,
    68, 45, 61, 109, 48, 108, 95, 92, 112, 96,
    70, 72, 63, 44, 111, 110, 117, 49, 51, 50,
    71, 116, 52, 64, 115, 97, 73, 53, 118,
)
STRIP = 16
ROUNDS = 5
BF = jnp.bfloat16
F32 = jnp.float32
EPS = 1e-05
MESH = pl.DeviceIdType.MESH


def block(r, d):
    return (r * 4 + d) * CHIP


def normalize(values):
    center = jnp.mean(values, axis=1, keepdims=True)
    shifted = values - center
    recip = lax.rsqrt(jnp.mean(shifted * shifted, axis=1, keepdims=True) + EPS)
    return shifted * recip, recip


def strips(rows, body):
    def step(i, carry):
        body(pl.ds(pl.multiple_of(i * STRIP, STRIP), STRIP), i)
        return carry

    lax.fori_loop(0, rows // STRIP, step, 0)


def columns(start, width):
    return pl.ds(pl.multiple_of(start, 128), width)


def kernel(
    x_ref, g_ref, s_ref, w_ref, gain_ref,
    next_ref, prev_ref, wg_ref, gg_ref,
    G, W, WC, PF, HN, XR, XO, NX, SO, NS, SR, SF, BHT, DH, GI, XRES, GS,
    SA, RA, SA2, RA2, SAF, RAF, SB2, RB2, SBF, RBF, SBX, RBX, OA, OB,
    QC, QS, QR, QF, EC, ES, ER, MT, RT,
    send_sem, recv_sem, local_sem, group_sem, heard,
):
    s = lax.axis_index("section")
    t = lax.axis_index("tensor")
    y, xl, c = t // 4, (t // 2) % 2, t % 2
    mirrored, following, previous = 7 - s, (s + 1) % 8, (s + 7) % 8

    def at(section, along_y, row, core):
        return (section, ((y + along_y) % 4) * 4 + row * 2 + core)

    def row(r):
        return xl if r == 0 else 1 - xl

    sib = at(s, 0, xl, 1 - c)
    yp, ym = at(s, 1, xl, c), at(s, 3, xl, c)
    pair = at(s, 0, 1 - xl, c)

    mine = c * HALF
    other = (1 - c) * HALF
    cols_a = columns(mine, GA)
    cols_b = columns(mine + GA, GB)
    own_rows = pl.ds(pl.multiple_of(c * ROWS, 16), ROWS)
    sib_rows = pl.ds(pl.multiple_of((1 - c) * ROWS, 16), ROWS)

    names = {}
    sent = []

    def send(name, src, dst, device):
        i = names.setdefault(name, (len(names), dst))[0]
        copy = pltpu.make_async_remote_copy(
            src_ref=src, dst_ref=dst, send_sem=send_sem.at[i], recv_sem=recv_sem.at[i],
            device_id=device, device_id_type=MESH,
        )
        copy.start()
        sent.append(copy)

    def arrived(ref, sem, scratch_sem):
        pltpu.make_async_remote_copy(
            src_ref=ref, dst_ref=ref, send_sem=scratch_sem, recv_sem=sem, device_id=sib, device_id_type=MESH
        ).wait_recv()

    def left(ref, sem, scratch_sem):
        pltpu.make_async_remote_copy(
            src_ref=ref, dst_ref=ref, send_sem=sem, recv_sem=scratch_sem, device_id=sib, device_id_type=MESH
        ).wait_send()

    def recv(*wanted):
        for name in wanted:
            i, landing = names[name]
            arrived(landing, recv_sem.at[i], send_sem.at[i])

    E_IN, E_OUT, P_IN, P_OUT, N_IN, N_OUT = range(6)

    def grouped(src, dst, out, into, device):
        pltpu.make_async_remote_copy(
            src_ref=src, dst_ref=dst, send_sem=group_sem.at[out], recv_sem=group_sem.at[into],
            device_id=device, device_id_type=MESH,
        ).start()

    barrier = pltpu.get_barrier_semaphore()
    across = at(s + 1 - 2 * (s % 2), 0, 1 - xl, c)
    nearest = [sib, yp, ym, pair, across, at((s + 2) % 8, 0, xl, c), at((s + 6) % 8, 0, xl, c)]
    for friend in nearest:
        pl.semaphore_signal(barrier, inc=1, device_id=friend, device_id_type=MESH)

    load_x = pltpu.make_async_copy(x_ref, XO, local_sem.at[0])
    load_g = pltpu.make_async_copy(g_ref, G.at[own_rows, :], local_sem.at[1])
    load_s = pltpu.make_async_copy(s_ref, SO, local_sem.at[2])
    load_w = pltpu.make_async_copy(w_ref, W, local_sem.at[3])
    weight_rows = pl.ds(pl.multiple_of(c * WIDTH, 128), WIDTH)
    load_wc = pltpu.make_async_copy(w_ref.at[:, columns(mine, HALF)], WC.at[weight_rows, :], local_sem.at[4])
    load_xres = pltpu.make_async_copy(x_ref.at[:, columns(mine, HALF)], XRES.at[own_rows, :], local_sem.at[5])
    for load in (load_x, load_g, load_s, load_wc, load_xres, load_w):
        load.start()
    scale = gain_ref[...].astype(F32)
    GS[:, columns(c * WIDTH, WIDTH)] = jnp.broadcast_to(scale, (8, WIDTH))

    pl.semaphore_wait(barrier, len(nearest))

    def own(cols, r=0, d=0, first=0, rows=CHIP):
        return G.at[block(r, d) + first : block(r, d) + first + rows, cols]

    def near(cols, rows, r, d):
        return G.at[pl.ds(pl.multiple_of(block(r, d) + rows.start, 16), ROWS), cols]

    def from_here(e, r):
        return r * 4 + (4 - e) % 4

    tasks = []

    def task(run):
        tasks.append(run)
        return run

    def round_task(i):
        def run():
            if i > 1:
                pl.semaphore_wait(heard.at[i - 2], len(nearest))
            if i <= ROUNDS:
                for friend in nearest:
                    pl.semaphore_signal(heard.at[i - 1], inc=1, device_id=friend, device_id_type=MESH)

        tasks.append(run)

    for i in range(1, ROUNDS + 2):
        round_task(i)

    def first_step(part, a, b):
        send(("b_x", part), b[0], near(cols_b, b[1], 1, 0), pair)
        send(("a_p", part), a[0], near(cols_a, a[1], 0, 3), yp)
        send(("a_m", part), a[0], near(cols_a, a[1], 0, 1), ym)
        send(("b_p", part), b[0], near(cols_b, b[1], 0, 3), yp)
        send(("b_m", part), b[0], near(cols_b, b[1], 0, 1), ym)
        send(("a_x0", part), a[0], near(cols_a, a[1], 1, 0), pair)

    @task
    def first_o():
        send("g_half", g_ref.at[:, columns(other, HALF)], G.at[own_rows, columns(other, HALF)], sib)
        first_step(0, (g_ref.at[:, cols_a], own_rows), (g_ref.at[:, cols_b], own_rows))

    @task
    def first_s():
        recv("g_half")
        first_step(1, (G.at[sib_rows, cols_a], sib_rows), (G.at[sib_rows, cols_b], sib_rows))

    @task
    def inchip():
        send("gain", GS.at[:, columns(c * WIDTH, WIDTH)], GS.at[:, columns(c * WIDTH, WIDTH)], sib)
        send("w_half", w_ref.at[:, columns(other, HALF)], WC.at[weight_rows, :], sib)
        send("x_half", x_ref.at[:, columns(other, HALF)], XRES.at[own_rows, :], sib)
        send("g_rest", g_ref.at[:, columns(mine, HALF)], G.at[own_rows, columns(mine, HALF)], sib)

    @task
    def norm_x():
        load_x.wait()

        def body(rows, i):
            NX[rows, :] = normalize(XO[rows, :].astype(F32))[0].astype(BF)

        strips(ROWS, body)

    def features(e, r):
        return columns((((y + e) % 4) * 2 + row(r)) * PAIRED, PAIRED)

    def x_task(e, r):
        def run():
            send(("x", r, e), NX.at[:, features(e, r)], XR.at[from_here(e, r)], at(s, e, row(r), c))

        tasks.append(run)

    @task
    def norm_s():
        load_s.wait()
        QC[...] = jnp.zeros(QC.shape, F32)

        def body(rows, i):
            normed, recip = normalize(SO[rows, :].astype(F32))
            NS[rows, :] = normed.astype(BF)
            QC[rows, :] = jnp.broadcast_to(recip, (STRIP, 128))

        strips(ROWS, body)
        QS[...] = QC[...].T[0:8, :]

    def s_task(e, r):
        def run():
            target = at(mirrored, e, row(r), c)
            send(("s", r, e), NS.at[:, features(e, r)], SR.at[from_here(e, r)], target)
            send(("q", r, e), QS, QR.at[from_here(e, r)], target)

        tasks.append(run)

    for e in range(4):
        for r in range(2):
            s_task(e, r)
            if (e, r) != (0, 0):
                x_task(e, r)

    def share(cols, r, d):
        ref = own(cols, r, d)
        send((cols is cols_a, r, d), ref, ref, sib)

    def halves(name):
        return (name, 0), (name, 1)

    @task
    def bx():
        recv(*halves("b_x"))
        send("bx_p", own(cols_b, 1, 0), own(cols_b, 1, 3), yp)
        send("bx_m", own(cols_b, 1, 0), own(cols_b, 1, 1), ym)
        share(cols_b, 1, 0)

    @task
    def ap():
        recv(*halves("a_p"))
        send("a_pp", own(cols_a, 0, 3, 0, ROWS), own(cols_a, 0, 2, 0, ROWS), yp)
        send("a_x3", own(cols_a, 0, 3), own(cols_a, 1, 3), pair)
        share(cols_a, 0, 3)

    @task
    def am():
        recv(*halves("a_m"))
        send("a_mm", own(cols_a, 0, 1, ROWS, ROWS), own(cols_a, 0, 2, ROWS, ROWS), ym)
        send("a_x1", own(cols_a, 0, 1), own(cols_a, 1, 1), pair)
        share(cols_a, 0, 1)

    @task
    def bp():
        recv(*halves("b_p"))
        send("b_pp", own(cols_b, 0, 3), own(cols_b, 0, 2), yp)
        share(cols_b, 0, 3)

    @task
    def bxm():
        recv("bx_m")
        send("bx_mm", own(cols_b, 1, 1), own(cols_b, 1, 2), ym)
        share(cols_b, 1, 1)

    @task
    def ax2():
        recv("a_pp", "a_mm")
        send("a_x2", own(cols_a, 0, 2), own(cols_a, 1, 2), pair)
        share(cols_a, 0, 2)

    def keep_task(wanted, cols, r, d):
        def run():
            recv(*wanted)
            share(cols, r, d)

        tasks.append(run)

    keep_task(halves("b_m"), cols_b, 0, 1)
    keep_task(("bx_p",), cols_b, 1, 3)
    keep_task(halves("a_x0"), cols_a, 1, 0)
    keep_task(("a_x3",), cols_a, 1, 3)
    keep_task(("a_x1",), cols_a, 1, 1)
    keep_task(("b_pp",), cols_b, 0, 2)
    keep_task(("bx_mm",), cols_b, 1, 2)
    keep_task(("a_x2",), cols_a, 1, 2)

    @task
    def hidden():
        load_g.wait()
        load_w.wait()
        recv("gain")
        both = GS[0:1, :]
        for d in (0, 3, 1, 2):
            for r in range(2):
                if (d, r) == (0, 0):
                    values = NX[:, features(0, 0)]
                else:
                    recv(("x", r, (4 - d) % 4))
                    values = XR[r * 4 + d]
                HN[r * 4 + d, own_rows, :] = (values.astype(F32) * both).astype(BF)
        send("hid", HN.at[:, own_rows, :], HN.at[:, own_rows, :], sib)

    def project(first, chips, start, width, store):
        def tile(i, carry):
            here = pl.multiple_of(i * 256, 256)
            there = pl.ds(pl.multiple_of(start + here, 256), 256)
            store(
                pl.ds(here, 256),
                there,
                jnp.dot(
                    HN[first : first + chips].reshape(chips * CHIP, PAIRED),
                    WC[:, there],
                    preferred_element_type=F32,
                ),
            )
            return carry

        lax.fori_loop(0, width // 256, tile, 0)

    @task
    def proj_a():
        load_wc.wait()
        load_xres.wait()
        recv("hid", "w_half", "x_half")

        def store(here, there, value):
            SA[0:CHIP, here] = (value[0:CHIP] + XRES[:, here].astype(F32)).astype(BF)
            SA[CHIP : 4 * CHIP, here] = value[CHIP : 4 * CHIP].astype(BF)

        project(0, 4, 0, CA, store)

    @task
    def proj_b():
        def store(here, there, value):
            PF[:, there] = value

        project(0, 8, CA, CB, store)

    @task
    def proj_c():
        def store(here, there, value):
            PF[4 * CHIP : 8 * CHIP, here] = value

        project(4, 4, 0, CA, store)

    def combine(dst, terms, width, first=0, rows=CHIP):
        def body(strip, i):
            total = None
            for ref, base, start in terms:
                here = pl.ds(pl.multiple_of(base + first + i * STRIP, STRIP), STRIP)
                value = ref[here, start : start + width].astype(F32)
                total = value if total is None else total + value
            ref, base, start = dst
            ref[pl.ds(pl.multiple_of(base + first + i * STRIP, STRIP), STRIP), start : start + width] = total.astype(BF)

        strips(rows, body)

    def deliver(src, start, width, offset):
        for core in range(2):
            grouped(
                src.at[core * ROWS : (core + 1) * ROWS, start : start + width],
                next_ref.at[:, columns(mine + offset + start, width)],
                N_OUT,
                N_IN,
                at(following, 0, 1 - xl, core),
            )

    def reduce_a(k):
        a, w = SUB_A[k]

        def pass_on(name, src, dst, first, rows, device):
            send(
                (name, k), src.at[first : first + rows, a : a + w], dst.at[first : first + rows, a : a + w], device
            )

        def cross(d):
            def run():
                pass_on(d, SA, RA, d * CHIP, CHIP, pair)

            tasks.append(run)

        for d in range(4):
            cross(d)

        def a2():
            recv((2, k))
            combine((SA2, 0, a), [(PF, block(1, 2), a), (RA, 2 * CHIP, a)], w)
            pass_on("ra2p", SA2, RA2, 0, ROWS, yp)
            pass_on("ra2m", SA2, RA2, ROWS, ROWS, ym)

        def a1():
            recv((1, k))
            combine((SAF, 0, a), [(PF, block(1, 1), a), (RA, CHIP, a)], w, ROWS, ROWS)
            pass_on("rafp1", SAF, RAF, ROWS, ROWS, yp)

        def a3():
            recv((3, k))
            combine((SAF, CHIP, a), [(PF, block(1, 3), a), (RA, 3 * CHIP, a)], w, 0, ROWS)
            pass_on("rafm0", SAF, RAF, CHIP, ROWS, ym)

        def a2p():
            recv(("ra2p", k))
            combine((SAF, 0, a), [(PF, block(1, 1), a), (RA, CHIP, a), (RA2, 0, a)], w, 0, ROWS)
            pass_on("rafp0", SAF, RAF, 0, ROWS, yp)

        def a2m():
            recv(("ra2m", k))
            combine((SAF, CHIP, a), [(PF, block(1, 3), a), (RA, 3 * CHIP, a), (RA2, 0, a)], w, ROWS, ROWS)
            pass_on("rafm1", SAF, RAF, CHIP + ROWS, ROWS, ym)

        def fin_a():
            for name in (0, "rafp0", "rafp1", "rafm0", "rafm1"):
                recv((name, k))
            combine((OA, 0, a), [(PF, block(1, 0), a), (RA, 0, a), (RAF, 0, a), (RAF, CHIP, a)], w)
            deliver(OA, a, w, 0)

        tasks.extend((a2, a1, a3, a2p, a2m, fin_a))

    def reduce_b(k):
        a, w = SUB_B[k]

        def hand(name, src, dst, first, device, terms):
            combine((src, first, a), terms, w)
            send(
                (name, k), src.at[first : first + CHIP, a : a + w], dst.at[first : first + CHIP, a : a + w], device
            )

        def rb2p():
            hand("rb2p", SB2, RB2, 0, yp, [(PF, block(0, 2), CA + a)])

        def rb2m():
            hand("rb2m", SB2, RB2, CHIP, ym, [(PF, block(1, 2), CA + a)])

        def rbf01():
            hand("rbf01", SBF, RBF, CHIP, yp, [(PF, block(1, 1), CA + a)])

        def rbf10():
            hand("rbf10", SBF, RBF, 2 * CHIP, ym, [(PF, block(0, 3), CA + a)])

        def rbf00():
            recv(("rb2p", k))
            hand("rbf00", SBF, RBF, 0, yp, [(PF, block(0, 1), CA + a), (RB2, 0, a)])

        def rbf11():
            recv(("rb2m", k))
            hand("rbf11", SBF, RBF, 3 * CHIP, ym, [(PF, block(1, 3), CA + a), (RB2, CHIP, a)])

        def rbx():
            recv(("rbf00", k), ("rbf10", k))
            hand(
                "rbx", SBX, RBX, 0, pair,
                [(PF, block(0, 0), CA + a), (RBF, 0, a), (RBF, 2 * CHIP, a), (XRES, 0, CA + a)],
            )

        def fin_b():
            recv(("rbf01", k), ("rbf11", k), ("rbx", k))
            combine((OB, 0, a), [(PF, block(1, 0), CA + a), (RBF, CHIP, a), (RBF, 3 * CHIP, a), (RBX, 0, a)], w)
            deliver(OB, a, w, CA)

        tasks.extend((rb2p, rb2m, rbf01, rbf10, rbf00, rbf11, rbx, fin_b))

    for k in range(len(SUB_A)):
        reduce_a(k)
    for k in range(len(SUB_B)):
        reduce_b(k)

    def dh_task(blocks, wanted):
        def run():
            recv(*wanted)
            first, second = (pl.ds(block(r, d), CHIP) for r, d in blocks)
            DH[first, :] = jnp.zeros((CHIP, WIDTH), F32)
            DH[second, :] = jnp.zeros((CHIP, WIDTH), F32)

            def step(j, carry):
                here = pl.ds(pl.multiple_of(j * 1024, 1024), 1024)
                part = lax.dot_general(
                    jnp.concatenate([G[first, here], G[second, here]], axis=0),
                    W[:, here],
                    (((1,), (1,)), ((), ())),
                    preferred_element_type=F32,
                )
                DH[first, :] += part[0:CHIP]
                DH[second, :] += part[CHIP : 2 * CHIP]
                return carry

            lax.fori_loop(0, D // 1024, step, 0)

        tasks.append(run)

    dh_task(((0, 0), (1, 0)), ("g_rest", (True, 1, 0), (False, 1, 0)))
    dh_task(((0, 1), (0, 3)), ((True, 0, 3), (True, 0, 1), (False, 0, 3), (False, 0, 1)))
    dh_task(((1, 1), (1, 3)), ((True, 1, 3), (True, 1, 1), (False, 1, 3), (False, 1, 1)))
    dh_task(((0, 2), (1, 2)), ((True, 0, 2), (True, 1, 2), (False, 0, 2), (False, 1, 2)))

    def local_copy(i, src, dst):
        copy = pltpu.make_async_copy(src, dst, local_sem.at[i])
        copy.start()
        return copy

    kept = {}

    @task
    def s_sib():
        for e in (1, 3, 2, 0):
            for r in range(2):
                recv(("s", r, e), ("q", r, e))
        send("s_sib", SR.at[:, :, columns((1 - c) * WIDTH, WIDTH)], SF.at[:, own_rows, :], sib)
        send("q_sib", QR, QF.at[:, c], sib)
        kept["s"] = local_copy(7, SR.at[:, :, columns(c * WIDTH, WIDTH)], SF.at[:, own_rows, :])
        kept["q"] = local_copy(8, QR, QF.at[:, c])

    def chip_of(b):
        return ((y + b % 4) % 4) * 2 + (xl + b // 4) % 2

    def add_sums(blocks):
        lane = lax.broadcasted_iota(jnp.int32, (CHIP, 128), 1)
        for b in blocks:
            grad = DH[b * CHIP : (b + 1) * CHIP, :]
            normed = SF[b].astype(F32)
            gg_ref[...] += jnp.sum(grad * normed, axis=0, keepdims=True)
            scaled = grad.astype(BF).astype(F32) * scale
            first = jnp.sum(scaled, axis=1, keepdims=True)
            second = jnp.sum(scaled * normed, axis=1, keepdims=True)
            place = 2 * chip_of(b)
            EC[0:CHIP, :] += jnp.where(lane == place, first, 0.0) + jnp.where(lane == place + 1, second, 0.0)

    @task
    def sums_a():
        recv("s_sib", "q_sib")
        kept["s"].wait()
        kept["q"].wait()
        EC[...] = jnp.zeros(EC.shape, F32)
        gg_ref[...] = jnp.zeros(gg_ref.shape, F32)
        add_sums((0, 4, 1, 3, 5, 7))

    @task
    def sums_b():
        add_sums((2, 6))
        ES[...] = EC[...].T[0:16, :]
        pltpu.make_async_copy(ES, ER.at[c], group_sem.at[E_IN]).start()
        for e in (2, 1, 3, 0):
            for r in range(2):
                grouped(ES, ER.at[from_here(e, r) * 2 + c], E_OUT, E_IN, at(s, e, row(r), 1 - c))
                if (e, r) != (0, 0):
                    grouped(ES, ER.at[from_here(e, r) * 2 + c], E_OUT, E_IN, at(s, e, row(r), c))

    @task
    def gi():
        arrived(ER, group_sem.at[E_IN], group_sem.at[E_OUT])
        total = ER[0]
        for k in range(1, 16):
            total = total + ER[k]
        QC[0:16, :] = total * (1.0 / D)
        EC[...] = jnp.zeros(EC.shape, F32)
        for b in range(8):
            EC[2 * b : 2 * b + 2, :] = QC[pl.ds(2 * chip_of(b), 2), :]
        MT[...] = EC[...].T
        QC[...] = jnp.zeros(QC.shape, F32)
        for b in range(8):
            for core in range(2):
                QC[b * 2 + core : b * 2 + core + 1, :] = QF[b, core, 0:1, :]
        RT[...] = QC[...].T

    def p_task(e, r):
        def run():
            b = r * 4 + e
            for core in range(2):
                k = b * 2 + core
                part = slice(core * ROWS, (core + 1) * ROWS)
                rows = slice(k * ROWS, (k + 1) * ROWS)
                mean_e = MT[part, 2 * b : 2 * b + 1]
                mean_en = MT[part, 2 * b + 1 : 2 * b + 2]
                recip = RT[0:ROWS, k : k + 1]
                scaled = DH[rows, :].astype(BF).astype(F32) * scale
                inner = scaled - mean_e - SF[b, part, :].astype(F32) * mean_en
                upstream = G[rows, columns(t * WIDTH, WIDTH)].astype(F32)
                GI[b, part, :] = (upstream + recip * inner).astype(BF)
                grouped(
                    GI.at[b, part, :],
                    prev_ref.at[:, columns(t * WIDTH, WIDTH)],
                    P_OUT,
                    P_IN,
                    at(previous, e, row(r), core),
                )

        tasks.append(run)

    for e in range(4):
        for r in range(2):
            p_task(e, r)

    @task
    def bht():
        BHT[...] = (SF[...].reshape(TOKENS, WIDTH).astype(F32) * scale).T.astype(BF)

    def wg_task(i):
        def run():
            def step(j, carry):
                here = pl.ds(pl.multiple_of(j * 256, 256), 256)
                wg_ref[:, here] = jnp.dot(BHT[...], G[:, here], preferred_element_type=F32).astype(BF)
                return carry

            lax.fori_loop(i * 6, (i + 1) * 6, step, 0)

        tasks.append(run)

    for i in range(4):
        wg_task(i)

    for i in ORDER:
        tasks[i]()

    for copy in sent:
        copy.wait_send()
    left(ER.at[0:15], group_sem.at[E_OUT], group_sem.at[E_IN])
    left(next_ref, group_sem.at[N_OUT], group_sem.at[N_IN])
    left(prev_ref, group_sem.at[P_OUT], group_sem.at[P_IN])
    arrived(prev_ref, group_sem.at[P_IN], group_sem.at[P_OUT])
    arrived(next_ref, group_sem.at[N_IN], group_sem.at[N_OUT])


def local(forward_in, grad_out, saved_in, weight, gain):
    anywhere = pl.BlockSpec(memory_space=pl.ANY)
    vmem = pl.BlockSpec(memory_space=pltpu.VMEM)
    v = pltpu.VMEM
    out_shape = (
        jax.ShapeDtypeStruct((ROWS, D), BF),
        jax.ShapeDtypeStruct((ROWS, D), BF),
        jax.ShapeDtypeStruct((WIDTH, D), BF),
        jax.ShapeDtypeStruct((1, WIDTH), F32),
    )
    next_input, prev_grad, weight_grad, gain_grad = pl.pallas_call(
        kernel,
        out_shape=tuple(v(out.shape, out.dtype) for out in out_shape),
        in_specs=[anywhere, anywhere, anywhere, anywhere, vmem],
        out_specs=(vmem,) * 4,
        scratch_shapes=[
            v((TOKENS, D), BF),
            v((WIDTH, D), BF),
            v((PAIRED, HALF), BF),
            v((TOKENS, HALF), F32),
            v((8, CHIP, PAIRED), BF),
            v((8, ROWS, PAIRED), BF),
            v((ROWS, D), BF),
            v((ROWS, D), BF),
            v((ROWS, D), BF),
            v((ROWS, D), BF),
            v((8, ROWS, PAIRED), BF),
            v((8, CHIP, WIDTH), BF),
            v((WIDTH, TOKENS), BF),
            v((TOKENS, WIDTH), F32),
            v((8, CHIP, WIDTH), BF),
            v((CHIP, HALF), BF),
            v((8, PAIRED), F32),
            v((4 * CHIP, CA), BF),
            v((4 * CHIP, CA), BF),
            v((CHIP, CA), BF),
            v((CHIP, CA), BF),
            v((2 * CHIP, CA), BF),
            v((2 * CHIP, CA), BF),
            v((2 * CHIP, CB), BF),
            v((2 * CHIP, CB), BF),
            v((4 * CHIP, CB), BF),
            v((4 * CHIP, CB), BF),
            v((CHIP, CB), BF),
            v((CHIP, CB), BF),
            v((CHIP, CA), BF),
            v((CHIP, CB), BF),
            v((128, 128), F32),
            v((8, 128), F32),
            v((8, 8, 128), F32),
            v((8, 2, 8, 128), F32),
            v((128, 128), F32),
            v((16, 128), F32),
            v((16, 16, 128), F32),
            v((128, 128), F32),
            v((128, 128), F32),
            pltpu.SemaphoreType.DMA((128,)),
            pltpu.SemaphoreType.DMA((128,)),
            pltpu.SemaphoreType.DMA((9,)),
            pltpu.SemaphoreType.DMA((6,)),
            pltpu.SemaphoreType.REGULAR((ROUNDS,)),
        ],
        compiler_params=pltpu.CompilerParams(
            collective_id=0, has_side_effects=True, vmem_limit_bytes=54 * 2**20
        ),
        cost_estimate=pl.CostEstimate(
            flops=6 * TOKENS * WIDTH * D, bytes_accessed=20 * 2**20, transcendentals=0
        ),
    )(forward_in[0], grad_out[0], saved_in[0], weight[0], gain)
    return next_input[None], prev_grad[None], weight_grad[None], gain_grad


def solution(mesh):
    rows = P("section", "tensor", None)
    return jax.shard_map(
        local,
        mesh=mesh,
        in_specs=(rows, rows, rows, rows, P("section", "tensor")),
        out_specs=(rows, rows, rows, P("section", "tensor")),
        check_vma=False,
    )
```

```python
import jax
import jax.numpy as jnp
from jax import lax
from jax.experimental import pallas as pl
from jax.experimental.pallas import tpu as pltpu
from jax.sharding import PartitionSpec as P

D = 6144
TOKENS = 768
ROWS = 48
CHIP = 96
WIDTH = 384
PAIRED = 2 * WIDTH
HALF = D // 2
GA = 1408
GB = HALF - GA
CA = 1280
CB = HALF - CA
SUB_A = ((0, 512), (512, 512), (1024, 256))
SUB_B = ((0, 1024), (1024, 512), (1536, 256))
ORDER = (
    6, 0, 9, 23, 1, 7, 10, 8, 19, 2,
    21, 17, 13, 25, 3, 15, 26, 28, 20, 40,
    4, 11, 32, 34, 22, 24, 27, 41, 12, 29,
    5, 33, 42, 45, 30, 74, 75, 16, 31, 18,
    43, 98, 14, 46, 47, 35, 36, 99, 38, 77,
    78, 100, 79, 49, 66, 56, 37, 76, 48, 39,
    102, 93, 68, 80, 101, 103, 104, 58, 82, 85,
    55, 81, 65, 90, 51, 91, 50, 105, 67, 110,
    109, 57, 52, 113, 114, 106, 94, 107, 69, 70,
    71, 83, 72, 111, 86, 44, 64, 59, 60, 54,
    117, 61, 53, 62, 108, 88, 84, 95, 87, 73,
    63, 96, 92, 112, 118, 89, 97, 115, 116,
)
STRIP = 16
ROUNDS = 5
BF = jnp.bfloat16
F32 = jnp.float32
EPS = 1e-05
MESH = pl.DeviceIdType.MESH


def block(r, d):
    return (r * 4 + d) * CHIP


def normalize(values):
    center = jnp.mean(values, axis=1, keepdims=True)
    shifted = values - center
    recip = lax.rsqrt(jnp.mean(shifted * shifted, axis=1, keepdims=True) + EPS)
    return shifted * recip, recip


def strips(rows, body):
    def step(i, carry):
        body(pl.ds(pl.multiple_of(i * STRIP, STRIP), STRIP), i)
        return carry

    lax.fori_loop(0, rows // STRIP, step, 0)


def columns(start, width):
    return pl.ds(pl.multiple_of(start, 128), width)


def kernel(
    x_ref, g_ref, s_ref, w_ref, gain_ref,
    next_ref, prev_ref, wg_ref, gg_ref,
    G, W, WC, PF, HN, XR, XO, NX, SO, NS, SR, SF, BHT, DH, GI, XRES, GS,
    SA, RA, SA2, RA2, SAF, RAF, SB2, RB2, SBF, RBF, SBX, RBX, OA, OB,
    QC, QS, QR, QF, EC, ES, ER, MT, RT,
    send_sem, recv_sem, local_sem, group_sem, heard,
):
    s = lax.axis_index("section")
    t = lax.axis_index("tensor")
    y, xl, c = t // 4, (t // 2) % 2, t % 2
    mirrored, following, previous = 7 - s, (s + 1) % 8, (s + 7) % 8

    def at(section, along_y, row, core):
        return (section, ((y + along_y) % 4) * 4 + row * 2 + core)

    def row(r):
        return xl if r == 0 else 1 - xl

    sib = at(s, 0, xl, 1 - c)
    yp, ym = at(s, 1, xl, c), at(s, 3, xl, c)
    pair = at(s, 0, 1 - xl, c)

    mine = c * HALF
    other = (1 - c) * HALF
    cols_a = columns(mine, GA)
    cols_b = columns(mine + GA, GB)
    own_rows = pl.ds(pl.multiple_of(c * ROWS, 16), ROWS)
    sib_rows = pl.ds(pl.multiple_of((1 - c) * ROWS, 16), ROWS)

    names = {}
    sent = []

    def send(name, src, dst, device):
        i = names.setdefault(name, (len(names), dst))[0]
        copy = pltpu.make_async_remote_copy(
            src_ref=src, dst_ref=dst, send_sem=send_sem.at[i], recv_sem=recv_sem.at[i],
            device_id=device, device_id_type=MESH,
        )
        copy.start()
        sent.append(copy)

    def arrived(ref, sem, scratch_sem):
        pltpu.make_async_remote_copy(
            src_ref=ref, dst_ref=ref, send_sem=scratch_sem, recv_sem=sem, device_id=sib, device_id_type=MESH
        ).wait_recv()

    def left(ref, sem, scratch_sem):
        pltpu.make_async_remote_copy(
            src_ref=ref, dst_ref=ref, send_sem=sem, recv_sem=scratch_sem, device_id=sib, device_id_type=MESH
        ).wait_send()

    def recv(*wanted):
        for name in wanted:
            i, landing = names[name]
            arrived(landing, recv_sem.at[i], send_sem.at[i])

    E_IN, E_OUT, P_IN, P_OUT, N_IN, N_OUT = range(6)

    def grouped(src, dst, out, into, device):
        pltpu.make_async_remote_copy(
            src_ref=src, dst_ref=dst, send_sem=group_sem.at[out], recv_sem=group_sem.at[into],
            device_id=device, device_id_type=MESH,
        ).start()

    barrier = pltpu.get_barrier_semaphore()
    across = at(s + 1 - 2 * (s % 2), 0, 1 - xl, c)
    nearest = [sib, yp, ym, pair, across, at((s + 2) % 8, 0, xl, c), at((s + 6) % 8, 0, xl, c)]
    for friend in nearest:
        pl.semaphore_signal(barrier, inc=1, device_id=friend, device_id_type=MESH)

    load_x = pltpu.make_async_copy(x_ref, XO, local_sem.at[0])
    load_g = pltpu.make_async_copy(g_ref, G.at[own_rows, :], local_sem.at[1])
    load_s = pltpu.make_async_copy(s_ref, SO, local_sem.at[2])
    load_w = pltpu.make_async_copy(w_ref, W, local_sem.at[3])
    weight_rows = pl.ds(pl.multiple_of(c * WIDTH, 128), WIDTH)
    load_wc = pltpu.make_async_copy(w_ref.at[:, columns(mine, HALF)], WC.at[weight_rows, :], local_sem.at[4])
    load_xres = pltpu.make_async_copy(x_ref.at[:, columns(mine, HALF)], XRES.at[own_rows, :], local_sem.at[5])
    for load in (load_x, load_g, load_s, load_wc, load_xres, load_w):
        load.start()
    scale = gain_ref[...].astype(F32)
    GS[:, columns(c * WIDTH, WIDTH)] = jnp.broadcast_to(scale, (8, WIDTH))

    pl.semaphore_wait(barrier, len(nearest))

    def own(cols, r=0, d=0, first=0, rows=CHIP):
        return G.at[block(r, d) + first : block(r, d) + first + rows, cols]

    def near(cols, rows, r, d):
        return G.at[pl.ds(pl.multiple_of(block(r, d) + rows.start, 16), ROWS), cols]

    def from_here(e, r):
        return r * 4 + (4 - e) % 4

    tasks = []

    def task(run):
        tasks.append(run)
        return run

    def round_task(i):
        def run():
            if i > 1:
                pl.semaphore_wait(heard.at[i - 2], len(nearest))
            if i <= ROUNDS:
                for friend in nearest:
                    pl.semaphore_signal(heard.at[i - 1], inc=1, device_id=friend, device_id_type=MESH)

        tasks.append(run)

    for i in range(1, ROUNDS + 2):
        round_task(i)

    def first_step(part, a, b):
        send(("b_x", part), b[0], near(cols_b, b[1], 1, 0), pair)
        send(("a_p", part), a[0], near(cols_a, a[1], 0, 3), yp)
        send(("a_m", part), a[0], near(cols_a, a[1], 0, 1), ym)
        send(("b_p", part), b[0], near(cols_b, b[1], 0, 3), yp)
        send(("b_m", part), b[0], near(cols_b, b[1], 0, 1), ym)
        send(("a_x0", part), a[0], near(cols_a, a[1], 1, 0), pair)

    @task
    def first_o():
        send("g_half", g_ref.at[:, columns(other, HALF)], G.at[own_rows, columns(other, HALF)], sib)
        first_step(0, (g_ref.at[:, cols_a], own_rows), (g_ref.at[:, cols_b], own_rows))

    @task
    def first_s():
        recv("g_half")
        first_step(1, (G.at[sib_rows, cols_a], sib_rows), (G.at[sib_rows, cols_b], sib_rows))

    @task
    def inchip():
        send("gain", GS.at[:, columns(c * WIDTH, WIDTH)], GS.at[:, columns(c * WIDTH, WIDTH)], sib)
        send("w_half", w_ref.at[:, columns(other, HALF)], WC.at[weight_rows, :], sib)
        send("x_half", x_ref.at[:, columns(other, HALF)], XRES.at[own_rows, :], sib)
        send("g_rest", g_ref.at[:, columns(mine, HALF)], G.at[own_rows, columns(mine, HALF)], sib)

    @task
    def norm_x():
        load_x.wait()

        def body(rows, i):
            NX[rows, :] = normalize(XO[rows, :].astype(F32))[0].astype(BF)

        strips(ROWS, body)

    def features(e, r):
        return columns((((y + e) % 4) * 2 + row(r)) * PAIRED, PAIRED)

    def x_task(e, r):
        def run():
            send(("x", r, e), NX.at[:, features(e, r)], XR.at[from_here(e, r)], at(s, e, row(r), c))

        tasks.append(run)

    @task
    def norm_s():
        load_s.wait()
        QC[...] = jnp.zeros(QC.shape, F32)

        def body(rows, i):
            normed, recip = normalize(SO[rows, :].astype(F32))
            NS[rows, :] = normed.astype(BF)
            QC[rows, :] = jnp.broadcast_to(recip, (STRIP, 128))

        strips(ROWS, body)
        QS[...] = QC[...].T[0:8, :]

    def s_task(e, r):
        def run():
            target = at(mirrored, e, row(r), c)
            send(("s", r, e), NS.at[:, features(e, r)], SR.at[from_here(e, r)], target)
            send(("q", r, e), QS, QR.at[from_here(e, r)], target)

        tasks.append(run)

    for e in range(4):
        for r in range(2):
            s_task(e, r)
            if (e, r) != (0, 0):
                x_task(e, r)

    def share(cols, r, d):
        ref = own(cols, r, d)
        send((cols is cols_a, r, d), ref, ref, sib)

    def halves(name):
        return (name, 0), (name, 1)

    @task
    def bx():
        recv(*halves("b_x"))
        send("bx_p", own(cols_b, 1, 0), own(cols_b, 1, 3), yp)
        send("bx_m", own(cols_b, 1, 0), own(cols_b, 1, 1), ym)
        share(cols_b, 1, 0)

    @task
    def ap():
        recv(*halves("a_p"))
        send("a_pp", own(cols_a, 0, 3, 0, ROWS), own(cols_a, 0, 2, 0, ROWS), yp)
        send("a_x3", own(cols_a, 0, 3), own(cols_a, 1, 3), pair)
        share(cols_a, 0, 3)

    @task
    def am():
        recv(*halves("a_m"))
        send("a_mm", own(cols_a, 0, 1, ROWS, ROWS), own(cols_a, 0, 2, ROWS, ROWS), ym)
        send("a_x1", own(cols_a, 0, 1), own(cols_a, 1, 1), pair)
        share(cols_a, 0, 1)

    @task
    def bp():
        recv(*halves("b_p"))
        send("b_pp", own(cols_b, 0, 3), own(cols_b, 0, 2), yp)
        share(cols_b, 0, 3)

    @task
    def bxm():
        recv("bx_m")
        send("bx_mm", own(cols_b, 1, 1), own(cols_b, 1, 2), ym)
        share(cols_b, 1, 1)

    @task
    def ax2():
        recv("a_pp", "a_mm")
        send("a_x2", own(cols_a, 0, 2), own(cols_a, 1, 2), pair)
        share(cols_a, 0, 2)

    def keep_task(wanted, cols, r, d):
        def run():
            recv(*wanted)
            share(cols, r, d)

        tasks.append(run)

    keep_task(halves("b_m"), cols_b, 0, 1)
    keep_task(("bx_p",), cols_b, 1, 3)
    keep_task(halves("a_x0"), cols_a, 1, 0)
    keep_task(("a_x3",), cols_a, 1, 3)
    keep_task(("a_x1",), cols_a, 1, 1)
    keep_task(("b_pp",), cols_b, 0, 2)
    keep_task(("bx_mm",), cols_b, 1, 2)
    keep_task(("a_x2",), cols_a, 1, 2)

    @task
    def hidden():
        load_g.wait()
        load_w.wait()
        recv("gain")
        both = GS[0:1, :]
        for d in (0, 3, 1, 2):
            for r in range(2):
                if (d, r) == (0, 0):
                    values = NX[:, features(0, 0)]
                else:
                    recv(("x", r, (4 - d) % 4))
                    values = XR[r * 4 + d]
                HN[r * 4 + d, own_rows, :] = (values.astype(F32) * both).astype(BF)
        send("hid", HN.at[:, own_rows, :], HN.at[:, own_rows, :], sib)

    def project(first, chips, start, width, store):
        def tile(i, carry):
            here = pl.multiple_of(i * 256, 256)
            there = pl.ds(pl.multiple_of(start + here, 256), 256)
            store(
                pl.ds(here, 256),
                there,
                jnp.dot(
                    HN[first : first + chips].reshape(chips * CHIP, PAIRED),
                    WC[:, there],
                    preferred_element_type=F32,
                ),
            )
            return carry

        lax.fori_loop(0, width // 256, tile, 0)

    @task
    def proj_a():
        load_wc.wait()
        load_xres.wait()
        recv("hid", "w_half", "x_half")

        def store(here, there, value):
            SA[0:CHIP, here] = (value[0:CHIP] + XRES[:, here].astype(F32)).astype(BF)
            SA[CHIP : 4 * CHIP, here] = value[CHIP : 4 * CHIP].astype(BF)

        project(0, 4, 0, CA, store)

    @task
    def proj_b():
        def store(here, there, value):
            PF[:, there] = value

        project(0, 8, CA, CB, store)

    @task
    def proj_c():
        def store(here, there, value):
            PF[4 * CHIP : 8 * CHIP, here] = value

        project(4, 4, 0, CA, store)

    def combine(dst, terms, width, first=0, rows=CHIP):
        def body(strip, i):
            total = None
            for ref, base, start in terms:
                here = pl.ds(pl.multiple_of(base + first + i * STRIP, STRIP), STRIP)
                value = ref[here, start : start + width].astype(F32)
                total = value if total is None else total + value
            ref, base, start = dst
            ref[pl.ds(pl.multiple_of(base + first + i * STRIP, STRIP), STRIP), start : start + width] = total.astype(BF)

        strips(rows, body)

    def deliver(src, start, width, offset):
        for core in range(2):
            grouped(
                src.at[core * ROWS : (core + 1) * ROWS, start : start + width],
                next_ref.at[:, columns(mine + offset + start, width)],
                N_OUT,
                N_IN,
                at(following, 0, 1 - xl, core),
            )

    def reduce_a(k):
        a, w = SUB_A[k]

        def pass_on(name, src, dst, first, rows, device):
            send(
                (name, k), src.at[first : first + rows, a : a + w], dst.at[first : first + rows, a : a + w], device
            )

        def cross(d):
            def run():
                pass_on(d, SA, RA, d * CHIP, CHIP, pair)

            tasks.append(run)

        for d in range(4):
            cross(d)

        def a2():
            recv((2, k))
            combine((SA2, 0, a), [(PF, block(1, 2), a), (RA, 2 * CHIP, a)], w)
            pass_on("ra2p", SA2, RA2, 0, ROWS, yp)
            pass_on("ra2m", SA2, RA2, ROWS, ROWS, ym)

        def a1():
            recv((1, k))
            combine((SAF, 0, a), [(PF, block(1, 1), a), (RA, CHIP, a)], w, ROWS, ROWS)
            pass_on("rafp1", SAF, RAF, ROWS, ROWS, yp)

        def a3():
            recv((3, k))
            combine((SAF, CHIP, a), [(PF, block(1, 3), a), (RA, 3 * CHIP, a)], w, 0, ROWS)
            pass_on("rafm0", SAF, RAF, CHIP, ROWS, ym)

        def a2p():
            recv(("ra2p", k))
            combine((SAF, 0, a), [(PF, block(1, 1), a), (RA, CHIP, a), (RA2, 0, a)], w, 0, ROWS)
            pass_on("rafp0", SAF, RAF, 0, ROWS, yp)

        def a2m():
            recv(("ra2m", k))
            combine((SAF, CHIP, a), [(PF, block(1, 3), a), (RA, 3 * CHIP, a), (RA2, 0, a)], w, ROWS, ROWS)
            pass_on("rafm1", SAF, RAF, CHIP + ROWS, ROWS, ym)

        def fin_a():
            for name in (0, "rafp0", "rafp1", "rafm0", "rafm1"):
                recv((name, k))
            combine((OA, 0, a), [(PF, block(1, 0), a), (RA, 0, a), (RAF, 0, a), (RAF, CHIP, a)], w)
            deliver(OA, a, w, 0)

        tasks.extend((a2, a1, a3, a2p, a2m, fin_a))

    def reduce_b(k):
        a, w = SUB_B[k]

        def hand(name, src, dst, first, device, terms):
            combine((src, first, a), terms, w)
            send(
                (name, k), src.at[first : first + CHIP, a : a + w], dst.at[first : first + CHIP, a : a + w], device
            )

        def rb2p():
            hand("rb2p", SB2, RB2, 0, yp, [(PF, block(0, 2), CA + a)])

        def rb2m():
            hand("rb2m", SB2, RB2, CHIP, ym, [(PF, block(1, 2), CA + a)])

        def rbf01():
            hand("rbf01", SBF, RBF, CHIP, yp, [(PF, block(1, 1), CA + a)])

        def rbf10():
            hand("rbf10", SBF, RBF, 2 * CHIP, ym, [(PF, block(0, 3), CA + a)])

        def rbf00():
            recv(("rb2p", k))
            hand("rbf00", SBF, RBF, 0, yp, [(PF, block(0, 1), CA + a), (RB2, 0, a)])

        def rbf11():
            recv(("rb2m", k))
            hand("rbf11", SBF, RBF, 3 * CHIP, ym, [(PF, block(1, 3), CA + a), (RB2, CHIP, a)])

        def rbx():
            recv(("rbf00", k), ("rbf10", k))
            hand(
                "rbx", SBX, RBX, 0, pair,
                [(PF, block(0, 0), CA + a), (RBF, 0, a), (RBF, 2 * CHIP, a), (XRES, 0, CA + a)],
            )

        def fin_b():
            recv(("rbf01", k), ("rbf11", k), ("rbx", k))
            combine((OB, 0, a), [(PF, block(1, 0), CA + a), (RBF, CHIP, a), (RBF, 3 * CHIP, a), (RBX, 0, a)], w)
            deliver(OB, a, w, CA)

        tasks.extend((rb2p, rb2m, rbf01, rbf10, rbf00, rbf11, rbx, fin_b))

    for k in range(len(SUB_A)):
        reduce_a(k)
    for k in range(len(SUB_B)):
        reduce_b(k)

    def dh_task(blocks, wanted):
        def run():
            recv(*wanted)
            first, second = (pl.ds(block(r, d), CHIP) for r, d in blocks)
            DH[first, :] = jnp.zeros((CHIP, WIDTH), F32)
            DH[second, :] = jnp.zeros((CHIP, WIDTH), F32)

            def step(j, carry):
                here = pl.ds(pl.multiple_of(j * 1024, 1024), 1024)
                part = lax.dot_general(
                    jnp.concatenate([G[first, here], G[second, here]], axis=0),
                    W[:, here],
                    (((1,), (1,)), ((), ())),
                    preferred_element_type=F32,
                )
                DH[first, :] += part[0:CHIP]
                DH[second, :] += part[CHIP : 2 * CHIP]
                return carry

            lax.fori_loop(0, D // 1024, step, 0)

        tasks.append(run)

    dh_task(((0, 0), (1, 0)), ("g_rest", (True, 1, 0), (False, 1, 0)))
    dh_task(((0, 1), (0, 3)), ((True, 0, 3), (True, 0, 1), (False, 0, 3), (False, 0, 1)))
    dh_task(((1, 1), (1, 3)), ((True, 1, 3), (True, 1, 1), (False, 1, 3), (False, 1, 1)))
    dh_task(((0, 2), (1, 2)), ((True, 0, 2), (True, 1, 2), (False, 0, 2), (False, 1, 2)))

    def local_copy(i, src, dst):
        copy = pltpu.make_async_copy(src, dst, local_sem.at[i])
        copy.start()
        return copy

    kept = {}

    @task
    def s_sib():
        for e in (1, 3, 2, 0):
            for r in range(2):
                recv(("s", r, e), ("q", r, e))
        send("s_sib", SR.at[:, :, columns((1 - c) * WIDTH, WIDTH)], SF.at[:, own_rows, :], sib)
        send("q_sib", QR, QF.at[:, c], sib)
        kept["s"] = local_copy(7, SR.at[:, :, columns(c * WIDTH, WIDTH)], SF.at[:, own_rows, :])
        kept["q"] = local_copy(8, QR, QF.at[:, c])

    def chip_of(b):
        return ((y + b % 4) % 4) * 2 + (xl + b // 4) % 2

    def add_sums(blocks):
        lane = lax.broadcasted_iota(jnp.int32, (CHIP, 128), 1)
        for b in blocks:
            grad = DH[b * CHIP : (b + 1) * CHIP, :]
            normed = SF[b].astype(F32)
            gg_ref[...] += jnp.sum(grad * normed, axis=0, keepdims=True)
            scaled = grad.astype(BF).astype(F32) * scale
            first = jnp.sum(scaled, axis=1, keepdims=True)
            second = jnp.sum(scaled * normed, axis=1, keepdims=True)
            place = 2 * chip_of(b)
            EC[0:CHIP, :] += jnp.where(lane == place, first, 0.0) + jnp.where(lane == place + 1, second, 0.0)

    @task
    def sums_a():
        recv("s_sib", "q_sib")
        kept["s"].wait()
        kept["q"].wait()
        EC[...] = jnp.zeros(EC.shape, F32)
        gg_ref[...] = jnp.zeros(gg_ref.shape, F32)
        add_sums((0, 4, 1, 3, 5, 7))

    @task
    def sums_b():
        add_sums((2, 6))
        ES[...] = EC[...].T[0:16, :]
        pltpu.make_async_copy(ES, ER.at[c], group_sem.at[E_IN]).start()
        for e in (2, 1, 3, 0):
            for r in range(2):
                grouped(ES, ER.at[from_here(e, r) * 2 + c], E_OUT, E_IN, at(s, e, row(r), 1 - c))
                if (e, r) != (0, 0):
                    grouped(ES, ER.at[from_here(e, r) * 2 + c], E_OUT, E_IN, at(s, e, row(r), c))

    @task
    def gi():
        arrived(ER, group_sem.at[E_IN], group_sem.at[E_OUT])
        total = ER[0]
        for k in range(1, 16):
            total = total + ER[k]
        QC[0:16, :] = total * (1.0 / D)
        EC[...] = jnp.zeros(EC.shape, F32)
        for b in range(8):
            EC[2 * b : 2 * b + 2, :] = QC[pl.ds(2 * chip_of(b), 2), :]
        MT[...] = EC[...].T
        QC[...] = jnp.zeros(QC.shape, F32)
        for b in range(8):
            for core in range(2):
                QC[b * 2 + core : b * 2 + core + 1, :] = QF[b, core, 0:1, :]
        RT[...] = QC[...].T

    def p_task(e, r):
        def run():
            b = r * 4 + e
            for core in range(2):
                k = b * 2 + core
                part = slice(core * ROWS, (core + 1) * ROWS)
                rows = slice(k * ROWS, (k + 1) * ROWS)
                mean_e = MT[part, 2 * b : 2 * b + 1]
                mean_en = MT[part, 2 * b + 1 : 2 * b + 2]
                recip = RT[0:ROWS, k : k + 1]
                scaled = DH[rows, :].astype(BF).astype(F32) * scale
                inner = scaled - mean_e - SF[b, part, :].astype(F32) * mean_en
                upstream = G[rows, columns(t * WIDTH, WIDTH)].astype(F32)
                GI[b, part, :] = (upstream + recip * inner).astype(BF)
                grouped(
                    GI.at[b, part, :],
                    prev_ref.at[:, columns(t * WIDTH, WIDTH)],
                    P_OUT,
                    P_IN,
                    at(previous, e, row(r), core),
                )

        tasks.append(run)

    for e in range(4):
        for r in range(2):
            p_task(e, r)

    @task
    def bht():
        BHT[...] = (SF[...].reshape(TOKENS, WIDTH).astype(F32) * scale).T.astype(BF)

    def wg_task(i):
        def run():
            def step(j, carry):
                here = pl.ds(pl.multiple_of(j * 256, 256), 256)
                wg_ref[:, here] = jnp.dot(BHT[...], G[:, here], preferred_element_type=F32).astype(BF)
                return carry

            lax.fori_loop(i * 6, (i + 1) * 6, step, 0)

        tasks.append(run)

    for i in range(4):
        wg_task(i)

    for i in ORDER:
        tasks[i]()

    for copy in sent:
        copy.wait_send()
    left(ER.at[0:15], group_sem.at[E_OUT], group_sem.at[E_IN])
    left(next_ref, group_sem.at[N_OUT], group_sem.at[N_IN])
    left(prev_ref, group_sem.at[P_OUT], group_sem.at[P_IN])
    arrived(prev_ref, group_sem.at[P_IN], group_sem.at[P_OUT])
    arrived(next_ref, group_sem.at[N_IN], group_sem.at[N_OUT])


def local(forward_in, grad_out, saved_in, weight, gain):
    anywhere = pl.BlockSpec(memory_space=pl.ANY)
    vmem = pl.BlockSpec(memory_space=pltpu.VMEM)
    v = pltpu.VMEM
    out_shape = (
        jax.ShapeDtypeStruct((ROWS, D), BF),
        jax.ShapeDtypeStruct((ROWS, D), BF),
        jax.ShapeDtypeStruct((WIDTH, D), BF),
        jax.ShapeDtypeStruct((1, WIDTH), F32),
    )
    next_input, prev_grad, weight_grad, gain_grad = pl.pallas_call(
        kernel,
        out_shape=tuple(v(out.shape, out.dtype) for out in out_shape),
        in_specs=[anywhere, anywhere, anywhere, anywhere, vmem],
        out_specs=(vmem,) * 4,
        scratch_shapes=[
            v((TOKENS, D), BF),
            v((WIDTH, D), BF),
            v((PAIRED, HALF), BF),
            v((TOKENS, HALF), F32),
            v((8, CHIP, PAIRED), BF),
            v((8, ROWS, PAIRED), BF),
            v((ROWS, D), BF),
            v((ROWS, D), BF),
            v((ROWS, D), BF),
            v((ROWS, D), BF),
            v((8, ROWS, PAIRED), BF),
            v((8, CHIP, WIDTH), BF),
            v((WIDTH, TOKENS), BF),
            v((TOKENS, WIDTH), F32),
            v((8, CHIP, WIDTH), BF),
            v((CHIP, HALF), BF),
            v((8, PAIRED), F32),
            v((4 * CHIP, CA), BF),
            v((4 * CHIP, CA), BF),
            v((CHIP, CA), BF),
            v((CHIP, CA), BF),
            v((2 * CHIP, CA), BF),
            v((2 * CHIP, CA), BF),
            v((2 * CHIP, CB), BF),
            v((2 * CHIP, CB), BF),
            v((4 * CHIP, CB), BF),
            v((4 * CHIP, CB), BF),
            v((CHIP, CB), BF),
            v((CHIP, CB), BF),
            v((CHIP, CA), BF),
            v((CHIP, CB), BF),
            v((128, 128), F32),
            v((8, 128), F32),
            v((8, 8, 128), F32),
            v((8, 2, 8, 128), F32),
            v((128, 128), F32),
            v((16, 128), F32),
            v((16, 16, 128), F32),
            v((128, 128), F32),
            v((128, 128), F32),
            pltpu.SemaphoreType.DMA((128,)),
            pltpu.SemaphoreType.DMA((128,)),
            pltpu.SemaphoreType.DMA((9,)),
            pltpu.SemaphoreType.DMA((6,)),
            pltpu.SemaphoreType.REGULAR((ROUNDS,)),
        ],
        compiler_params=pltpu.CompilerParams(
            collective_id=0, has_side_effects=True, vmem_limit_bytes=54 * 2**20
        ),
        cost_estimate=pl.CostEstimate(
            flops=6 * TOKENS * WIDTH * D, bytes_accessed=20 * 2**20, transcendentals=0
        ),
    )(forward_in[0], grad_out[0], saved_in[0], weight[0], gain)
    return next_input[None], prev_grad[None], weight_grad[None], gain_grad


def solution(mesh):
    rows = P("section", "tensor", None)
    return jax.shard_map(
        local,
        mesh=mesh,
        in_specs=(rows, rows, rows, rows, P("section", "tensor")),
        out_specs=(rows, rows, rows, P("section", "tensor")),
        check_vma=False,
    )
```

```python
import jax
import jax.numpy as jnp
from jax import lax
from jax.experimental import pallas as pl
from jax.experimental.pallas import tpu as pltpu
from jax.sharding import PartitionSpec as P

D = 6144
TOKENS = 768
ROWS = 48
CHIP = 96
WIDTH = 384
PAIRED = 2 * WIDTH
HALF = D // 2
GA = 1408
GB = HALF - GA
CA = 1280
CB = HALF - CA
SUB_A = ((0, 512), (512, 512), (1024, 256))
SUB_B = ((0, 1024), (1024, 512), (1536, 256))
ORDER = (
    6, 0, 9, 23, 1, 7, 10, 8, 19, 2,
    21, 17, 13, 25, 3, 15, 26, 28, 20, 40,
    4, 11, 32, 34, 22, 24, 27, 41, 12, 29,
    5, 33, 42, 45, 30, 74, 75, 16, 31, 18,
    43, 98, 14, 46, 47, 35, 36, 99, 38, 77,
    78, 100, 79, 49, 66, 56, 37, 76, 48, 39,
    102, 93, 68, 80, 101, 103, 104, 58, 82, 85,
    55, 81, 65, 90, 51, 91, 50, 105, 67, 110,
    109, 57, 52, 113, 114, 106, 94, 107, 69, 70,
    71, 83, 72, 111, 86, 44, 64, 59, 60, 54,
    117, 61, 53, 62, 108, 88, 84, 95, 87, 73,
    63, 96, 92, 112, 118, 89, 97, 115, 116,
)
STRIP = 16
ROUNDS = 5
BF = jnp.bfloat16
F32 = jnp.float32
EPS = 1e-05
MESH = pl.DeviceIdType.MESH


def block(r, d):
    return (r * 4 + d) * CHIP


def normalize(values):
    center = jnp.mean(values, axis=1, keepdims=True)
    shifted = values - center
    recip = lax.rsqrt(jnp.mean(shifted * shifted, axis=1, keepdims=True) + EPS)
    return shifted * recip, recip


def strips(rows, body):
    def step(i, carry):
        body(pl.ds(pl.multiple_of(i * STRIP, STRIP), STRIP), i)
        return carry

    lax.fori_loop(0, rows // STRIP, step, 0)


def columns(start, width):
    return pl.ds(pl.multiple_of(start, 128), width)


def kernel(
    x_ref, g_ref, s_ref, w_ref, gain_ref,
    next_ref, prev_ref, wg_ref, gg_ref,
    G, W, WC, PF, HN, XR, XO, NX, SO, NS, SR, SF, BHT, DH, GI, XRES, GS,
    SA, RA, SA2, RA2, SAF, RAF, SB2, RB2, SBF, RBF, SBX, RBX, OA, OB,
    QC, QS, QR, QF, EC, ES, ER, MT, RT,
    send_sem, recv_sem, local_sem, group_sem, heard,
):
    s = lax.axis_index("section")
    t = lax.axis_index("tensor")
    y, xl, c = t // 4, (t // 2) % 2, t % 2
    mirrored, following, previous = 7 - s, (s + 1) % 8, (s + 7) % 8

    def at(section, along_y, row, core):
        return (section, ((y + along_y) % 4) * 4 + row * 2 + core)

    def row(r):
        return xl if r == 0 else 1 - xl

    sib = at(s, 0, xl, 1 - c)
    yp, ym = at(s, 1, xl, c), at(s, 3, xl, c)
    pair = at(s, 0, 1 - xl, c)

    mine = c * HALF
    other = (1 - c) * HALF
    cols_a = columns(mine, GA)
    cols_b = columns(mine + GA, GB)
    own_rows = pl.ds(pl.multiple_of(c * ROWS, 16), ROWS)
    sib_rows = pl.ds(pl.multiple_of((1 - c) * ROWS, 16), ROWS)

    names = {}
    sent = []

    def send(name, src, dst, device):
        i = names.setdefault(name, (len(names), dst))[0]
        copy = pltpu.make_async_remote_copy(
            src_ref=src, dst_ref=dst, send_sem=send_sem.at[i], recv_sem=recv_sem.at[i],
            device_id=device, device_id_type=MESH,
        )
        copy.start()
        sent.append(copy)

    def arrived(ref, sem, scratch_sem):
        pltpu.make_async_remote_copy(
            src_ref=ref, dst_ref=ref, send_sem=scratch_sem, recv_sem=sem, device_id=sib, device_id_type=MESH
        ).wait_recv()

    def left(ref, sem, scratch_sem):
        pltpu.make_async_remote_copy(
            src_ref=ref, dst_ref=ref, send_sem=sem, recv_sem=scratch_sem, device_id=sib, device_id_type=MESH
        ).wait_send()

    def recv(*wanted):
        for name in wanted:
            i, landing = names[name]
            arrived(landing, recv_sem.at[i], send_sem.at[i])

    E_IN, E_OUT, P_IN, P_OUT, N_IN, N_OUT = range(6)

    def grouped(src, dst, out, into, device):
        pltpu.make_async_remote_copy(
            src_ref=src, dst_ref=dst, send_sem=group_sem.at[out], recv_sem=group_sem.at[into],
            device_id=device, device_id_type=MESH,
        ).start()

    barrier = pltpu.get_barrier_semaphore()
    across = at(s + 1 - 2 * (s % 2), 0, 1 - xl, c)
    nearest = [sib, yp, ym, pair, across, at((s + 2) % 8, 0, xl, c), at((s + 6) % 8, 0, xl, c)]
    for friend in nearest:
        pl.semaphore_signal(barrier, inc=1, device_id=friend, device_id_type=MESH)

    load_x = pltpu.make_async_copy(x_ref, XO, local_sem.at[0])
    load_g = pltpu.make_async_copy(g_ref, G.at[own_rows, :], local_sem.at[1])
    load_s = pltpu.make_async_copy(s_ref, SO, local_sem.at[2])
    load_w = pltpu.make_async_copy(w_ref, W, local_sem.at[3])
    weight_rows = pl.ds(pl.multiple_of(c * WIDTH, 128), WIDTH)
    load_wc = pltpu.make_async_copy(w_ref.at[:, columns(mine, HALF)], WC.at[weight_rows, :], local_sem.at[4])
    load_xres = pltpu.make_async_copy(x_ref.at[:, columns(mine, HALF)], XRES.at[own_rows, :], local_sem.at[5])
    for load in (load_x, load_g, load_s, load_wc, load_xres, load_w):
        load.start()
    scale = gain_ref[...].astype(F32)
    GS[:, columns(c * WIDTH, WIDTH)] = jnp.broadcast_to(scale, (8, WIDTH))

    pl.semaphore_wait(barrier, len(nearest))

    def own(cols, r=0, d=0, first=0, rows=CHIP):
        return G.at[block(r, d) + first : block(r, d) + first + rows, cols]

    def near(cols, rows, r, d):
        return G.at[pl.ds(pl.multiple_of(block(r, d) + rows.start, 16), ROWS), cols]

    def from_here(e, r):
        return r * 4 + (4 - e) % 4

    tasks = []

    def task(run):
        tasks.append(run)
        return run

    def round_task(i):
        def run():
            if i > 1:
                pl.semaphore_wait(heard.at[i - 2], len(nearest))
            if i <= ROUNDS:
                for friend in nearest:
                    pl.semaphore_signal(heard.at[i - 1], inc=1, device_id=friend, device_id_type=MESH)

        tasks.append(run)

    for i in range(1, ROUNDS + 2):
        round_task(i)

    def first_step(part, a, b):
        send(("b_x", part), b[0], near(cols_b, b[1], 1, 0), pair)
        send(("a_p", part), a[0], near(cols_a, a[1], 0, 3), yp)
        send(("a_m", part), a[0], near(cols_a, a[1], 0, 1), ym)
        send(("b_p", part), b[0], near(cols_b, b[1], 0, 3), yp)
        send(("b_m", part), b[0], near(cols_b, b[1], 0, 1), ym)
        send(("a_x0", part), a[0], near(cols_a, a[1], 1, 0), pair)

    @task
    def first_o():
        send("g_half", g_ref.at[:, columns(other, HALF)], G.at[own_rows, columns(other, HALF)], sib)
        first_step(0, (g_ref.at[:, cols_a], own_rows), (g_ref.at[:, cols_b], own_rows))

    @task
    def first_s():
        recv("g_half")
        first_step(1, (G.at[sib_rows, cols_a], sib_rows), (G.at[sib_rows, cols_b], sib_rows))

    @task
    def inchip():
        send("gain", GS.at[:, columns(c * WIDTH, WIDTH)], GS.at[:, columns(c * WIDTH, WIDTH)], sib)
        send("w_half", w_ref.at[:, columns(other, HALF)], WC.at[weight_rows, :], sib)
        send("x_half", x_ref.at[:, columns(other, HALF)], XRES.at[own_rows, :], sib)
        send("g_rest", g_ref.at[:, columns(mine, HALF)], G.at[own_rows, columns(mine, HALF)], sib)

    @task
    def norm_x():
        load_x.wait()

        def body(rows, i):
            NX[rows, :] = normalize(XO[rows, :].astype(F32))[0].astype(BF)

        strips(ROWS, body)

    def features(e, r):
        return columns((((y + e) % 4) * 2 + row(r)) * PAIRED, PAIRED)

    def x_task(e, r):
        def run():
            send(("x", r, e), NX.at[:, features(e, r)], XR.at[from_here(e, r)], at(s, e, row(r), c))

        tasks.append(run)

    @task
    def norm_s():
        load_s.wait()
        QC[...] = jnp.zeros(QC.shape, F32)

        def body(rows, i):
            normed, recip = normalize(SO[rows, :].astype(F32))
            NS[rows, :] = normed.astype(BF)
            QC[rows, :] = jnp.broadcast_to(recip, (STRIP, 128))

        strips(ROWS, body)
        QS[...] = QC[...].T[0:8, :]

    def s_task(e, r):
        def run():
            target = at(mirrored, e, row(r), c)
            send(("s", r, e), NS.at[:, features(e, r)], SR.at[from_here(e, r)], target)
            send(("q", r, e), QS, QR.at[from_here(e, r)], target)

        tasks.append(run)

    for e in range(4):
        for r in range(2):
            s_task(e, r)
            if (e, r) != (0, 0):
                x_task(e, r)

    def share(cols, r, d):
        ref = own(cols, r, d)
        send((cols is cols_a, r, d), ref, ref, sib)

    def halves(name):
        return (name, 0), (name, 1)

    @task
    def bx():
        recv(*halves("b_x"))
        send("bx_p", own(cols_b, 1, 0), own(cols_b, 1, 3), yp)
        send("bx_m", own(cols_b, 1, 0), own(cols_b, 1, 1), ym)
        share(cols_b, 1, 0)

    @task
    def ap():
        recv(*halves("a_p"))
        send("a_pp", own(cols_a, 0, 3, 0, ROWS), own(cols_a, 0, 2, 0, ROWS), yp)
        send("a_x3", own(cols_a, 0, 3), own(cols_a, 1, 3), pair)
        share(cols_a, 0, 3)

    @task
    def am():
        recv(*halves("a_m"))
        send("a_mm", own(cols_a, 0, 1, ROWS, ROWS), own(cols_a, 0, 2, ROWS, ROWS), ym)
        send("a_x1", own(cols_a, 0, 1), own(cols_a, 1, 1), pair)
        share(cols_a, 0, 1)

    @task
    def bp():
        recv(*halves("b_p"))
        send("b_pp", own(cols_b, 0, 3), own(cols_b, 0, 2), yp)
        share(cols_b, 0, 3)

    @task
    def bxm():
        recv("bx_m")
        send("bx_mm", own(cols_b, 1, 1), own(cols_b, 1, 2), ym)
        share(cols_b, 1, 1)

    @task
    def ax2():
        recv("a_pp", "a_mm")
        send("a_x2", own(cols_a, 0, 2), own(cols_a, 1, 2), pair)
        share(cols_a, 0, 2)

    def keep_task(wanted, cols, r, d):
        def run():
            recv(*wanted)
            share(cols, r, d)

        tasks.append(run)

    keep_task(halves("b_m"), cols_b, 0, 1)
    keep_task(("bx_p",), cols_b, 1, 3)
    keep_task(halves("a_x0"), cols_a, 1, 0)
    keep_task(("a_x3",), cols_a, 1, 3)
    keep_task(("a_x1",), cols_a, 1, 1)
    keep_task(("b_pp",), cols_b, 0, 2)
    keep_task(("bx_mm",), cols_b, 1, 2)
    keep_task(("a_x2",), cols_a, 1, 2)

    @task
    def hidden():
        load_g.wait()
        load_w.wait()
        recv("gain")
        both = GS[0:1, :]
        for d in (0, 3, 1, 2):
            for r in range(2):
                if (d, r) == (0, 0):
                    values = NX[:, features(0, 0)]
                else:
                    recv(("x", r, (4 - d) % 4))
                    values = XR[r * 4 + d]
                HN[r * 4 + d, own_rows, :] = (values.astype(F32) * both).astype(BF)
        send("hid", HN.at[:, own_rows, :], HN.at[:, own_rows, :], sib)

    def project(first, chips, start, width, store):
        def tile(i, carry):
            here = pl.multiple_of(i * 256, 256)
            there = pl.ds(pl.multiple_of(start + here, 256), 256)
            store(
                pl.ds(here, 256),
                there,
                jnp.dot(
                    HN[first : first + chips].reshape(chips * CHIP, PAIRED),
                    WC[:, there],
                    preferred_element_type=F32,
                ),
            )
            return carry

        lax.fori_loop(0, width // 256, tile, 0)

    @task
    def proj_a():
        load_wc.wait()
        load_xres.wait()
        recv("hid", "w_half", "x_half")

        def store(here, there, value):
            SA[0:CHIP, here] = (value[0:CHIP] + XRES[:, here].astype(F32)).astype(BF)
            SA[CHIP : 4 * CHIP, here] = value[CHIP : 4 * CHIP].astype(BF)

        project(0, 4, 0, CA, store)

    @task
    def proj_b():
        def store(here, there, value):
            PF[:, there] = value

        project(0, 8, CA, CB, store)

    @task
    def proj_c():
        def store(here, there, value):
            PF[4 * CHIP : 8 * CHIP, here] = value

        project(4, 4, 0, CA, store)

    def combine(dst, terms, width, first=0, rows=CHIP):
        def body(strip, i):
            total = None
            for ref, base, start in terms:
                here = pl.ds(pl.multiple_of(base + first + i * STRIP, STRIP), STRIP)
                value = ref[here, start : start + width].astype(F32)
                total = value if total is None else total + value
            ref, base, start = dst
            ref[pl.ds(pl.multiple_of(base + first + i * STRIP, STRIP), STRIP), start : start + width] = total.astype(BF)

        strips(rows, body)

    def deliver(src, start, width, offset):
        for core in range(2):
            grouped(
                src.at[core * ROWS : (core + 1) * ROWS, start : start + width],
                next_ref.at[:, columns(mine + offset + start, width)],
                N_OUT,
                N_IN,
                at(following, 0, 1 - xl, core),
            )

    def reduce_a(k):
        a, w = SUB_A[k]

        def pass_on(name, src, dst, first, rows, device):
            send(
                (name, k), src.at[first : first + rows, a : a + w], dst.at[first : first + rows, a : a + w], device
            )

        def cross(d):
            def run():
                pass_on(d, SA, RA, d * CHIP, CHIP, pair)

            tasks.append(run)

        for d in range(4):
            cross(d)

        def a2():
            recv((2, k))
            combine((SA2, 0, a), [(PF, block(1, 2), a), (RA, 2 * CHIP, a)], w)
            pass_on("ra2p", SA2, RA2, 0, ROWS, yp)
            pass_on("ra2m", SA2, RA2, ROWS, ROWS, ym)

        def a1():
            recv((1, k))
            combine((SAF, 0, a), [(PF, block(1, 1), a), (RA, CHIP, a)], w, ROWS, ROWS)
            pass_on("rafp1", SAF, RAF, ROWS, ROWS, yp)

        def a3():
            recv((3, k))
            combine((SAF, CHIP, a), [(PF, block(1, 3), a), (RA, 3 * CHIP, a)], w, 0, ROWS)
            pass_on("rafm0", SAF, RAF, CHIP, ROWS, ym)

        def a2p():
            recv(("ra2p", k))
            combine((SAF, 0, a), [(PF, block(1, 1), a), (RA, CHIP, a), (RA2, 0, a)], w, 0, ROWS)
            pass_on("rafp0", SAF, RAF, 0, ROWS, yp)

        def a2m():
            recv(("ra2m", k))
            combine((SAF, CHIP, a), [(PF, block(1, 3), a), (RA, 3 * CHIP, a), (RA2, 0, a)], w, ROWS, ROWS)
            pass_on("rafm1", SAF, RAF, CHIP + ROWS, ROWS, ym)

        def fin_a():
            for name in (0, "rafp0", "rafp1", "rafm0", "rafm1"):
                recv((name, k))
            combine((OA, 0, a), [(PF, block(1, 0), a), (RA, 0, a), (RAF, 0, a), (RAF, CHIP, a)], w)
            deliver(OA, a, w, 0)

        tasks.extend((a2, a1, a3, a2p, a2m, fin_a))

    def reduce_b(k):
        a, w = SUB_B[k]

        def hand(name, src, dst, first, device, terms):
            combine((src, first, a), terms, w)
            send(
                (name, k), src.at[first : first + CHIP, a : a + w], dst.at[first : first + CHIP, a : a + w], device
            )

        def rb2p():
            hand("rb2p", SB2, RB2, 0, yp, [(PF, block(0, 2), CA + a)])

        def rb2m():
            hand("rb2m", SB2, RB2, CHIP, ym, [(PF, block(1, 2), CA + a)])

        def rbf01():
            hand("rbf01", SBF, RBF, CHIP, yp, [(PF, block(1, 1), CA + a)])

        def rbf10():
            hand("rbf10", SBF, RBF, 2 * CHIP, ym, [(PF, block(0, 3), CA + a)])

        def rbf00():
            recv(("rb2p", k))
            hand("rbf00", SBF, RBF, 0, yp, [(PF, block(0, 1), CA + a), (RB2, 0, a)])

        def rbf11():
            recv(("rb2m", k))
            hand("rbf11", SBF, RBF, 3 * CHIP, ym, [(PF, block(1, 3), CA + a), (RB2, CHIP, a)])

        def rbx():
            recv(("rbf00", k), ("rbf10", k))
            hand(
                "rbx", SBX, RBX, 0, pair,
                [(PF, block(0, 0), CA + a), (RBF, 0, a), (RBF, 2 * CHIP, a), (XRES, 0, CA + a)],
            )

        def fin_b():
            recv(("rbf01", k), ("rbf11", k), ("rbx", k))
            combine((OB, 0, a), [(PF, block(1, 0), CA + a), (RBF, CHIP, a), (RBF, 3 * CHIP, a), (RBX, 0, a)], w)
            deliver(OB, a, w, CA)

        tasks.extend((rb2p, rb2m, rbf01, rbf10, rbf00, rbf11, rbx, fin_b))

    for k in range(len(SUB_A)):
        reduce_a(k)
    for k in range(len(SUB_B)):
        reduce_b(k)

    def dh_task(blocks, wanted):
        def run():
            recv(*wanted)
            first, second = (pl.ds(block(r, d), CHIP) for r, d in blocks)
            DH[first, :] = jnp.zeros((CHIP, WIDTH), F32)
            DH[second, :] = jnp.zeros((CHIP, WIDTH), F32)

            def step(j, carry):
                here = pl.ds(pl.multiple_of(j * 1024, 1024), 1024)
                part = lax.dot_general(
                    jnp.concatenate([G[first, here], G[second, here]], axis=0),
                    W[:, here],
                    (((1,), (1,)), ((), ())),
                    preferred_element_type=F32,
                )
                DH[first, :] += part[0:CHIP]
                DH[second, :] += part[CHIP : 2 * CHIP]
                return carry

            lax.fori_loop(0, D // 1024, step, 0)

        tasks.append(run)

    dh_task(((0, 0), (1, 0)), ("g_rest", (True, 1, 0), (False, 1, 0)))
    dh_task(((0, 1), (0, 3)), ((True, 0, 3), (True, 0, 1), (False, 0, 3), (False, 0, 1)))
    dh_task(((1, 1), (1, 3)), ((True, 1, 3), (True, 1, 1), (False, 1, 3), (False, 1, 1)))
    dh_task(((0, 2), (1, 2)), ((True, 0, 2), (True, 1, 2), (False, 0, 2), (False, 1, 2)))

    def local_copy(i, src, dst):
        copy = pltpu.make_async_copy(src, dst, local_sem.at[i])
        copy.start()
        return copy

    kept = {}

    @task
    def s_sib():
        for e in (1, 3, 2, 0):
            for r in range(2):
                recv(("s", r, e), ("q", r, e))
        send("s_sib", SR.at[:, :, columns((1 - c) * WIDTH, WIDTH)], SF.at[:, own_rows, :], sib)
        send("q_sib", QR, QF.at[:, c], sib)
        kept["s"] = local_copy(7, SR.at[:, :, columns(c * WIDTH, WIDTH)], SF.at[:, own_rows, :])
        kept["q"] = local_copy(8, QR, QF.at[:, c])

    def chip_of(b):
        return ((y + b % 4) % 4) * 2 + (xl + b // 4) % 2

    def add_sums(blocks):
        lane = lax.broadcasted_iota(jnp.int32, (CHIP, 128), 1)
        for b in blocks:
            grad = DH[b * CHIP : (b + 1) * CHIP, :]
            normed = SF[b].astype(F32)
            gg_ref[...] += jnp.sum(grad * normed, axis=0, keepdims=True)
            scaled = grad.astype(BF).astype(F32) * scale
            first = jnp.sum(scaled, axis=1, keepdims=True)
            second = jnp.sum(scaled * normed, axis=1, keepdims=True)
            place = 2 * chip_of(b)
            EC[0:CHIP, :] += jnp.where(lane == place, first, 0.0) + jnp.where(lane == place + 1, second, 0.0)

    @task
    def sums_a():
        recv("s_sib", "q_sib")
        kept["s"].wait()
        kept["q"].wait()
        EC[...] = jnp.zeros(EC.shape, F32)
        gg_ref[...] = jnp.zeros(gg_ref.shape, F32)
        add_sums((0, 4, 1, 3, 5, 7))

    @task
    def sums_b():
        add_sums((2, 6))
        ES[...] = EC[...].T[0:16, :].astype(BF)
        pltpu.make_async_copy(ES, ER.at[c], group_sem.at[E_IN]).start()
        for e in (2, 1, 3, 0):
            for r in range(2):
                grouped(ES, ER.at[from_here(e, r) * 2 + c], E_OUT, E_IN, at(s, e, row(r), 1 - c))
                if (e, r) != (0, 0):
                    grouped(ES, ER.at[from_here(e, r) * 2 + c], E_OUT, E_IN, at(s, e, row(r), c))

    @task
    def gi():
        arrived(ER, group_sem.at[E_IN], group_sem.at[E_OUT])
        total = ER[0].astype(F32)
        for k in range(1, 16):
            total = total + ER[k].astype(F32)
        QC[0:16, :] = total * (1.0 / D)
        EC[...] = jnp.zeros(EC.shape, F32)
        for b in range(8):
            EC[2 * b : 2 * b + 2, :] = QC[pl.ds(2 * chip_of(b), 2), :]
        MT[...] = EC[...].T
        QC[...] = jnp.zeros(QC.shape, F32)
        for b in range(8):
            for core in range(2):
                QC[b * 2 + core : b * 2 + core + 1, :] = QF[b, core, 0:1, :]
        RT[...] = QC[...].T

    def p_task(e, r):
        def run():
            b = r * 4 + e
            for core in range(2):
                k = b * 2 + core
                part = slice(core * ROWS, (core + 1) * ROWS)
                rows = slice(k * ROWS, (k + 1) * ROWS)
                mean_e = MT[part, 2 * b : 2 * b + 1]
                mean_en = MT[part, 2 * b + 1 : 2 * b + 2]
                recip = RT[0:ROWS, k : k + 1]
                scaled = DH[rows, :].astype(BF).astype(F32) * scale
                inner = scaled - mean_e - SF[b, part, :].astype(F32) * mean_en
                upstream = G[rows, columns(t * WIDTH, WIDTH)].astype(F32)
                GI[b, part, :] = (upstream + recip * inner).astype(BF)
                grouped(
                    GI.at[b, part, :],
                    prev_ref.at[:, columns(t * WIDTH, WIDTH)],
                    P_OUT,
                    P_IN,
                    at(previous, e, row(r), core),
                )

        tasks.append(run)

    for e in range(4):
        for r in range(2):
            p_task(e, r)

    @task
    def bht():
        BHT[...] = (SF[...].reshape(TOKENS, WIDTH).astype(F32) * scale).T.astype(BF)

    def wg_task(i):
        def run():
            def step(j, carry):
                here = pl.ds(pl.multiple_of(j * 256, 256), 256)
                wg_ref[:, here] = jnp.dot(BHT[...], G[:, here], preferred_element_type=F32).astype(BF)
                return carry

            lax.fori_loop(i * 6, (i + 1) * 6, step, 0)

        tasks.append(run)

    for i in range(4):
        wg_task(i)

    for i in ORDER:
        tasks[i]()

    for copy in sent:
        copy.wait_send()
    left(ER.at[0:15], group_sem.at[E_OUT], group_sem.at[E_IN])
    left(next_ref, group_sem.at[N_OUT], group_sem.at[N_IN])
    left(prev_ref, group_sem.at[P_OUT], group_sem.at[P_IN])
    arrived(prev_ref, group_sem.at[P_IN], group_sem.at[P_OUT])
    arrived(next_ref, group_sem.at[N_IN], group_sem.at[N_OUT])


def local(forward_in, grad_out, saved_in, weight, gain):
    anywhere = pl.BlockSpec(memory_space=pl.ANY)
    vmem = pl.BlockSpec(memory_space=pltpu.VMEM)
    v = pltpu.VMEM
    out_shape = (
        jax.ShapeDtypeStruct((ROWS, D), BF),
        jax.ShapeDtypeStruct((ROWS, D), BF),
        jax.ShapeDtypeStruct((WIDTH, D), BF),
        jax.ShapeDtypeStruct((1, WIDTH), F32),
    )
    next_input, prev_grad, weight_grad, gain_grad = pl.pallas_call(
        kernel,
        out_shape=tuple(v(out.shape, out.dtype) for out in out_shape),
        in_specs=[anywhere, anywhere, anywhere, anywhere, vmem],
        out_specs=(vmem,) * 4,
        scratch_shapes=[
            v((TOKENS, D), BF),
            v((WIDTH, D), BF),
            v((PAIRED, HALF), BF),
            v((TOKENS, HALF), F32),
            v((8, CHIP, PAIRED), BF),
            v((8, ROWS, PAIRED), BF),
            v((ROWS, D), BF),
            v((ROWS, D), BF),
            v((ROWS, D), BF),
            v((ROWS, D), BF),
            v((8, ROWS, PAIRED), BF),
            v((8, CHIP, WIDTH), BF),
            v((WIDTH, TOKENS), BF),
            v((TOKENS, WIDTH), F32),
            v((8, CHIP, WIDTH), BF),
            v((CHIP, HALF), BF),
            v((8, PAIRED), F32),
            v((4 * CHIP, CA), BF),
            v((4 * CHIP, CA), BF),
            v((CHIP, CA), BF),
            v((CHIP, CA), BF),
            v((2 * CHIP, CA), BF),
            v((2 * CHIP, CA), BF),
            v((2 * CHIP, CB), BF),
            v((2 * CHIP, CB), BF),
            v((4 * CHIP, CB), BF),
            v((4 * CHIP, CB), BF),
            v((CHIP, CB), BF),
            v((CHIP, CB), BF),
            v((CHIP, CA), BF),
            v((CHIP, CB), BF),
            v((128, 128), F32),
            v((8, 128), F32),
            v((8, 8, 128), F32),
            v((8, 2, 8, 128), F32),
            v((128, 128), F32),
            v((16, 128), BF),
            v((16, 16, 128), BF),
            v((128, 128), F32),
            v((128, 128), F32),
            pltpu.SemaphoreType.DMA((128,)),
            pltpu.SemaphoreType.DMA((128,)),
            pltpu.SemaphoreType.DMA((9,)),
            pltpu.SemaphoreType.DMA((6,)),
            pltpu.SemaphoreType.REGULAR((ROUNDS,)),
        ],
        compiler_params=pltpu.CompilerParams(
            collective_id=0, has_side_effects=True, vmem_limit_bytes=54 * 2**20
        ),
        cost_estimate=pl.CostEstimate(
            flops=6 * TOKENS * WIDTH * D, bytes_accessed=20 * 2**20, transcendentals=0
        ),
    )(forward_in[0], grad_out[0], saved_in[0], weight[0], gain)
    return next_input[None], prev_grad[None], weight_grad[None], gain_grad


def solution(mesh):
    rows = P("section", "tensor", None)
    return jax.shard_map(
        local,
        mesh=mesh,
        in_specs=(rows, rows, rows, rows, P("section", "tensor")),
        out_specs=(rows, rows, rows, P("section", "tensor")),
        check_vma=False,
    )
```

```python
import jax
import jax.numpy as jnp
from jax import lax
from jax.experimental import pallas as pl
from jax.experimental.pallas import tpu as pltpu
from jax.sharding import PartitionSpec as P

D = 6144
TOKENS = 768
ROWS = 48
CHIP = 96
WIDTH = 384
PAIRED = 2 * WIDTH
HALF = D // 2
GA = 1408
GB = HALF - GA
CA = 1280
CB = HALF - CA
SUB_A = ((0, 512), (512, 512), (1024, 256))
SUB_B = ((0, 1024), (1024, 512), (1536, 256))
ORDER = (
    6, 0, 9, 23, 1, 7, 10, 8, 19, 2,
    21, 17, 13, 25, 3, 15, 26, 28, 20, 40,
    4, 11, 32, 34, 22, 24, 27, 41, 12, 29,
    5, 33, 42, 45, 30, 74, 75, 16, 31, 18,
    43, 98, 14, 46, 47, 35, 36, 99, 38, 77,
    78, 100, 79, 49, 66, 56, 37, 76, 48, 39,
    102, 93, 68, 80, 101, 103, 104, 58, 82, 85,
    55, 81, 65, 90, 51, 91, 50, 105, 67, 110,
    109, 57, 52, 113, 114, 106, 94, 107, 69, 70,
    71, 83, 72, 111, 86, 44, 64, 59, 60, 54,
    117, 61, 53, 62, 108, 88, 84, 95, 87, 73,
    63, 96, 92, 112, 118, 89, 97, 115, 116,
)
STRIP = 16
ROUNDS = 5
BF = jnp.bfloat16
F32 = jnp.float32
EPS = 1e-05
MESH = pl.DeviceIdType.MESH


def block(r, d):
    return (r * 4 + d) * CHIP


def normalize(values):
    center = jnp.mean(values, axis=1, keepdims=True)
    shifted = values - center
    recip = lax.rsqrt(jnp.mean(shifted * shifted, axis=1, keepdims=True) + EPS)
    return shifted * recip, recip


def strips(rows, body):
    def step(i, carry):
        body(pl.ds(pl.multiple_of(i * STRIP, STRIP), STRIP), i)
        return carry

    lax.fori_loop(0, rows // STRIP, step, 0)


def columns(start, width):
    return pl.ds(pl.multiple_of(start, 128), width)


def kernel(
    x_ref, g_ref, s_ref, w_ref, gain_ref,
    next_ref, prev_ref, wg_ref, gg_ref,
    G, W, WC, PF, HN, XR, XO, NX, SO, NS, SR, SF, BHT, DH, GI, XRES, GS,
    SA, RA, SA2, RA2, SAF, RAF, SB2, RB2, SBF, RBF, SBX, RBX, OA, OB,
    QC, QS, QR, QF, EC, ES, ER, MT, RT,
    send_sem, recv_sem, local_sem, group_sem, heard,
):
    s = lax.axis_index("section")
    t = lax.axis_index("tensor")
    y, xl, c = t // 4, (t // 2) % 2, t % 2
    mirrored, following, previous = 7 - s, (s + 1) % 8, (s + 7) % 8

    def at(section, along_y, row, core):
        return (section, ((y + along_y) % 4) * 4 + row * 2 + core)

    def row(r):
        return xl if r == 0 else 1 - xl

    sib = at(s, 0, xl, 1 - c)
    yp, ym = at(s, 1, xl, c), at(s, 3, xl, c)
    pair = at(s, 0, 1 - xl, c)

    mine = c * HALF
    other = (1 - c) * HALF
    cols_a = columns(mine, GA)
    cols_b = columns(mine + GA, GB)
    own_rows = pl.ds(pl.multiple_of(c * ROWS, 16), ROWS)
    sib_rows = pl.ds(pl.multiple_of((1 - c) * ROWS, 16), ROWS)

    names = {}
    sent = []

    def send(name, src, dst, device):
        i = names.setdefault(name, (len(names), dst))[0]
        copy = pltpu.make_async_remote_copy(
            src_ref=src, dst_ref=dst, send_sem=send_sem.at[i], recv_sem=recv_sem.at[i],
            device_id=device, device_id_type=MESH,
        )
        copy.start()
        sent.append(copy)

    def arrived(ref, sem, scratch_sem):
        pltpu.make_async_remote_copy(
            src_ref=ref, dst_ref=ref, send_sem=scratch_sem, recv_sem=sem, device_id=sib, device_id_type=MESH
        ).wait_recv()

    def left(ref, sem, scratch_sem):
        pltpu.make_async_remote_copy(
            src_ref=ref, dst_ref=ref, send_sem=sem, recv_sem=scratch_sem, device_id=sib, device_id_type=MESH
        ).wait_send()

    def recv(*wanted):
        for name in wanted:
            i, landing = names[name]
            arrived(landing, recv_sem.at[i], send_sem.at[i])

    E_IN, E_OUT, P_IN, P_OUT, N_IN, N_OUT = range(6)

    def grouped(src, dst, out, into, device):
        pltpu.make_async_remote_copy(
            src_ref=src, dst_ref=dst, send_sem=group_sem.at[out], recv_sem=group_sem.at[into],
            device_id=device, device_id_type=MESH,
        ).start()

    barrier = pltpu.get_barrier_semaphore()
    across = at(s + 1 - 2 * (s % 2), 0, 1 - xl, c)
    nearest = [sib, yp, ym, pair, across, at((s + 2) % 8, 0, xl, c), at((s + 6) % 8, 0, xl, c)]
    for friend in nearest:
        pl.semaphore_signal(barrier, inc=1, device_id=friend, device_id_type=MESH)

    load_x = pltpu.make_async_copy(x_ref, XO, local_sem.at[0])
    load_g = pltpu.make_async_copy(g_ref, G.at[own_rows, :], local_sem.at[1])
    load_s = pltpu.make_async_copy(s_ref, SO, local_sem.at[2])
    load_w = pltpu.make_async_copy(w_ref, W, local_sem.at[3])
    weight_rows = pl.ds(pl.multiple_of(c * WIDTH, 128), WIDTH)
    load_wc = pltpu.make_async_copy(w_ref.at[:, columns(mine, HALF)], WC.at[weight_rows, :], local_sem.at[4])
    load_xres = pltpu.make_async_copy(x_ref.at[:, columns(mine, HALF)], XRES.at[own_rows, :], local_sem.at[5])
    for load in (load_x, load_g, load_s, load_wc, load_xres, load_w):
        load.start()
    scale = gain_ref[...].astype(F32)
    GS[:, columns(c * WIDTH, WIDTH)] = jnp.broadcast_to(scale, (8, WIDTH))

    pl.semaphore_wait(barrier, len(nearest))

    def own(cols, r=0, d=0, first=0, rows=CHIP):
        return G.at[block(r, d) + first : block(r, d) + first + rows, cols]

    def near(cols, rows, r, d):
        return G.at[pl.ds(pl.multiple_of(block(r, d) + rows.start, 16), ROWS), cols]

    def from_here(e, r):
        return r * 4 + (4 - e) % 4

    tasks = []

    def task(run):
        tasks.append(run)
        return run

    def round_task(i):
        def run():
            if i > 1:
                pl.semaphore_wait(heard.at[i - 2], len(nearest))
            if i <= ROUNDS:
                for friend in nearest:
                    pl.semaphore_signal(heard.at[i - 1], inc=1, device_id=friend, device_id_type=MESH)

        tasks.append(run)

    for i in range(1, ROUNDS + 2):
        round_task(i)

    def first_step(part, a, b):
        send(("b_x", part), b[0], near(cols_b, b[1], 1, 0), pair)
        send(("a_p", part), a[0], near(cols_a, a[1], 0, 3), yp)
        send(("a_m", part), a[0], near(cols_a, a[1], 0, 1), ym)
        send(("b_p", part), b[0], near(cols_b, b[1], 0, 3), yp)
        send(("b_m", part), b[0], near(cols_b, b[1], 0, 1), ym)
        send(("a_x0", part), a[0], near(cols_a, a[1], 1, 0), pair)

    @task
    def first_o():
        send("g_half", g_ref.at[:, columns(other, HALF)], G.at[own_rows, columns(other, HALF)], sib)
        first_step(0, (g_ref.at[:, cols_a], own_rows), (g_ref.at[:, cols_b], own_rows))

    @task
    def first_s():
        recv("g_half")
        first_step(1, (G.at[sib_rows, cols_a], sib_rows), (G.at[sib_rows, cols_b], sib_rows))

    @task
    def inchip():
        send("gain", GS.at[:, columns(c * WIDTH, WIDTH)], GS.at[:, columns(c * WIDTH, WIDTH)], sib)
        send("w_half", w_ref.at[:, columns(other, HALF)], WC.at[weight_rows, :], sib)
        send("x_half", x_ref.at[:, columns(other, HALF)], XRES.at[own_rows, :], sib)
        send("g_rest", g_ref.at[:, columns(mine, HALF)], G.at[own_rows, columns(mine, HALF)], sib)

    @task
    def norm_x():
        load_x.wait()

        def body(rows, i):
            NX[rows, :] = normalize(XO[rows, :].astype(F32))[0].astype(BF)

        strips(ROWS, body)

    def features(e, r):
        return columns((((y + e) % 4) * 2 + row(r)) * PAIRED, PAIRED)

    def x_task(e, r):
        def run():
            send(("x", r, e), NX.at[:, features(e, r)], XR.at[from_here(e, r)], at(s, e, row(r), c))

        tasks.append(run)

    @task
    def norm_s():
        load_s.wait()
        QC[...] = jnp.zeros(QC.shape, F32)

        def body(rows, i):
            normed, recip = normalize(SO[rows, :].astype(F32))
            NS[rows, :] = normed.astype(BF)
            QC[rows, :] = jnp.broadcast_to(recip, (STRIP, 128))

        strips(ROWS, body)
        QS[...] = QC[...].T[0:1, :]

    def s_task(e, r):
        def run():
            target = at(mirrored, e, row(r), c)
            send(("s", r, e), NS.at[:, features(e, r)], SR.at[from_here(e, r)], target)
            send(("q", r, e), QS, QR.at[from_here(e, r)], target)

        tasks.append(run)

    for e in range(4):
        for r in range(2):
            s_task(e, r)
            if (e, r) != (0, 0):
                x_task(e, r)

    def share(cols, r, d):
        ref = own(cols, r, d)
        send((cols is cols_a, r, d), ref, ref, sib)

    def halves(name):
        return (name, 0), (name, 1)

    @task
    def bx():
        recv(*halves("b_x"))
        send("bx_p", own(cols_b, 1, 0), own(cols_b, 1, 3), yp)
        send("bx_m", own(cols_b, 1, 0), own(cols_b, 1, 1), ym)
        share(cols_b, 1, 0)

    @task
    def ap():
        recv(*halves("a_p"))
        send("a_pp", own(cols_a, 0, 3, 0, ROWS), own(cols_a, 0, 2, 0, ROWS), yp)
        send("a_x3", own(cols_a, 0, 3), own(cols_a, 1, 3), pair)
        share(cols_a, 0, 3)

    @task
    def am():
        recv(*halves("a_m"))
        send("a_mm", own(cols_a, 0, 1, ROWS, ROWS), own(cols_a, 0, 2, ROWS, ROWS), ym)
        send("a_x1", own(cols_a, 0, 1), own(cols_a, 1, 1), pair)
        share(cols_a, 0, 1)

    @task
    def bp():
        recv(*halves("b_p"))
        send("b_pp", own(cols_b, 0, 3), own(cols_b, 0, 2), yp)
        share(cols_b, 0, 3)

    @task
    def bxm():
        recv("bx_m")
        send("bx_mm", own(cols_b, 1, 1), own(cols_b, 1, 2), ym)
        share(cols_b, 1, 1)

    @task
    def ax2():
        recv("a_pp", "a_mm")
        send("a_x2", own(cols_a, 0, 2), own(cols_a, 1, 2), pair)
        share(cols_a, 0, 2)

    def keep_task(wanted, cols, r, d):
        def run():
            recv(*wanted)
            share(cols, r, d)

        tasks.append(run)

    keep_task(halves("b_m"), cols_b, 0, 1)
    keep_task(("bx_p",), cols_b, 1, 3)
    keep_task(halves("a_x0"), cols_a, 1, 0)
    keep_task(("a_x3",), cols_a, 1, 3)
    keep_task(("a_x1",), cols_a, 1, 1)
    keep_task(("b_pp",), cols_b, 0, 2)
    keep_task(("bx_mm",), cols_b, 1, 2)
    keep_task(("a_x2",), cols_a, 1, 2)

    @task
    def hidden():
        load_g.wait()
        load_w.wait()
        recv("gain")
        both = GS[0:1, :]
        for d in (0, 3, 1, 2):
            for r in range(2):
                if (d, r) == (0, 0):
                    values = NX[:, features(0, 0)]
                else:
                    recv(("x", r, (4 - d) % 4))
                    values = XR[r * 4 + d]
                HN[r * 4 + d, own_rows, :] = (values.astype(F32) * both).astype(BF)
        send("hid", HN.at[:, own_rows, :], HN.at[:, own_rows, :], sib)

    def project(first, chips, start, width, store):
        def tile(i, carry):
            here = pl.multiple_of(i * 256, 256)
            there = pl.ds(pl.multiple_of(start + here, 256), 256)
            store(
                pl.ds(here, 256),
                there,
                jnp.dot(
                    HN[first : first + chips].reshape(chips * CHIP, PAIRED),
                    WC[:, there],
                    preferred_element_type=F32,
                ),
            )
            return carry

        lax.fori_loop(0, width // 256, tile, 0)

    @task
    def proj_a():
        load_wc.wait()
        load_xres.wait()
        recv("hid", "w_half", "x_half")

        def store(here, there, value):
            SA[0:CHIP, here] = (value[0:CHIP] + XRES[:, here].astype(F32)).astype(BF)
            SA[CHIP : 4 * CHIP, here] = value[CHIP : 4 * CHIP].astype(BF)

        project(0, 4, 0, CA, store)

    @task
    def proj_b():
        def store(here, there, value):
            PF[:, there] = value

        project(0, 8, CA, CB, store)

    @task
    def proj_c():
        def store(here, there, value):
            PF[4 * CHIP : 8 * CHIP, here] = value

        project(4, 4, 0, CA, store)

    def combine(dst, terms, width, first=0, rows=CHIP):
        def body(strip, i):
            total = None
            for ref, base, start in terms:
                here = pl.ds(pl.multiple_of(base + first + i * STRIP, STRIP), STRIP)
                value = ref[here, start : start + width].astype(F32)
                total = value if total is None else total + value
            ref, base, start = dst
            ref[pl.ds(pl.multiple_of(base + first + i * STRIP, STRIP), STRIP), start : start + width] = total.astype(BF)

        strips(rows, body)

    def deliver(src, start, width, offset):
        for core in range(2):
            grouped(
                src.at[core * ROWS : (core + 1) * ROWS, start : start + width],
                next_ref.at[:, columns(mine + offset + start, width)],
                N_OUT,
                N_IN,
                at(following, 0, 1 - xl, core),
            )

    def reduce_a(k):
        a, w = SUB_A[k]

        def pass_on(name, src, dst, first, rows, device):
            send(
                (name, k), src.at[first : first + rows, a : a + w], dst.at[first : first + rows, a : a + w], device
            )

        def cross(d):
            def run():
                pass_on(d, SA, RA, d * CHIP, CHIP, pair)

            tasks.append(run)

        for d in range(4):
            cross(d)

        def a2():
            recv((2, k))
            combine((SA2, 0, a), [(PF, block(1, 2), a), (RA, 2 * CHIP, a)], w)
            pass_on("ra2p", SA2, RA2, 0, ROWS, yp)
            pass_on("ra2m", SA2, RA2, ROWS, ROWS, ym)

        def a1():
            recv((1, k))
            combine((SAF, 0, a), [(PF, block(1, 1), a), (RA, CHIP, a)], w, ROWS, ROWS)
            pass_on("rafp1", SAF, RAF, ROWS, ROWS, yp)

        def a3():
            recv((3, k))
            combine((SAF, CHIP, a), [(PF, block(1, 3), a), (RA, 3 * CHIP, a)], w, 0, ROWS)
            pass_on("rafm0", SAF, RAF, CHIP, ROWS, ym)

        def a2p():
            recv(("ra2p", k))
            combine((SAF, 0, a), [(PF, block(1, 1), a), (RA, CHIP, a), (RA2, 0, a)], w, 0, ROWS)
            pass_on("rafp0", SAF, RAF, 0, ROWS, yp)

        def a2m():
            recv(("ra2m", k))
            combine((SAF, CHIP, a), [(PF, block(1, 3), a), (RA, 3 * CHIP, a), (RA2, 0, a)], w, ROWS, ROWS)
            pass_on("rafm1", SAF, RAF, CHIP + ROWS, ROWS, ym)

        def fin_a():
            for name in (0, "rafp0", "rafp1", "rafm0", "rafm1"):
                recv((name, k))
            combine((OA, 0, a), [(PF, block(1, 0), a), (RA, 0, a), (RAF, 0, a), (RAF, CHIP, a)], w)
            deliver(OA, a, w, 0)

        tasks.extend((a2, a1, a3, a2p, a2m, fin_a))

    def reduce_b(k):
        a, w = SUB_B[k]

        def hand(name, src, dst, first, device, terms):
            combine((src, first, a), terms, w)
            send(
                (name, k), src.at[first : first + CHIP, a : a + w], dst.at[first : first + CHIP, a : a + w], device
            )

        def rb2p():
            hand("rb2p", SB2, RB2, 0, yp, [(PF, block(0, 2), CA + a)])

        def rb2m():
            hand("rb2m", SB2, RB2, CHIP, ym, [(PF, block(1, 2), CA + a)])

        def rbf01():
            hand("rbf01", SBF, RBF, CHIP, yp, [(PF, block(1, 1), CA + a)])

        def rbf10():
            hand("rbf10", SBF, RBF, 2 * CHIP, ym, [(PF, block(0, 3), CA + a)])

        def rbf00():
            recv(("rb2p", k))
            hand("rbf00", SBF, RBF, 0, yp, [(PF, block(0, 1), CA + a), (RB2, 0, a)])

        def rbf11():
            recv(("rb2m", k))
            hand("rbf11", SBF, RBF, 3 * CHIP, ym, [(PF, block(1, 3), CA + a), (RB2, CHIP, a)])

        def rbx():
            recv(("rbf00", k), ("rbf10", k))
            hand(
                "rbx", SBX, RBX, 0, pair,
                [(PF, block(0, 0), CA + a), (RBF, 0, a), (RBF, 2 * CHIP, a), (XRES, 0, CA + a)],
            )

        def fin_b():
            recv(("rbf01", k), ("rbf11", k), ("rbx", k))
            combine((OB, 0, a), [(PF, block(1, 0), CA + a), (RBF, CHIP, a), (RBF, 3 * CHIP, a), (RBX, 0, a)], w)
            deliver(OB, a, w, CA)

        tasks.extend((rb2p, rb2m, rbf01, rbf10, rbf00, rbf11, rbx, fin_b))

    for k in range(len(SUB_A)):
        reduce_a(k)
    for k in range(len(SUB_B)):
        reduce_b(k)

    def dh_task(blocks, wanted):
        def run():
            recv(*wanted)
            first, second = (pl.ds(block(r, d), CHIP) for r, d in blocks)
            DH[first, :] = jnp.zeros((CHIP, WIDTH), F32)
            DH[second, :] = jnp.zeros((CHIP, WIDTH), F32)

            def step(j, carry):
                here = pl.ds(pl.multiple_of(j * 1024, 1024), 1024)
                part = lax.dot_general(
                    jnp.concatenate([G[first, here], G[second, here]], axis=0),
                    W[:, here],
                    (((1,), (1,)), ((), ())),
                    preferred_element_type=F32,
                )
                DH[first, :] += part[0:CHIP]
                DH[second, :] += part[CHIP : 2 * CHIP]
                return carry

            lax.fori_loop(0, D // 1024, step, 0)

        tasks.append(run)

    dh_task(((0, 0), (1, 0)), ("g_rest", (True, 1, 0), (False, 1, 0)))
    dh_task(((0, 1), (0, 3)), ((True, 0, 3), (True, 0, 1), (False, 0, 3), (False, 0, 1)))
    dh_task(((1, 1), (1, 3)), ((True, 1, 3), (True, 1, 1), (False, 1, 3), (False, 1, 1)))
    dh_task(((0, 2), (1, 2)), ((True, 0, 2), (True, 1, 2), (False, 0, 2), (False, 1, 2)))

    def local_copy(i, src, dst):
        copy = pltpu.make_async_copy(src, dst, local_sem.at[i])
        copy.start()
        return copy

    kept = {}

    @task
    def s_sib():
        for e in (1, 3, 2, 0):
            for r in range(2):
                recv(("s", r, e), ("q", r, e))
        send("s_sib", SR.at[:, :, columns((1 - c) * WIDTH, WIDTH)], SF.at[:, own_rows, :], sib)
        send("q_sib", QR, QF.at[:, c], sib)
        kept["s"] = local_copy(7, SR.at[:, :, columns(c * WIDTH, WIDTH)], SF.at[:, own_rows, :])
        kept["q"] = local_copy(8, QR, QF.at[:, c])

    def chip_of(b):
        return ((y + b % 4) % 4) * 2 + (xl + b // 4) % 2

    def add_sums(blocks):
        lane = lax.broadcasted_iota(jnp.int32, (CHIP, 128), 1)
        for b in blocks:
            grad = DH[b * CHIP : (b + 1) * CHIP, :]
            normed = SF[b].astype(F32)
            gg_ref[...] += jnp.sum(grad * normed, axis=0, keepdims=True)
            scaled = grad.astype(BF).astype(F32) * scale
            first = jnp.sum(scaled, axis=1, keepdims=True)
            second = jnp.sum(scaled * normed, axis=1, keepdims=True)
            place = 2 * chip_of(b)
            EC[0:CHIP, :] += jnp.where(lane == place, first, 0.0) + jnp.where(lane == place + 1, second, 0.0)

    @task
    def sums_a():
        recv("s_sib", "q_sib")
        kept["s"].wait()
        kept["q"].wait()
        EC[...] = jnp.zeros(EC.shape, F32)
        gg_ref[...] = jnp.zeros(gg_ref.shape, F32)
        add_sums((0, 4, 1, 3, 5, 7))

    @task
    def sums_b():
        add_sums((2, 6))
        ES[...] = EC[...].T[0:16, :].astype(BF)
        pltpu.make_async_copy(ES, ER.at[c], group_sem.at[E_IN]).start()
        for e in (2, 1, 3, 0):
            for r in range(2):
                grouped(ES, ER.at[from_here(e, r) * 2 + c], E_OUT, E_IN, at(s, e, row(r), 1 - c))
                if (e, r) != (0, 0):
                    grouped(ES, ER.at[from_here(e, r) * 2 + c], E_OUT, E_IN, at(s, e, row(r), c))

    @task
    def gi():
        arrived(ER, group_sem.at[E_IN], group_sem.at[E_OUT])
        total = ER[0].astype(F32)
        for k in range(1, 16):
            total = total + ER[k].astype(F32)
        QC[0:16, :] = total * (1.0 / D)
        EC[...] = jnp.zeros(EC.shape, F32)
        for b in range(8):
            EC[2 * b : 2 * b + 2, :] = QC[pl.ds(2 * chip_of(b), 2), :]
        MT[...] = EC[...].T
        QC[...] = jnp.zeros(QC.shape, F32)
        for b in range(8):
            for core in range(2):
                QC[b * 2 + core : b * 2 + core + 1, :] = QF[b, core, 0:1, :]
        RT[...] = QC[...].T

    def p_task(e, r):
        def run():
            b = r * 4 + e
            for core in range(2):
                k = b * 2 + core
                part = slice(core * ROWS, (core + 1) * ROWS)
                rows = slice(k * ROWS, (k + 1) * ROWS)
                mean_e = MT[part, 2 * b : 2 * b + 1]
                mean_en = MT[part, 2 * b + 1 : 2 * b + 2]
                recip = RT[0:ROWS, k : k + 1]
                scaled = DH[rows, :].astype(BF).astype(F32) * scale
                inner = scaled - mean_e - SF[b, part, :].astype(F32) * mean_en
                upstream = G[rows, columns(t * WIDTH, WIDTH)].astype(F32)
                GI[b, part, :] = (upstream + recip * inner).astype(BF)
                grouped(
                    GI.at[b, part, :],
                    prev_ref.at[:, columns(t * WIDTH, WIDTH)],
                    P_OUT,
                    P_IN,
                    at(previous, e, row(r), core),
                )

        tasks.append(run)

    for e in range(4):
        for r in range(2):
            p_task(e, r)

    @task
    def bht():
        BHT[...] = (SF[...].reshape(TOKENS, WIDTH).astype(F32) * scale).T.astype(BF)

    def wg_task(i):
        def run():
            def step(j, carry):
                here = pl.ds(pl.multiple_of(j * 256, 256), 256)
                wg_ref[:, here] = jnp.dot(BHT[...], G[:, here], preferred_element_type=F32).astype(BF)
                return carry

            lax.fori_loop(i * 6, (i + 1) * 6, step, 0)

        tasks.append(run)

    for i in range(4):
        wg_task(i)

    for i in ORDER:
        tasks[i]()

    for copy in sent:
        copy.wait_send()
    left(ER.at[0:15], group_sem.at[E_OUT], group_sem.at[E_IN])
    left(next_ref, group_sem.at[N_OUT], group_sem.at[N_IN])
    left(prev_ref, group_sem.at[P_OUT], group_sem.at[P_IN])
    arrived(prev_ref, group_sem.at[P_IN], group_sem.at[P_OUT])
    arrived(next_ref, group_sem.at[N_IN], group_sem.at[N_OUT])


def local(forward_in, grad_out, saved_in, weight, gain):
    anywhere = pl.BlockSpec(memory_space=pl.ANY)
    vmem = pl.BlockSpec(memory_space=pltpu.VMEM)
    v = pltpu.VMEM
    out_shape = (
        jax.ShapeDtypeStruct((ROWS, D), BF),
        jax.ShapeDtypeStruct((ROWS, D), BF),
        jax.ShapeDtypeStruct((WIDTH, D), BF),
        jax.ShapeDtypeStruct((1, WIDTH), F32),
    )
    next_input, prev_grad, weight_grad, gain_grad = pl.pallas_call(
        kernel,
        out_shape=tuple(v(out.shape, out.dtype) for out in out_shape),
        in_specs=[anywhere, anywhere, anywhere, anywhere, vmem],
        out_specs=(vmem,) * 4,
        scratch_shapes=[
            v((TOKENS, D), BF),
            v((WIDTH, D), BF),
            v((PAIRED, HALF), BF),
            v((TOKENS, HALF), F32),
            v((8, CHIP, PAIRED), BF),
            v((8, ROWS, PAIRED), BF),
            v((ROWS, D), BF),
            v((ROWS, D), BF),
            v((ROWS, D), BF),
            v((ROWS, D), BF),
            v((8, ROWS, PAIRED), BF),
            v((8, CHIP, WIDTH), BF),
            v((WIDTH, TOKENS), BF),
            v((TOKENS, WIDTH), F32),
            v((8, CHIP, WIDTH), BF),
            v((CHIP, HALF), BF),
            v((8, PAIRED), F32),
            v((4 * CHIP, CA), BF),
            v((4 * CHIP, CA), BF),
            v((CHIP, CA), BF),
            v((CHIP, CA), BF),
            v((2 * CHIP, CA), BF),
            v((2 * CHIP, CA), BF),
            v((2 * CHIP, CB), BF),
            v((2 * CHIP, CB), BF),
            v((4 * CHIP, CB), BF),
            v((4 * CHIP, CB), BF),
            v((CHIP, CB), BF),
            v((CHIP, CB), BF),
            v((CHIP, CA), BF),
            v((CHIP, CB), BF),
            v((128, 128), F32),
            v((1, 128), F32),
            v((8, 1, 128), F32),
            v((8, 2, 1, 128), F32),
            v((128, 128), F32),
            v((16, 128), BF),
            v((16, 16, 128), BF),
            v((128, 128), F32),
            v((128, 128), F32),
            pltpu.SemaphoreType.DMA((128,)),
            pltpu.SemaphoreType.DMA((128,)),
            pltpu.SemaphoreType.DMA((9,)),
            pltpu.SemaphoreType.DMA((6,)),
            pltpu.SemaphoreType.REGULAR((ROUNDS,)),
        ],
        compiler_params=pltpu.CompilerParams(
            collective_id=0, has_side_effects=True, vmem_limit_bytes=54 * 2**20
        ),
        cost_estimate=pl.CostEstimate(
            flops=6 * TOKENS * WIDTH * D, bytes_accessed=20 * 2**20, transcendentals=0
        ),
    )(forward_in[0], grad_out[0], saved_in[0], weight[0], gain)
    return next_input[None], prev_grad[None], weight_grad[None], gain_grad


def solution(mesh):
    rows = P("section", "tensor", None)
    return jax.shard_map(
        local,
        mesh=mesh,
        in_specs=(rows, rows, rows, rows, P("section", "tensor")),
        out_specs=(rows, rows, rows, P("section", "tensor")),
        check_vma=False,
    )
```
